32 devices in a mesh: rad: 2 (over x), az: 16 (over z, y, core).
Axes of the slice: x: 2, y: 2, z: 4, core: 2. Of those that a mesh axis runs over, the one named last changes fastest.
Arguments:
- fields: float32 [7, 32, 256, 128], P(None, 'rad', 'az'), may hold values from -6 to 6
- density: float32 [32, 256, 128], P('rad', 'az'), may hold values from 0.3 to 3
- shift_int: int32 [32], P('rad'), may hold values from 0 to 255
- frac_num: int32 [32], P('rad'), may hold values from 0 to 63
- boundary_shift: int32 [1], replicated, may hold values from 0 to 255
Outputs:
- new_fields: float32 [7, 32, 256, 128], P(None, 'rad', 'az')
- new_density: float32 [32, 256, 128], P('rad', 'az')
The draws below stay inside these ranges and needn't reach their ends.
All inputs are finite; a program needn't handle non-finite values.
Results may differ from the reference program's by a relative error of at most 0.00002.
Values sent between devices are 32-bit elements; how exact they have to be, the bound alone decides.
No kernel may reach another device: no remote copies, remote signals or barrier semaphores. Data moves between devices by JAX's collectives and lax.ppermute only.
A program may use at most 64 MiB of HBM per device.

```python
import math
import jax
import jax.numpy as jnp
from jax import lax

FRAC_DEN = 64
NX = 32
NY = 256
NZ = 128


def touch_ends(values, key, low, largest):
    longest = values.shape.index(max(values.shape))
    spots = []
    for shift in (0, 1):
        where = [jax.random.randint(jax.random.fold_in(key, axis), (), 0, length) for axis, length in enumerate(values.shape)]
        where[longest] = (where[longest] + shift) % values.shape[longest]
        spots.append(tuple(where))
    return values.at[spots[0]].set(low).at[spots[1]].set(largest)


def block_scale(own_key, extent, pieces, smallest, top_value):
    gain = 1.0
    for axis_at, blocks in pieces:
        heights = jax.random.uniform(jax.random.fold_in(jax.random.fold_in(own_key, 6), axis_at), (blocks,), jnp.float32, smallest / len(pieces), top_value / len(pieces))
        gain = gain * jnp.repeat(jnp.exp(heights), extent[axis_at] // blocks).reshape((-1,) + (1,) * (len(extent) - 1 - axis_at))
    return gain


def scatter_about(rng, shape, scale, most, pieces=(), kind=jnp.bfloat16):
    array = jax.random.normal(rng, shape, jnp.float32) * scale
    if len(pieces) > 0:
        array = block_scale(rng, shape, pieces, -0.22, 0.18) * array
    return jnp.clip(array, min=-most, max=most).astype(kind)


def setup_inputs(seed: int = 0) -> dict:
    splits = jax.random.split(jax.random.key(seed), 6)
    return {
        "fields": scatter_about(splits[0], (7, NX, NY, NZ), 1.0, 6.0, ((1, 2), (2, 16)), jnp.float32),
        "density": jnp.clip(jnp.exp(math.log(3.0) - 2.3025851 * jax.random.uniform(splits[1], (NX, NY, NZ), jnp.float32) ** block_scale(splits[1], (NX, NY, NZ), ((0, 2), (1, 16)), -0.2, 0.2)), 0.3, 3.0),
        "shift_int": touch_ends(jax.random.randint(splits[2], (NX,), 0, NY), jax.random.fold_in(splits[2], 1), 0, NY - 1).astype(jnp.int32),
        "frac_num": touch_ends(jax.random.randint(splits[3], (NX,), 0, FRAC_DEN), jax.random.fold_in(splits[3], 1), 0, FRAC_DEN - 1).astype(jnp.int32),
        "boundary_shift": jax.random.randint(splits[4], (1,), 0, NY).astype(jnp.int32),
    }


shear_jump = 1.5
visc_step = 0.05
field_floor = 0.25

def vertical_slope(values):
    padded = jnp.concatenate([values[..., :1], values, values[..., -1:]], axis=-1)
    return (padded[..., 2:] - padded[..., :-2]) * 0.5

def field_stress(padded):
    velocity = padded[1:4]
    grad_x = (velocity[:, 2:, 1:-1] - velocity[:, :-2, 1:-1]) * 0.5
    grad_y = (velocity[:, 1:-1, 2:] - velocity[:, 1:-1, :-2]) * 0.5
    interior = padded[:, 1:-1, 1:-1]
    grad_z = vertical_slope(interior[1:4])
    magnet = interior[4:7]
    mag_square = magnet[0] * magnet[0] + magnet[1] * magnet[1] + magnet[2] * magnet[2]
    unit_field = magnet / jnp.sqrt(jnp.maximum(mag_square, field_floor))
    slopes = (grad_x, grad_y, grad_z)
    aligned = jnp.zeros_like(mag_square)
    for first_axis in range(3):
        for second_axis in range(3):
            aligned = aligned + unit_field[first_axis] * unit_field[second_axis] * slopes[second_axis][first_axis]
    velocity_div = grad_x[0] + grad_y[1] + grad_z[2]
    anisotropy = aligned - velocity_div / 3.0
    pressure_gap = 3.0 * visc_step * interior[0] * anisotropy
    tensor = jnp.stack([pressure_gap * (unit_field[0] * unit_field[0] - 1.0 / 3.0), pressure_gap * (unit_field[1] * unit_field[1] - 1.0 / 3.0), pressure_gap * (unit_field[2] * unit_field[2] - 1.0 / 3.0), pressure_gap * unit_field[0] * unit_field[1], pressure_gap * unit_field[0] * unit_field[2], pressure_gap * unit_field[1] * unit_field[2]])
    return (tensor, pressure_gap * anisotropy)

def divergence(padded):
    interior = padded[:, 1:-1, 1:-1]

    def along_x(component):
        return (padded[component, 2:, 1:-1] - padded[component, :-2, 1:-1]) * 0.5

    def along_y(component):
        return (padded[component, 1:-1, 2:] - padded[component, 1:-1, :-2]) * 0.5
    vertical = vertical_slope(interior)
    force_x = along_x(0) + along_y(3) + vertical[4]
    force_y = along_x(3) + along_y(1) + vertical[5]
    force_z = along_x(4) + along_y(5) + vertical[2]
    return jnp.stack([force_x, force_y, force_z])

def fromm_blend(back_two, back_one, centre, ahead_one, fraction):
    slope_here = (ahead_one - back_one) * 0.5
    slope_back = (centre - back_two) * 0.5
    return centre + fraction * (back_one - centre) + fraction * (1.0 - fraction) * 0.5 * (slope_back - slope_here)

def shear_pad(block_data, cells_wide, jump_row, shear_cells):
    lower_rim = jnp.roll(block_data[:, -cells_wide:], shear_cells, axis=2)
    upper_rim = jnp.roll(block_data[:, :cells_wide], -shear_cells, axis=2)
    if jump_row is not None:
        lower_rim = lower_rim.at[jump_row].add(shear_jump)
        upper_rim = upper_rim.at[jump_row].add(-shear_jump)
    widened = jnp.concatenate([lower_rim, block_data, upper_rim], axis=1)
    return jnp.concatenate([widened[:, :, -cells_wide:], widened, widened[:, :, :cells_wide]], axis=2)

def remap_all(updated, shift_int, frac_num):
    total_az = updated.shape[2]
    positions = jnp.arange(total_az, dtype=jnp.int32)
    fraction = (frac_num.astype(jnp.float32) / FRAC_DEN)[:, None, None]

    def remap_field(one_field):

        def sample(offset):
            lookup = (positions[None, :] - shift_int[:, None] + offset) % total_az
            lookup = jnp.broadcast_to(lookup[:, :, None], one_field.shape).astype(jnp.int32)
            return jnp.take_along_axis(one_field, lookup, axis=1)
        return fromm_blend(sample(-2), sample(-1), sample(0), sample(1), fraction)
    return lax.map(remap_field, updated)

def reference(fields, density, shift_int, frac_num, boundary_shift):
    stacked = jnp.concatenate([density[None], fields], axis=0)
    shear_cells = boundary_shift[0]
    padded = shear_pad(stacked, 1, 2, shear_cells)
    tensor, heating = field_stress(padded)
    tensor_pad = shear_pad(tensor, 1, None, shear_cells)
    force_terms = divergence(tensor_pad)
    updated = jnp.concatenate([stacked[0:1], stacked[1:4] + force_terms / stacked[0], stacked[4:7], (stacked[7] + heating)[None]], axis=0)
    result = remap_all(updated, shift_int, frac_num)
    return (result[1:], result[0])
```

```python
import jax
import jax.numpy as jnp
from jax import lax
from jax.sharding import PartitionSpec as P

FRAC_DEN = 64

shear_jump = 1.5
visc_step = 0.05
field_floor = 0.25


def vertical_slope(values):
    padded = jnp.concatenate([values[..., :1], values, values[..., -1:]], axis=-1)
    return (padded[..., 2:] - padded[..., :-2]) * 0.5


def field_stress(padded):
    velocity = padded[1:4]
    grad_x = (velocity[:, 2:, 1:-1] - velocity[:, :-2, 1:-1]) * 0.5
    grad_y = (velocity[:, 1:-1, 2:] - velocity[:, 1:-1, :-2]) * 0.5
    interior = padded[:, 1:-1, 1:-1]
    grad_z = vertical_slope(interior[1:4])
    magnet = interior[4:7]
    mag_square = magnet[0] * magnet[0] + magnet[1] * magnet[1] + magnet[2] * magnet[2]
    unit_field = magnet / jnp.sqrt(jnp.maximum(mag_square, field_floor))
    slopes = (grad_x, grad_y, grad_z)
    aligned = jnp.zeros_like(mag_square)
    for first_axis in range(3):
        for second_axis in range(3):
            aligned = (
                aligned
                + unit_field[first_axis] * unit_field[second_axis] * slopes[second_axis][first_axis]
            )
    velocity_div = grad_x[0] + grad_y[1] + grad_z[2]
    anisotropy = aligned - velocity_div / 3.0
    pressure_gap = 3.0 * visc_step * interior[0] * anisotropy
    tensor = jnp.stack(
        [
            pressure_gap * (unit_field[0] * unit_field[0] - 1.0 / 3.0),
            pressure_gap * (unit_field[1] * unit_field[1] - 1.0 / 3.0),
            pressure_gap * (unit_field[2] * unit_field[2] - 1.0 / 3.0),
            pressure_gap * unit_field[0] * unit_field[1],
            pressure_gap * unit_field[0] * unit_field[2],
            pressure_gap * unit_field[1] * unit_field[2],
        ]
    )
    return (tensor, pressure_gap * anisotropy)


def divergence(padded):
    interior = padded[:, 1:-1, 1:-1]

    def along_x(component):
        return (padded[component, 2:, 1:-1] - padded[component, :-2, 1:-1]) * 0.5

    def along_y(component):
        return (padded[component, 1:-1, 2:] - padded[component, 1:-1, :-2]) * 0.5

    vertical = vertical_slope(interior)
    force_x = along_x(0) + along_y(3) + vertical[4]
    force_y = along_x(3) + along_y(1) + vertical[5]
    force_z = along_x(4) + along_y(5) + vertical[2]
    return jnp.stack([force_x, force_y, force_z])


def fromm_blend(back_two, back_one, centre, ahead_one, fraction):
    slope_here = (ahead_one - back_one) * 0.5
    slope_back = (centre - back_two) * 0.5
    return (
        centre
        + fraction * (back_one - centre)
        + fraction * (1.0 - fraction) * 0.5 * (slope_back - slope_here)
    )


def radial_ghosts(density, velocity, magnet, shear_cells):
    az_cells = density.shape[1]
    radials = lax.axis_size("rad")
    azimuths = lax.axis_size("az")
    me = lax.axis_index("rad")

    def strip(near, far):
        return jnp.concatenate(
            [velocity[:, near], density[None, near], magnet[:, near], velocity[:, far]], axis=0
        )

    low = strip(0, 1)
    high = strip(-1, -2)
    blocks = shear_cells // az_cells
    remainder = shear_cells % az_cells

    def flat(rad, az):
        return rad * azimuths + az % azimuths

    last = radials - 1

    def wrap(data, steps):
        pairs = [(flat(last, az), flat(0, az + steps)) for az in range(azimuths)]
        pairs += [(flat(0, az), flat(last, az - steps)) for az in range(azimuths)]
        return lax.ppermute(data, ("rad", "az"), pairs)

    def branch(steps):
        def run(data):
            return wrap(data, steps), wrap(data, steps + 1)

        return run

    edge = jnp.where(me == 0, low, high)
    if radials == 2:
        other = jnp.where(me == 0, high, low)
        straight = lax.ppermute(other, "rad", [(0, 1), (1, 0)])
        from_below = from_above = straight
    else:
        from_below = lax.ppermute(high, "rad", [(i, i + 1) for i in range(last)])
        from_above = lax.ppermute(low, "rad", [(i + 1, i) for i in range(last)])
    whole, next_one = lax.switch(blocks, [branch(k) for k in range(azimuths)], edge)
    joined = jnp.concatenate(
        [jnp.where(me == 0, next_one, whole), jnp.where(me == 0, whole, next_one)], axis=1
    )
    start = jnp.where(me == 0, az_cells - remainder, remainder)
    sheared = lax.dynamic_slice_in_dim(joined, start, az_cells, axis=1)
    marker = jnp.zeros((10, 1, 1), jnp.float32).at[jnp.array([1, 8])].set(shear_jump)
    below = jnp.where(me == 0, sheared + marker, from_below)
    above = jnp.where(me == last, sheared - marker, from_above)
    return below, above


def widen(fields, density, shear_cells):
    velocity, magnet = fields[0:3], fields[3:6]
    below, above = radial_ghosts(density, velocity, magnet, shear_cells)
    stacked = jnp.concatenate([density[None], fields[:6]], axis=0)

    def nearest(strip):
        return jnp.concatenate([strip[3:4], strip[0:3], strip[4:7]], axis=0)[:, None]

    def second(strip):
        return jnp.concatenate([strip[0:1] * 0, strip[7:10], strip[4:7] * 0], axis=0)[:, None]

    tall = jnp.concatenate(
        [second(below), nearest(below), stacked, nearest(above), second(above)], axis=1
    )
    azimuths = lax.axis_size("az")
    head, tail = tall[:, :, :2], tall[:, :, -2:]
    before = lax.ppermute(tail, "az", [(i, (i + 1) % azimuths) for i in range(azimuths)])
    after = lax.ppermute(head, "az", [((i + 1) % azimuths, i) for i in range(azimuths)])
    return jnp.concatenate([before, tall, after], axis=2)


def remap(updated, shift_int, frac_num):
    quantities, columns, az_cells, depth = updated.shape
    azimuths = lax.axis_size("az")
    share = quantities * columns // azimuths
    pieces = updated.transpose(1, 0, 2, 3).reshape(azimuths * share, az_cells, depth)
    gathered = lax.all_to_all(pieces, "az", 0, 0, tiled=True)
    total = azimuths * az_cells
    whole = gathered.reshape(azimuths, share, az_cells, depth).transpose(1, 0, 2, 3)
    whole = whole.reshape(share, total, depth)
    mine = (lax.axis_index("az") * share + jnp.arange(share)) // quantities
    amounts = jnp.take(shift_int, mine)
    fractions = jnp.take(frac_num, mine).astype(jnp.float32) / FRAC_DEN
    doubled = jnp.concatenate([whole[:, -2:], whole, whole, whole[:, :1]], axis=1)

    def move(rows, amount):
        return lax.dynamic_slice_in_dim(rows, (total - amount) % total, total + 3, axis=0)

    if quantities % share == 0:
        around = lax.dynamic_slice_in_dim(
            doubled, (total - amounts[0]) % total, total + 3, axis=1
        )
    else:
        around = jax.vmap(move)(doubled, amounts)
    moved = fromm_blend(
        around[:, 0:total],
        around[:, 1 : total + 1],
        around[:, 2 : total + 2],
        around[:, 3 : total + 3],
        fractions[:, None, None],
    )
    back = moved.reshape(share, azimuths, az_cells, depth).transpose(1, 0, 2, 3)
    back = back.reshape(azimuths * share, az_cells, depth)
    result = lax.all_to_all(back, "az", 0, 0, tiled=True)
    return result.reshape(columns, quantities, az_cells, depth).transpose(1, 0, 2, 3)


def local(fields, density, shift_int, frac_num, boundary_shift):
    padded = widen(fields, density, boundary_shift[0])
    tensor, heating = field_stress(padded)
    force_terms = divergence(tensor)
    updated = jnp.concatenate(
        [
            density[None],
            fields[0:3] + force_terms / density,
            fields[3:6],
            (fields[6] + heating[1:-1, 1:-1])[None],
        ],
        axis=0,
    )
    result = remap(updated, shift_int, frac_num)
    return (result[1:], result[0])


def solution(mesh):
    in_specs = (P(None, "rad", "az", None), P("rad", "az", None), P("rad"), P("rad"), P())
    out_specs = (P(None, "rad", "az", None), P("rad", "az", None))
    return jax.shard_map(local, mesh=mesh, in_specs=in_specs, out_specs=out_specs, check_vma=False)
```

```python
import jax
import jax.numpy as jnp
from jax import lax
from jax.sharding import PartitionSpec as P

FRAC_DEN = 64

shear_jump = 1.5
visc_step = 0.05
field_floor = 0.25


def vertical_slope(values):
    padded = jnp.concatenate([values[..., :1], values, values[..., -1:]], axis=-1)
    return (padded[..., 2:] - padded[..., :-2]) * 0.5


def field_stress(padded):
    velocity = padded[1:4]
    grad_x = (velocity[:, 2:, 1:-1] - velocity[:, :-2, 1:-1]) * 0.5
    grad_y = (velocity[:, 1:-1, 2:] - velocity[:, 1:-1, :-2]) * 0.5
    interior = padded[:, 1:-1, 1:-1]
    grad_z = vertical_slope(interior[1:4])
    magnet = interior[4:7]
    mag_square = magnet[0] * magnet[0] + magnet[1] * magnet[1] + magnet[2] * magnet[2]
    unit_field = magnet / jnp.sqrt(jnp.maximum(mag_square, field_floor))
    slopes = (grad_x, grad_y, grad_z)
    aligned = jnp.zeros_like(mag_square)
    for first_axis in range(3):
        for second_axis in range(3):
            aligned = (
                aligned
                + unit_field[first_axis] * unit_field[second_axis] * slopes[second_axis][first_axis]
            )
    velocity_div = grad_x[0] + grad_y[1] + grad_z[2]
    anisotropy = aligned - velocity_div / 3.0
    pressure_gap = 3.0 * visc_step * interior[0] * anisotropy
    tensor = jnp.stack(
        [
            pressure_gap * (unit_field[0] * unit_field[0] - 1.0 / 3.0),
            pressure_gap * (unit_field[1] * unit_field[1] - 1.0 / 3.0),
            pressure_gap * (unit_field[2] * unit_field[2] - 1.0 / 3.0),
            pressure_gap * unit_field[0] * unit_field[1],
            pressure_gap * unit_field[0] * unit_field[2],
            pressure_gap * unit_field[1] * unit_field[2],
        ]
    )
    return (tensor, pressure_gap * anisotropy)


def divergence(padded):
    interior = padded[:, 1:-1, 1:-1]

    def along_x(component):
        return (padded[component, 2:, 1:-1] - padded[component, :-2, 1:-1]) * 0.5

    def along_y(component):
        return (padded[component, 1:-1, 2:] - padded[component, 1:-1, :-2]) * 0.5

    vertical = vertical_slope(interior)
    force_x = along_x(0) + along_y(3) + vertical[4]
    force_y = along_x(3) + along_y(1) + vertical[5]
    force_z = along_x(4) + along_y(5) + vertical[2]
    return jnp.stack([force_x, force_y, force_z])


def fromm_blend(back_two, back_one, centre, ahead_one, fraction):
    slope_here = (ahead_one - back_one) * 0.5
    slope_back = (centre - back_two) * 0.5
    return (
        centre
        + fraction * (back_one - centre)
        + fraction * (1.0 - fraction) * 0.5 * (slope_back - slope_here)
    )


def radial_ghosts(density, velocity, magnet, shear_cells):
    az_cells = density.shape[1]
    radials = lax.axis_size("rad")
    azimuths = lax.axis_size("az")
    me = lax.axis_index("rad")

    def strip(near, far):
        return jnp.concatenate(
            [velocity[:, near], density[None, near], magnet[:, near], velocity[:, far]], axis=0
        )

    low = strip(0, 1)
    high = strip(-1, -2)
    blocks = shear_cells // az_cells
    remainder = shear_cells % az_cells

    def flat(rad, az):
        return rad * azimuths + az % azimuths

    last = radials - 1

    def wrap(data, steps):
        pairs = [(flat(last, az), flat(0, az + steps)) for az in range(azimuths)]
        pairs += [(flat(0, az), flat(last, az - steps)) for az in range(azimuths)]
        return lax.ppermute(data, ("rad", "az"), pairs)

    def branch(steps):
        def run(data):
            return wrap(data, steps), wrap(data, steps + 1)

        return run

    edge = jnp.where(me == 0, low, high)
    if radials == 2:
        other = jnp.where(me == 0, high, low)
        straight = lax.ppermute(other, "rad", [(0, 1), (1, 0)])
        from_below = from_above = straight
    else:
        from_below = lax.ppermute(high, "rad", [(i, i + 1) for i in range(last)])
        from_above = lax.ppermute(low, "rad", [(i + 1, i) for i in range(last)])
    whole, next_one = lax.switch(blocks, [branch(k) for k in range(azimuths)], edge)
    joined = jnp.concatenate(
        [jnp.where(me == 0, next_one, whole), jnp.where(me == 0, whole, next_one)], axis=1
    )
    start = jnp.where(me == 0, az_cells - remainder, remainder)
    sheared = lax.dynamic_slice_in_dim(joined, start, az_cells, axis=1)
    marker = jnp.zeros((10, 1, 1), jnp.float32).at[jnp.array([1, 8])].set(shear_jump)
    below = jnp.where(me == 0, sheared + marker, from_below)
    above = jnp.where(me == last, sheared - marker, from_above)
    return below, above


def widen(fields, density, shear_cells):
    velocity, magnet = fields[0:3], fields[3:6]
    below, above = radial_ghosts(density, velocity, magnet, shear_cells)
    stacked = jnp.concatenate([density[None], fields[:6]], axis=0)

    def nearest(strip):
        return jnp.concatenate([strip[3:4], strip[0:3], strip[4:7]], axis=0)[:, None]

    def second(strip):
        return jnp.concatenate([strip[0:1] * 0, strip[7:10], strip[4:7] * 0], axis=0)[:, None]

    tall = jnp.concatenate(
        [second(below), nearest(below), stacked, nearest(above), second(above)], axis=1
    )
    azimuths = lax.axis_size("az")
    head, tail = tall[:, :, :2], tall[:, :, -2:]
    before = lax.ppermute(tail, "az", [(i, (i + 1) % azimuths) for i in range(azimuths)])
    after = lax.ppermute(head, "az", [((i + 1) % azimuths, i) for i in range(azimuths)])
    return jnp.concatenate([before, tall, after], axis=2)


def gather_columns(block):
    quantities, columns, az_cells, depth = block.shape
    azimuths = lax.axis_size("az")
    share = quantities * columns // azimuths
    pieces = block.transpose(1, 0, 2, 3).reshape(azimuths * share, az_cells, depth)
    gathered = lax.all_to_all(pieces, "az", 0, 0, tiled=True)
    whole = gathered.reshape(azimuths, share, az_cells, depth).transpose(1, 0, 2, 3)
    return whole.reshape(share, azimuths * az_cells, depth)


def move_columns(whole, quantities, shift_int, frac_num):
    share, total, _ = whole.shape
    mine = (lax.axis_index("az") * share + jnp.arange(share)) // quantities
    amounts = jnp.take(shift_int, mine)
    fractions = jnp.take(frac_num, mine).astype(jnp.float32) / FRAC_DEN
    doubled = jnp.concatenate([whole[:, -2:], whole, whole, whole[:, :1]], axis=1)

    def move(rows, amount):
        return lax.dynamic_slice_in_dim(rows, (total - amount) % total, total + 3, axis=0)

    if quantities % share == 0:
        around = lax.dynamic_slice_in_dim(
            doubled, (total - amounts[0]) % total, total + 3, axis=1
        )
    else:
        around = jax.vmap(move)(doubled, amounts)
    return fromm_blend(
        around[:, 0:total],
        around[:, 1 : total + 1],
        around[:, 2 : total + 2],
        around[:, 3 : total + 3],
        fractions[:, None, None],
    )


def return_columns(moved, quantities, columns):
    share, total, depth = moved.shape
    azimuths = lax.axis_size("az")
    az_cells = total // azimuths
    back = moved.reshape(share, azimuths, az_cells, depth).transpose(1, 0, 2, 3)
    back = back.reshape(azimuths * share, az_cells, depth)
    result = lax.all_to_all(back, "az", 0, 0, tiled=True)
    return result.reshape(columns, quantities, az_cells, depth).transpose(1, 0, 2, 3)


def remap(block, shift_int, frac_num):
    whole = gather_columns(block)
    moved = move_columns(whole, block.shape[0], shift_int, frac_num)
    return return_columns(moved, block.shape[0], block.shape[1])


def local(fields, density, shift_int, frac_num, boundary_shift):
    still = remap(jnp.concatenate([density[None], fields[3:6]], axis=0), shift_int, frac_num)
    padded = widen(fields, density, boundary_shift[0])
    tensor, heating = field_stress(padded)
    force_terms = divergence(tensor)
    updated = jnp.concatenate(
        [
            fields[0:3] + force_terms / density,
            (fields[6] + heating[1:-1, 1:-1])[None],
        ],
        axis=0,
    )
    result = remap(updated, shift_int, frac_num)
    return (jnp.concatenate([result[0:3], still[1:4], result[3:4]], axis=0), still[0])


def solution(mesh):
    in_specs = (P(None, "rad", "az", None), P("rad", "az", None), P("rad"), P("rad"), P())
    out_specs = (P(None, "rad", "az", None), P("rad", "az", None))
    return jax.shard_map(local, mesh=mesh, in_specs=in_specs, out_specs=out_specs, check_vma=False)
```

```python
import jax
import jax.numpy as jnp
from jax import lax
from jax.sharding import PartitionSpec as P

FRAC_DEN = 64

shear_jump = 1.5
visc_step = 0.05
field_floor = 0.25


def vertical_slope(values):
    padded = jnp.concatenate([values[..., :1], values, values[..., -1:]], axis=-1)
    return (padded[..., 2:] - padded[..., :-2]) * 0.5


def field_stress(padded):
    velocity = padded[1:4]
    grad_x = (velocity[:, 2:, 1:-1] - velocity[:, :-2, 1:-1]) * 0.5
    grad_y = (velocity[:, 1:-1, 2:] - velocity[:, 1:-1, :-2]) * 0.5
    interior = padded[:, 1:-1, 1:-1]
    grad_z = vertical_slope(interior[1:4])
    magnet = interior[4:7]
    mag_square = magnet[0] * magnet[0] + magnet[1] * magnet[1] + magnet[2] * magnet[2]
    unit_field = magnet / jnp.sqrt(jnp.maximum(mag_square, field_floor))
    slopes = (grad_x, grad_y, grad_z)
    aligned = jnp.zeros_like(mag_square)
    for first_axis in range(3):
        for second_axis in range(3):
            aligned = (
                aligned
                + unit_field[first_axis] * unit_field[second_axis] * slopes[second_axis][first_axis]
            )
    velocity_div = grad_x[0] + grad_y[1] + grad_z[2]
    anisotropy = aligned - velocity_div / 3.0
    pressure_gap = 3.0 * visc_step * interior[0] * anisotropy
    tensor = jnp.stack(
        [
            pressure_gap * (unit_field[0] * unit_field[0] - 1.0 / 3.0),
            pressure_gap * (unit_field[1] * unit_field[1] - 1.0 / 3.0),
            pressure_gap * (unit_field[2] * unit_field[2] - 1.0 / 3.0),
            pressure_gap * unit_field[0] * unit_field[1],
            pressure_gap * unit_field[0] * unit_field[2],
            pressure_gap * unit_field[1] * unit_field[2],
        ]
    )
    return (tensor, pressure_gap * anisotropy)


def divergence(padded):
    interior = padded[:, 1:-1, 1:-1]

    def along_x(component):
        return (padded[component, 2:, 1:-1] - padded[component, :-2, 1:-1]) * 0.5

    def along_y(component):
        return (padded[component, 1:-1, 2:] - padded[component, 1:-1, :-2]) * 0.5

    vertical = vertical_slope(interior)
    force_x = along_x(0) + along_y(3) + vertical[4]
    force_y = along_x(3) + along_y(1) + vertical[5]
    force_z = along_x(4) + along_y(5) + vertical[2]
    return jnp.stack([force_x, force_y, force_z])


def fromm_blend(back_two, back_one, centre, ahead_one, fraction):
    slope_here = (ahead_one - back_one) * 0.5
    slope_back = (centre - back_two) * 0.5
    return (
        centre
        + fraction * (back_one - centre)
        + fraction * (1.0 - fraction) * 0.5 * (slope_back - slope_here)
    )


def radial_ghosts(density, velocity, magnet, shear_cells, pieces):
    az_cells = density.shape[1]
    radials = lax.axis_size("rad")
    azimuths = lax.axis_size("az")
    me = lax.axis_index("rad")

    def strip(near, far):
        return jnp.concatenate(
            [velocity[:, near], density[None, near], magnet[:, near], velocity[:, far]], axis=0
        )

    low = strip(0, 1)
    high = strip(-1, -2)
    blocks = shear_cells // az_cells
    remainder = shear_cells % az_cells

    def flat(rad, az):
        return rad * azimuths + az % azimuths

    last = radials - 1

    def wrap(data, steps):
        pairs = [(flat(last, az), flat(0, az + steps)) for az in range(azimuths)]
        pairs += [(flat(0, az), flat(last, az - steps)) for az in range(azimuths)]
        return lax.ppermute(data, ("rad", "az"), pairs)

    def branch(steps):
        def run(data, other, pieces):
            return (
                wrap(data, steps),
                wrap(data, steps + 1),
                straight_of(other),
                lax.all_to_all(pieces, "az", 0, 0, tiled=True),
            )

        return run

    def straight_of(other):
        if radials == 2:
            return (lax.ppermute(other[0], "rad", [(0, 1), (1, 0)]),) * 2
        return (
            lax.ppermute(other[0], "rad", [(i, i + 1) for i in range(last)]),
            lax.ppermute(other[1], "rad", [(i + 1, i) for i in range(last)]),
        )

    edge = jnp.where(me == 0, low, high)
    other = (jnp.where(me == 0, high, low),) if radials == 2 else (high, low)
    whole, next_one, (from_below, from_above), gathered = lax.switch(
        blocks, [branch(k) for k in range(azimuths)], edge, other, pieces
    )
    joined = jnp.concatenate(
        [jnp.where(me == 0, next_one, whole), jnp.where(me == 0, whole, next_one)], axis=1
    )
    start = jnp.where(me == 0, az_cells - remainder, remainder)
    sheared = lax.dynamic_slice_in_dim(joined, start, az_cells, axis=1)
    marker = jnp.zeros((10, 1, 1), jnp.float32).at[jnp.array([1, 8])].set(shear_jump)
    below = jnp.where(me == 0, sheared + marker, from_below)
    above = jnp.where(me == last, sheared - marker, from_above)
    return below, above, gathered


def widen(fields, density, shear_cells, pieces):
    velocity, magnet = fields[0:3], fields[3:6]
    below, above, gathered = radial_ghosts(density, velocity, magnet, shear_cells, pieces)
    stacked = jnp.concatenate([density[None], fields[:6]], axis=0)

    def nearest(strip):
        return jnp.concatenate([strip[3:4], strip[0:3], strip[4:7]], axis=0)[:, None]

    def second(strip):
        return jnp.concatenate([strip[0:1] * 0, strip[7:10], strip[4:7] * 0], axis=0)[:, None]

    tall = jnp.concatenate(
        [second(below), nearest(below), stacked, nearest(above), second(above)], axis=1
    )
    azimuths = lax.axis_size("az")
    head, tail = tall[:, :, :2], tall[:, :, -2:]
    before = lax.ppermute(tail, "az", [(i, (i + 1) % azimuths) for i in range(azimuths)])
    after = lax.ppermute(head, "az", [((i + 1) % azimuths, i) for i in range(azimuths)])
    return jnp.concatenate([before, tall, after], axis=2), gathered


def cut_columns(block):
    quantities, columns, az_cells, depth = block.shape
    azimuths = lax.axis_size("az")
    return block.transpose(1, 0, 2, 3).reshape(azimuths, -1, az_cells, depth)


def move_columns(gathered, quantities, shift_int, frac_num):
    azimuths, share, az_cells, depth = gathered.shape
    total = azimuths * az_cells
    whole = gathered.transpose(1, 0, 2, 3).reshape(share, total, depth)
    mine = (lax.axis_index("az") * share + jnp.arange(share)) // quantities
    amounts = jnp.take(shift_int, mine)
    fractions = jnp.take(frac_num, mine).astype(jnp.float32) / FRAC_DEN
    doubled = jnp.concatenate([whole[:, -2:], whole, whole, whole[:, :1]], axis=1)

    def move(rows, amount):
        return lax.dynamic_slice_in_dim(rows, (total - amount) % total, total + 3, axis=0)

    if quantities % share == 0:
        around = lax.dynamic_slice_in_dim(
            doubled, (total - amounts[0]) % total, total + 3, axis=1
        )
    else:
        around = jax.vmap(move)(doubled, amounts)
    moved = fromm_blend(
        around[:, 0:total],
        around[:, 1 : total + 1],
        around[:, 2 : total + 2],
        around[:, 3 : total + 3],
        fractions[:, None, None],
    )
    return moved.reshape(share, azimuths, az_cells, depth).transpose(1, 0, 2, 3)


def join_columns(returned, quantities):
    azimuths, share, az_cells, depth = returned.shape
    return returned.reshape(-1, quantities, az_cells, depth).transpose(1, 0, 2, 3)


def local(fields, density, shift_int, frac_num, boundary_shift):
    still = jnp.concatenate([density[None], fields[3:6]], axis=0)
    padded, gathered = widen(fields, density, boundary_shift[0], cut_columns(still))
    still_moved = move_columns(gathered, 4, shift_int, frac_num)
    tensor, heating = field_stress(padded)
    force_terms = divergence(tensor)
    updated = jnp.concatenate(
        [
            fields[0:3] + force_terms / density,
            (fields[6] + heating[1:-1, 1:-1])[None],
        ],
        axis=0,
    )
    share = still_moved.shape[1]
    both = jnp.concatenate([cut_columns(updated), still_moved], axis=1)
    both = lax.all_to_all(both, "az", 0, 0, tiled=True)
    still = join_columns(both[:, share:], 4)
    updated_moved = move_columns(both[:, :share], 4, shift_int, frac_num)
    result = join_columns(lax.all_to_all(updated_moved, "az", 0, 0, tiled=True), 4)
    return (jnp.concatenate([result[0:3], still[1:4], result[3:4]], axis=0), still[0])


def solution(mesh):
    in_specs = (P(None, "rad", "az", None), P("rad", "az", None), P("rad"), P("rad"), P())
    out_specs = (P(None, "rad", "az", None), P("rad", "az", None))
    return jax.shard_map(local, mesh=mesh, in_specs=in_specs, out_specs=out_specs, check_vma=False)
```

```python
import functools

import jax
import jax.numpy as jnp
from jax import lax
from jax.experimental import pallas as pl
from jax.experimental.pallas import tpu as pltpu
from jax.sharding import PartitionSpec as P

FRAC_DEN = 64

shear_jump = 1.5
visc_step = 0.05
field_floor = 0.25

PACKED = 10
TOP = 8


def up_and_down(values):
    lane = lax.broadcasted_iota(jnp.int32, values.shape, values.ndim - 1)
    depth = values.shape[-1]
    up = pltpu.roll(values, depth - 1, values.ndim - 1)
    down = pltpu.roll(values, 1, values.ndim - 1)
    return jnp.where(lane == depth - 1, values, up), jnp.where(lane == 0, values, down)


def vertical_slope(values):
    up, down = up_and_down(values)
    return (up - down) * 0.5


def stress(density, magnet, grad_x, grad_y, grad_z):
    square = magnet[0] * magnet[0] + magnet[1] * magnet[1] + magnet[2] * magnet[2]
    inverse = lax.rsqrt(jnp.maximum(square, field_floor))
    unit = [component * inverse for component in magnet]
    slopes = (grad_x, grad_y, grad_z)
    aligned = None
    for direction in range(3):
        along = (
            unit[0] * slopes[direction][0]
            + unit[1] * slopes[direction][1]
            + unit[2] * slopes[direction][2]
        )
        term = unit[direction] * along
        aligned = term if aligned is None else aligned + term
    anisotropy = aligned - (grad_x[0] + grad_y[1] + grad_z[2]) * (1.0 / 3.0)
    gap = (3.0 * visc_step) * density * anisotropy
    return gap, anisotropy, unit


def stress_kernel(
    info,
    fields,
    density,
    head,
    tail,
    before,
    after,
    straight_below,
    straight_above,
    whole,
    next_one,
    out,
    joined,
    vel,
    mass,
    px,
    py,
    pzz,
    heat,
):
    columns, cells, depth = density.shape
    first, last, remainder = info[0], info[1], info[2]
    end = TOP + cells

    def place(far, near, ghost, start, jump):
        for component in range(3):
            added = jump if component == 1 else 0.0
            vel[component, near, TOP - 1 : end + 1] = (
                joined[component, pl.ds(start, cells + 2)] + added
            )
            vel[component, far, TOP:end] = joined[7 + component, pl.ds(start + 1, cells)] + added
        for row in range(4):
            mass[row, ghost] = joined[3 + row, pl.ds(start + 1, cells)]

    def lay(one, two):
        for row in range(PACKED):
            joined[row, 1 : cells + 1] = one[row]
            if two is not None:
                joined[row, cells + 1 : 2 * cells + 1] = two[row]
        final = one if two is None else two
        spot = (1 if two is None else 2) * cells + 1
        for component in range(3):
            joined[component, 0:1] = one[PACKED, 2 * component : 2 * component + 1]
            joined[component, spot : spot + 1] = final[PACKED, 2 * component + 1 : 2 * component + 2]

    below = (0, 1, 0)
    above = (columns + 3, columns + 2, columns + 1)

    @pl.when(first == 1)
    def _():
        lay(next_one, whole)
        place(*below, cells - remainder, shear_jump)

    @pl.when(first == 0)
    def _():
        lay(straight_below, None)
        place(*below, 0, 0.0)

    @pl.when(last == 1)
    def _():
        lay(whole, next_one)
        place(*above, remainder, -shear_jump)

    @pl.when(last == 0)
    def _():
        lay(straight_above, None)
        place(*above, 0, 0.0)

    vel[:, 2 : columns + 2, TOP:end] = fields[0:3]
    mass[0, 1 : columns + 1] = density[...]
    mass[1:4, 1 : columns + 1] = fields[3:6]
    for component in range(3):
        for column in range(columns):
            vel[component, 2 + column, TOP - 1 : TOP] = before[component, column : column + 1]
            vel[component, 2 + column, end : end + 1] = after[component, column : column + 1]

    for layer, spot, high, low in (
        (before, TOP - 1, (head, 0), (before, 7)),
        (after, end, (after, 7), (tail, 0)),
    ):
        grad_x, grad_y, grad_z = [], [], []
        for component in range(3):
            row = layer[component]
            left = jnp.concatenate(
                [vel[component, 1, spot : spot + 1], layer[component, 0 : columns - 1]], axis=0
            )
            right = jnp.concatenate(
                [layer[component, 1:columns], vel[component, columns + 2, spot : spot + 1]], axis=0
            )
            grad_x.append((right - left) * 0.5)
            grad_y.append((high[0][high[1] + component] - low[0][low[1] + component]) * 0.5)
            grad_z.append(vertical_slope(row))
        magnet = [layer[4], layer[5], layer[6]]
        gap, _, unit = stress(layer[3], magnet, grad_x, grad_y, grad_z)
        edge = gap * unit[1]
        parts = (edge * unit[0], edge * unit[1] - gap * (1.0 / 3.0), edge * unit[2])
        for row in range(3):
            for column in range(columns):
                py[row, 1 + column, spot : spot + 1] = parts[row][column : column + 1]

    def tensor_column(ghost, carry):
        here = ghost + 1
        grad_x = [
            (vel[i, here + 1, TOP:end] - vel[i, here - 1, TOP:end]) * 0.5 for i in range(3)
        ]
        grad_y = [
            (vel[i, here, TOP + 1 : end + 1] - vel[i, here, TOP - 1 : end - 1]) * 0.5
            for i in range(3)
        ]
        grad_z = [vertical_slope(vel[i, here, TOP:end]) for i in range(3)]
        magnet = [mass[1, ghost], mass[2, ghost], mass[3, ghost]]
        gap, anisotropy, unit = stress(mass[0, ghost], magnet, grad_x, grad_y, grad_z)
        third = gap * (1.0 / 3.0)
        along_x, along_y = gap * unit[0], gap * unit[1]
        px[0, ghost] = along_x * unit[0] - third
        cross = along_x * unit[1]
        px[1, ghost] = cross
        px[2, ghost] = along_x * unit[2]
        py[0, ghost, TOP:end] = cross
        py[1, ghost, TOP:end] = along_y * unit[1] - third
        py[2, ghost, TOP:end] = along_y * unit[2]
        pzz[ghost] = gap * unit[2] * unit[2] - third
        heat[ghost] = gap * anisotropy
        return carry

    lax.fori_loop(0, columns + 2, tensor_column, 0)

    def update_column(column, carry):
        ghost = column + 1
        inverse = 1.0 / mass[0, ghost]

        def slope(axis):
            return (px[axis, ghost + 1] - px[axis, ghost - 1]) * 0.5 + (
                py[axis, ghost, TOP + 1 : end + 1] - py[axis, ghost, TOP - 1 : end - 1]
            ) * 0.5

        vertical = (px[2, ghost], py[2, ghost, TOP:end], pzz[ghost])
        for axis in range(3):
            force = slope(axis) + vertical_slope(vertical[axis])
            out[column, axis] = fields[axis, column] + force * inverse
        out[column, 3] = fields[6, column] + heat[ghost]
        return carry

    lax.fori_loop(0, columns, update_column, 0)


def updated_columns(info, fields, density, *layers):
    columns, cells, depth = density.shape
    tall = cells + 2 * TOP
    smem = pl.BlockSpec(memory_space=pltpu.SMEM)
    vmem = pl.BlockSpec(memory_space=pltpu.VMEM)
    f32 = jnp.float32
    return pl.pallas_call(
        stress_kernel,
        out_shape=jax.ShapeDtypeStruct((columns, 4, cells, depth), f32),
        in_specs=[smem] + [vmem] * 10,
        out_specs=vmem,
        scratch_shapes=[
            pltpu.VMEM((PACKED, 2 * cells + TOP, depth), f32),
            pltpu.VMEM((3, columns + 4, tall, depth), f32),
            pltpu.VMEM((4, columns + 2, cells, depth), f32),
            pltpu.VMEM((3, columns + 2, cells, depth), f32),
            pltpu.VMEM((3, columns + 2, tall, depth), f32),
            pltpu.VMEM((columns + 2, cells, depth), f32),
            pltpu.VMEM((columns + 2, cells, depth), f32),
        ],
        compiler_params=pltpu.CompilerParams(vmem_limit_bytes=24 * 2**20),
        name="stress_update",
    )(info, fields, density, *layers)


def move_kernel(quantities, rank, shift, frac, gathered, out, twice):
    azimuths, share, cells, depth = gathered.shape
    total = azimuths * cells
    for pair in range(share):
        for block in range(azimuths):
            rows = gathered[block, pair]
            twice[pair, TOP + block * cells : TOP + (block + 1) * cells] = rows
            twice[pair, TOP + total + block * cells : TOP + total + (block + 1) * cells] = rows
        twice[pair, 0:TOP] = gathered[azimuths - 1, pair, cells - TOP : cells]
        column = (rank[0] * share + pair) // quantities
        amount = shift[column]
        fraction = frac[column].astype(jnp.float32) * (1.0 / FRAC_DEN)
        bend = fraction * (1.0 - fraction) * 0.25
        start = TOP + lax.rem(total - amount, total)

        def blend(block, carry):
            spot = start + block * cells
            back_two = twice[pair, pl.ds(spot - 2, cells)]
            back_one = twice[pair, pl.ds(spot - 1, cells)]
            centre = twice[pair, pl.ds(spot, cells)]
            ahead = twice[pair, pl.ds(spot + 1, cells)]
            out[block, pair] = (
                centre
                + fraction * (back_one - centre)
                + bend * ((centre - back_two) - (ahead - back_one))
            )
            return carry

        lax.fori_loop(0, azimuths, blend, 0)


def move_columns(gathered, quantities, rank, shift_int, frac_num):
    azimuths, share, cells, depth = gathered.shape
    smem = pl.BlockSpec(memory_space=pltpu.SMEM)
    vmem = pl.BlockSpec(memory_space=pltpu.VMEM)
    return pl.pallas_call(
        functools.partial(move_kernel, quantities),
        out_shape=jax.ShapeDtypeStruct(gathered.shape, jnp.float32),
        in_specs=[smem, smem, smem, vmem],
        out_specs=vmem,
        scratch_shapes=[pltpu.VMEM((share, 2 * azimuths * cells + TOP, depth), jnp.float32)],
        compiler_params=pltpu.CompilerParams(vmem_limit_bytes=16 * 2**20),
        name="move",
    )(rank, shift_int, frac_num, gathered)


def cut_columns(block):
    quantities, columns, cells, depth = block.shape
    azimuths = lax.axis_size("az")
    return block.transpose(1, 0, 2, 3).reshape(azimuths, -1, cells, depth)


def join_columns(returned, quantities):
    azimuths, share, cells, depth = returned.shape
    return returned.reshape(-1, quantities, cells, depth).transpose(1, 0, 2, 3)


def exchange(blocks, head, tail, low, high, pieces):
    radials = lax.axis_size("rad")
    azimuths = lax.axis_size("az")
    rad = lax.axis_index("rad")
    even = lax.axis_index("az") % 2 == 0
    last = radials - 1

    def flat(rad, az):
        return rad * azimuths + az % azimuths

    def wrap(data, steps):
        pairs = [(flat(last, az), flat(0, az + steps)) for az in range(azimuths)]
        pairs += [(flat(0, az), flat(last, az - steps)) for az in range(azimuths)]
        return lax.ppermute(data, ("rad", "az"), pairs)

    def layers(head, tail):
        inner = [(az, az ^ 1) for az in range(azimuths)]
        outer = [(az, (az - 1 if az % 2 == 0 else az + 1) % azimuths) for az in range(azimuths)]
        far = lax.ppermute(jnp.where(even, head, tail), "az", outer)
        near = lax.ppermute(jnp.where(even, tail, head), "az", inner)
        return jnp.where(even, far, near), jnp.where(even, near, far)

    def rim(main, before, after, column):
        ends = jnp.stack([before[0:3, column], after[0:3, column]], axis=1)
        ends = ends.reshape(1, 6, main.shape[-1])
        ends = jnp.pad(ends, ((0, 0), (0, main.shape[1] - 6), (0, 0)))
        return jnp.concatenate([main, ends], axis=0)

    def branch(steps):
        def run(head, tail, low, high, pieces):
            gathered = lax.all_to_all(pieces, "az", 0, 0, tiled=True)
            before, after = layers(head, tail)
            low = rim(low, before, after, 0)
            high = rim(high, before, after, -1)
            edge = jnp.where(rad == 0, low, high)
            whole = wrap(edge, steps)
            next_one = wrap(edge, steps + 1)
            if radials == 2:
                other = jnp.where(rad == 0, high, low)
                below = above = lax.ppermute(other, "rad", [(0, 1), (1, 0)])
            else:
                below = lax.ppermute(high, "rad", [(i, i + 1) for i in range(last)])
                above = lax.ppermute(low, "rad", [(i + 1, i) for i in range(last)])
            return before, after, below, above, whole, next_one, gathered

        return run

    return lax.switch(
        blocks, [branch(steps) for steps in range(azimuths)], head, tail, low, high, pieces
    )


def local(fields, density, shift_int, frac_num, boundary_shift):
    velocity, magnet = fields[0:3], fields[3:6]
    cells = density.shape[1]
    radials = lax.axis_size("rad")
    rad = lax.axis_index("rad")
    shear_cells = boundary_shift[0]

    def layer(near, far):
        return jnp.concatenate(
            [velocity[:, :, near], density[None, :, near], magnet[:, :, near], velocity[:, :, far]]
        )

    def strip(near, far):
        return jnp.concatenate(
            [velocity[:, near], density[None, near], magnet[:, near], velocity[:, far]]
        )

    head, tail = layer(0, 1), layer(-1, -2)
    low, high = strip(0, 1), strip(-1, -2)
    still = jnp.concatenate([density[None], magnet], axis=0)
    before, after, below, above, whole, next_one, gathered = exchange(
        shear_cells // cells, head, tail, low, high, cut_columns(still)
    )
    rank = lax.axis_index("az").reshape(1)
    still_moved = move_columns(gathered, 4, rank, shift_int, frac_num)
    info = jnp.stack(
        [
            (rad == 0).astype(jnp.int32),
            (rad == radials - 1).astype(jnp.int32),
            shear_cells % cells,
        ]
    )
    updated = updated_columns(
        info, fields, density, head, tail, before, after, below, above, whole, next_one
    )
    share = still_moved.shape[1]
    updated = updated.reshape(still_moved.shape)
    both = jnp.concatenate([updated, still_moved], axis=1)
    both = lax.all_to_all(both, "az", 0, 0, tiled=True)
    still = join_columns(both[:, share:], 4)
    updated_moved = move_columns(both[:, :share], 4, rank, shift_int, frac_num)
    result = join_columns(lax.all_to_all(updated_moved, "az", 0, 0, tiled=True), 4)
    return (jnp.concatenate([result[0:3], still[1:4], result[3:4]], axis=0), still[0])


def solution(mesh):
    in_specs = (P(None, "rad", "az", None), P("rad", "az", None), P("rad"), P("rad"), P())
    out_specs = (P(None, "rad", "az", None), P("rad", "az", None))
    return jax.shard_map(local, mesh=mesh, in_specs=in_specs, out_specs=out_specs, check_vma=False)
```

```python
import functools

import jax
import jax.numpy as jnp
from jax import lax
from jax.experimental import pallas as pl
from jax.experimental.pallas import tpu as pltpu
from jax.sharding import PartitionSpec as P

FRAC_DEN = 64

shear_jump = 1.5
visc_step = 0.05
field_floor = 0.25

PACKED = 10
TOP = 8


def up_and_down(values):
    lane = lax.broadcasted_iota(jnp.int32, values.shape, values.ndim - 1)
    depth = values.shape[-1]
    up = pltpu.roll(values, depth - 1, values.ndim - 1)
    down = pltpu.roll(values, 1, values.ndim - 1)
    return jnp.where(lane == depth - 1, values, up), jnp.where(lane == 0, values, down)


def vertical_slope(values):
    up, down = up_and_down(values)
    return (up - down) * 0.5


def stress(density, magnet, grad_x, grad_y, grad_z):
    square = magnet[0] * magnet[0] + magnet[1] * magnet[1] + magnet[2] * magnet[2]
    inverse = lax.rsqrt(jnp.maximum(square, field_floor))
    unit = [component * inverse for component in magnet]
    slopes = (grad_x, grad_y, grad_z)
    aligned = None
    for direction in range(3):
        along = (
            unit[0] * slopes[direction][0]
            + unit[1] * slopes[direction][1]
            + unit[2] * slopes[direction][2]
        )
        term = unit[direction] * along
        aligned = term if aligned is None else aligned + term
    anisotropy = aligned - (grad_x[0] + grad_y[1] + grad_z[2]) * (1.0 / 3.0)
    gap = (3.0 * visc_step) * density * anisotropy
    return gap, anisotropy, unit


def pack_kernel(quantities, rank, fields, density, head, tail, low, high, still):
    columns, cells, depth = density.shape
    slots, share = still.shape[0], still.shape[1]

    def source(row):
        if row == 3:
            return density
        return fields.at[row if row < 3 else row - 1 if row < 7 else row - 7]

    for row in range(PACKED):
        second = 1 if row >= 7 else 0
        origin = source(row)
        low[row] = origin[second]
        high[row] = origin[columns - 1 - second]
        for column in range(columns):
            head[row, column : column + 1] = origin[column, second : second + 1]
            tail[row, column : column + 1] = origin[column, cells - 1 - second : cells - second]
    for slot in range(slots):
        for item in range(share):
            column, row = pair_of(lax.bitwise_xor(rank[0], slot), item, share, quantities)
            if isinstance(row, int):
                still[slot, item] = density[column] if row == 0 else fields[2 + row, column]
            else:
                still[slot, item] = jnp.where(
                    row == 0, density[column], fields[jnp.maximum(row, 1) + 2, column]
                )


def pair_of(rank, item, share, quantities):
    if share % quantities == 0:
        return rank * (share // quantities) + item // quantities, item % quantities
    flat = rank * share + item
    return flat // quantities, flat % quantities


def pack(rank, fields, density):
    columns, cells, depth = density.shape
    slots = lax.axis_size("az")
    share = 4 * columns // slots
    f32 = jnp.float32
    layer = jax.ShapeDtypeStruct((PACKED, columns, depth), f32)
    rim = jax.ShapeDtypeStruct((PACKED, cells, depth), f32)
    vmem = pl.BlockSpec(memory_space=pltpu.VMEM)
    return pl.pallas_call(
        functools.partial(pack_kernel, 4),
        out_shape=(
            layer,
            layer,
            rim,
            rim,
            jax.ShapeDtypeStruct((slots, share, cells, depth), f32),
        ),
        in_specs=[pl.BlockSpec(memory_space=pltpu.SMEM), vmem, vmem],
        out_specs=[vmem] * 5,
        compiler_params=pltpu.CompilerParams(vmem_limit_bytes=16 * 2**20),
        name="pack",
    )(rank, fields, density)


def join_kernel(quantities, rank, moving, still, new_fields, new_density):
    slots, share = still.shape[0], still.shape[1]
    for slot in range(slots):
        for item in range(share):
            column, row = pair_of(lax.bitwise_xor(rank[0], slot), item, share, quantities)
            if isinstance(row, int):
                new_fields[6 if row == 3 else row, column] = moving[slot, item]
                if row == 0:
                    new_density[column] = still[slot, item]
                else:
                    new_fields[2 + row, column] = still[slot, item]
            else:
                new_fields[jnp.where(row == 3, 6, row), column] = moving[slot, item]

                @pl.when(row == 0)
                def _():
                    new_density[column] = still[slot, item]

                @pl.when(row > 0)
                def _():
                    new_fields[2 + row, column] = still[slot, item]


def join(rank, moving, still, columns):
    _, _, cells, depth = still.shape
    f32 = jnp.float32
    vmem = pl.BlockSpec(memory_space=pltpu.VMEM)
    return pl.pallas_call(
        functools.partial(join_kernel, 4),
        out_shape=(
            jax.ShapeDtypeStruct((7, columns, cells, depth), f32),
            jax.ShapeDtypeStruct((columns, cells, depth), f32),
        ),
        in_specs=[pl.BlockSpec(memory_space=pltpu.SMEM), vmem, vmem],
        out_specs=[vmem] * 2,
        compiler_params=pltpu.CompilerParams(vmem_limit_bytes=16 * 2**20),
        name="join",
    )(rank, moving, still)


def swap(slots):
    count = slots.shape[0]
    stride = count
    while stride > 1:
        radix = 4 if stride % 4 == 0 else 2
        stride //= radix
        cut = slots.reshape(count // (radix * stride), radix, stride, *slots.shape[1:])
        parts = [cut[:, 0]]
        for step in range(1, radix):
            pairs = [(rank, rank ^ (step * stride)) for rank in range(count)]
            parts.append(lax.ppermute(cut[:, step], "az", pairs))
        slots = jnp.stack(parts, axis=1).reshape(slots.shape)
    return slots


def stress_kernel(
    info,
    fields,
    density,
    head,
    tail,
    before,
    after,
    straight_below,
    straight_above,
    whole,
    next_one,
    out,
    joined,
    vel,
    mass,
    px,
    py,
    pzz,
    heat,
):
    columns, cells, depth = density.shape
    share = out.shape[1]
    first, last, remainder = info[0], info[1], info[2]
    end = TOP + cells

    def place(far, near, ghost, start, jump):
        for component in range(3):
            added = jump if component == 1 else 0.0
            vel[component, near, TOP - 1 : end + 1] = (
                joined[component, pl.ds(start, cells + 2)] + added
            )
            vel[component, far, TOP:end] = joined[7 + component, pl.ds(start + 1, cells)] + added
        for row in range(4):
            mass[row, ghost] = joined[3 + row, pl.ds(start + 1, cells)]

    def lay(one, two):
        for row in range(PACKED):
            joined[row, 1 : cells + 1] = one[row]
            if two is not None:
                joined[row, cells + 1 : 2 * cells + 1] = two[row]
        final = one if two is None else two
        spot = (1 if two is None else 2) * cells + 1
        for component in range(3):
            joined[component, 0:1] = one[PACKED, 2 * component : 2 * component + 1]
            joined[component, spot : spot + 1] = final[PACKED, 2 * component + 1 : 2 * component + 2]

    below = (0, 1, 0)
    above = (columns + 3, columns + 2, columns + 1)

    @pl.when(first == 1)
    def _():
        lay(next_one, whole)
        place(*below, cells - remainder, shear_jump)

    @pl.when(first == 0)
    def _():
        lay(straight_below, None)
        place(*below, 0, 0.0)

    @pl.when(last == 1)
    def _():
        lay(whole, next_one)
        place(*above, remainder, -shear_jump)

    @pl.when(last == 0)
    def _():
        lay(straight_above, None)
        place(*above, 0, 0.0)

    vel[:, 2 : columns + 2, TOP:end] = fields[0:3]
    mass[0, 1 : columns + 1] = density[...]
    mass[1:4, 1 : columns + 1] = fields[3:6]
    for component in range(3):
        for column in range(columns):
            vel[component, 2 + column, TOP - 1 : TOP] = before[component, column : column + 1]
            vel[component, 2 + column, end : end + 1] = after[component, column : column + 1]

    for layer, spot, high, low in (
        (before, TOP - 1, (head, 0), (before, 7)),
        (after, end, (after, 7), (tail, 0)),
    ):
        grad_x, grad_y, grad_z = [], [], []
        for component in range(3):
            row = layer[component]
            left = jnp.concatenate(
                [vel[component, 1, spot : spot + 1], layer[component, 0 : columns - 1]], axis=0
            )
            right = jnp.concatenate(
                [layer[component, 1:columns], vel[component, columns + 2, spot : spot + 1]], axis=0
            )
            grad_x.append((right - left) * 0.5)
            grad_y.append((high[0][high[1] + component] - low[0][low[1] + component]) * 0.5)
            grad_z.append(vertical_slope(row))
        magnet = [layer[4], layer[5], layer[6]]
        gap, _, unit = stress(layer[3], magnet, grad_x, grad_y, grad_z)
        edge = gap * unit[1]
        parts = (edge * unit[0], edge * unit[1] - gap * (1.0 / 3.0), edge * unit[2])
        for row in range(3):
            for column in range(columns):
                py[row, 1 + column, spot : spot + 1] = parts[row][column : column + 1]

    def tensor_column(ghost, carry):
        here = ghost + 1
        grad_x = [
            (vel[i, here + 1, TOP:end] - vel[i, here - 1, TOP:end]) * 0.5 for i in range(3)
        ]
        grad_y = [
            (vel[i, here, TOP + 1 : end + 1] - vel[i, here, TOP - 1 : end - 1]) * 0.5
            for i in range(3)
        ]
        grad_z = [vertical_slope(vel[i, here, TOP:end]) for i in range(3)]
        magnet = [mass[1, ghost], mass[2, ghost], mass[3, ghost]]
        gap, anisotropy, unit = stress(mass[0, ghost], magnet, grad_x, grad_y, grad_z)
        third = gap * (1.0 / 3.0)
        along_x, along_y = gap * unit[0], gap * unit[1]
        px[0, ghost] = along_x * unit[0] - third
        cross = along_x * unit[1]
        px[1, ghost] = cross
        px[2, ghost] = along_x * unit[2]
        py[0, ghost, TOP:end] = cross
        py[1, ghost, TOP:end] = along_y * unit[1] - third
        py[2, ghost, TOP:end] = along_y * unit[2]
        pzz[ghost] = gap * unit[2] * unit[2] - third
        heat[ghost] = gap * anisotropy
        return carry

    lax.fori_loop(0, columns + 2, tensor_column, 0)

    def update_column(column, carry):
        ghost = column + 1
        inverse = 1.0 / mass[0, ghost]

        def slope(axis):
            return (px[axis, ghost + 1] - px[axis, ghost - 1]) * 0.5 + (
                py[axis, ghost, TOP + 1 : end + 1] - py[axis, ghost, TOP - 1 : end - 1]
            ) * 0.5

        vertical = (px[2, ghost], py[2, ghost, TOP:end], pzz[ghost])
        for axis in range(4):
            flat = column * 4 + axis
            slot = lax.bitwise_xor(info[3], flat // share)
            if axis < 3:
                force = slope(axis) + vertical_slope(vertical[axis])
                out[slot, flat % share] = fields[axis, column] + force * inverse
            else:
                out[slot, flat % share] = fields[6, column] + heat[ghost]
        return carry

    lax.fori_loop(0, columns, update_column, 0)


def updated_columns(info, fields, density, *layers):
    columns, cells, depth = density.shape
    tall = cells + 2 * TOP
    slots = lax.axis_size("az")
    smem = pl.BlockSpec(memory_space=pltpu.SMEM)
    vmem = pl.BlockSpec(memory_space=pltpu.VMEM)
    f32 = jnp.float32
    return pl.pallas_call(
        stress_kernel,
        out_shape=jax.ShapeDtypeStruct((slots, 4 * columns // slots, cells, depth), f32),
        in_specs=[smem] + [vmem] * 10,
        out_specs=vmem,
        scratch_shapes=[
            pltpu.VMEM((PACKED, 2 * cells + TOP, depth), f32),
            pltpu.VMEM((3, columns + 4, tall, depth), f32),
            pltpu.VMEM((4, columns + 2, cells, depth), f32),
            pltpu.VMEM((3, columns + 2, cells, depth), f32),
            pltpu.VMEM((3, columns + 2, tall, depth), f32),
            pltpu.VMEM((columns + 2, cells, depth), f32),
            pltpu.VMEM((columns + 2, cells, depth), f32),
        ],
        compiler_params=pltpu.CompilerParams(vmem_limit_bytes=24 * 2**20),
        name="stress_update",
    )(info, fields, density, *layers)


def move_kernel(quantities, rank, shift, frac, gathered, out, twice):
    slots, share, cells, depth = gathered.shape
    total = slots * cells
    me = rank[0]
    for item in range(share):
        column, _ = pair_of(me, item, share, quantities)
        fraction = frac[column].astype(jnp.float32) * (1.0 / FRAC_DEN)
        bend = fraction * (1.0 - fraction) * 0.25
        start = TOP + lax.rem(total - shift[column], total)

        def lay(slot, carry):
            rows = gathered[slot, item]
            spot = pl.multiple_of(TOP + lax.bitwise_xor(me, slot) * cells, TOP)
            twice[item, pl.ds(spot, cells)] = rows
            twice[item, pl.ds(pl.multiple_of(spot + total, TOP), cells)] = rows
            return carry

        lax.fori_loop(0, slots, lay, 0, unroll=4)
        twice[item, 0:TOP] = twice[item, total : total + TOP]

        def blend(slot, carry):
            spot = start + lax.bitwise_xor(me, slot) * cells
            back_two = twice[item, pl.ds(spot - 2, cells)]
            back_one = twice[item, pl.ds(spot - 1, cells)]
            centre = twice[item, pl.ds(spot, cells)]
            ahead = twice[item, pl.ds(spot + 1, cells)]
            out[slot, item] = (
                centre
                + fraction * (back_one - centre)
                + bend * ((centre - back_two) - (ahead - back_one))
            )
            return carry

        lax.fori_loop(0, slots, blend, 0, unroll=4)


def move_columns(gathered, quantities, rank, shift_int, frac_num):
    azimuths, share, cells, depth = gathered.shape
    smem = pl.BlockSpec(memory_space=pltpu.SMEM)
    vmem = pl.BlockSpec(memory_space=pltpu.VMEM)
    return pl.pallas_call(
        functools.partial(move_kernel, quantities),
        out_shape=jax.ShapeDtypeStruct(gathered.shape, jnp.float32),
        in_specs=[smem, smem, smem, vmem],
        out_specs=vmem,
        scratch_shapes=[pltpu.VMEM((share, 2 * azimuths * cells + TOP, depth), jnp.float32)],
        compiler_params=pltpu.CompilerParams(vmem_limit_bytes=16 * 2**20),
        name="move",
    )(rank, shift_int, frac_num, gathered)


def azimuthal_layers(head, tail):
    azimuths = lax.axis_size("az")
    even = lax.axis_index("az") % 2 == 0
    inner = [(az, az ^ 1) for az in range(azimuths)]
    outer = [(az, (az - 1 if az % 2 == 0 else az + 1) % azimuths) for az in range(azimuths)]
    far = lax.ppermute(jnp.where(even, head, tail), "az", outer)
    near = lax.ppermute(jnp.where(even, tail, head), "az", inner)
    return jnp.where(even, far, near), jnp.where(even, near, far)


def rims(blocks, low, high, before, after):
    radials = lax.axis_size("rad")
    azimuths = lax.axis_size("az")
    rad = lax.axis_index("rad")
    last = radials - 1

    def flat(rad, az):
        return rad * azimuths + az % azimuths

    def wrap(data, steps):
        pairs = [(flat(last, az), flat(0, az + steps)) for az in range(azimuths)]
        pairs += [(flat(0, az), flat(last, az - steps)) for az in range(azimuths)]
        return lax.ppermute(data, ("rad", "az"), pairs)

    def with_ends(main, column):
        ends = jnp.stack([before[0:3, column], after[0:3, column]], axis=1)
        ends = ends.reshape(1, 6, main.shape[-1])
        ends = jnp.pad(ends, ((0, 0), (0, main.shape[1] - 6), (0, 0)))
        return jnp.concatenate([main, ends], axis=0)

    low, high = with_ends(low, 0), with_ends(high, -1)
    edge = jnp.where(rad == 0, low, high)
    if radials == 2:
        other = jnp.where(rad == 0, high, low)
        below = above = lax.ppermute(other, "rad", [(0, 1), (1, 0)])
    else:
        below = lax.ppermute(high, "rad", [(i, i + 1) for i in range(last)])
        above = lax.ppermute(low, "rad", [(i + 1, i) for i in range(last)])

    def branch(steps):
        return lambda data: (wrap(data, steps), wrap(data, steps + 1))

    whole, next_one = lax.switch(blocks, [branch(steps) for steps in range(azimuths)], edge)
    return below, above, whole, next_one


def local(fields, density, shift_int, frac_num, boundary_shift):
    columns, cells, _ = density.shape
    radials = lax.axis_size("rad")
    rad = lax.axis_index("rad")
    shear_cells = boundary_shift[0]
    az = lax.axis_index("az")
    rank = az.reshape(1)
    head, tail, low, high, still = pack(rank, fields, density)
    before, after = azimuthal_layers(head, tail)
    before, after, still = lax.optimization_barrier((before, after, still))
    still = swap(still)
    layers = rims(shear_cells // cells, low, high, before, after)
    info = jnp.stack(
        [
            (rad == 0).astype(jnp.int32),
            (rad == radials - 1).astype(jnp.int32),
            shear_cells % cells,
            az,
        ]
    )
    moving = updated_columns(info, fields, density, head, tail, before, after, *layers)
    moving = swap(moving)
    still = swap(move_columns(still, 4, rank, shift_int, frac_num))
    moving = swap(move_columns(moving, 4, rank, shift_int, frac_num))
    return join(rank, moving, still, columns)


def solution(mesh):
    in_specs = (P(None, "rad", "az", None), P("rad", "az", None), P("rad"), P("rad"), P())
    out_specs = (P(None, "rad", "az", None), P("rad", "az", None))
    return jax.shard_map(local, mesh=mesh, in_specs=in_specs, out_specs=out_specs, check_vma=False)
```

```python
import functools

import jax
import jax.numpy as jnp
from jax import lax
from jax.experimental import pallas as pl
from jax.experimental.pallas import tpu as pltpu
from jax.sharding import PartitionSpec as P

FRAC_DEN = 64

shear_jump = 1.5
visc_step = 0.05
field_floor = 0.25

PACKED = 10
TOP = 8


def up_and_down(values):
    lane = lax.broadcasted_iota(jnp.int32, values.shape, values.ndim - 1)
    depth = values.shape[-1]
    up = pltpu.roll(values, depth - 1, values.ndim - 1)
    down = pltpu.roll(values, 1, values.ndim - 1)
    return jnp.where(lane == depth - 1, values, up), jnp.where(lane == 0, values, down)


def vertical_slope(values):
    up, down = up_and_down(values)
    return (up - down) * 0.5


def stress(density, magnet, grad_x, grad_y, grad_z):
    square = magnet[0] * magnet[0] + magnet[1] * magnet[1] + magnet[2] * magnet[2]
    inverse = lax.rsqrt(jnp.maximum(square, field_floor))
    unit = [component * inverse for component in magnet]
    slopes = (grad_x, grad_y, grad_z)
    aligned = None
    for direction in range(3):
        along = (
            unit[0] * slopes[direction][0]
            + unit[1] * slopes[direction][1]
            + unit[2] * slopes[direction][2]
        )
        term = unit[direction] * along
        aligned = term if aligned is None else aligned + term
    anisotropy = aligned - (grad_x[0] + grad_y[1] + grad_z[2]) * (1.0 / 3.0)
    gap = (3.0 * visc_step) * density * anisotropy
    return gap, anisotropy, unit


def pack_kernel(quantities, rank, fields, density, head, tail, low, high, still):
    columns, cells, depth = density.shape
    slots, share = still.shape[0], still.shape[1]

    def source(row):
        if row == 3:
            return density
        return fields.at[row if row < 3 else row - 1 if row < 7 else row - 7]

    for row in range(PACKED):
        second = 1 if row >= 7 else 0
        origin = source(row)
        low[row] = origin[second]
        high[row] = origin[columns - 1 - second]
        for column in range(columns):
            head[row, column : column + 1] = origin[column, second : second + 1]
            tail[row, column : column + 1] = origin[column, cells - 1 - second : cells - second]
    for slot in range(slots):
        for item in range(share):
            column, row = pair_of(lax.bitwise_xor(rank[0], slot), item, share, quantities)
            if isinstance(row, int):
                still[slot, item] = density[column] if row == 0 else fields[2 + row, column]
            else:
                still[slot, item] = jnp.where(
                    row == 0, density[column], fields[jnp.maximum(row, 1) + 2, column]
                )


def pair_of(rank, item, share, quantities):
    if share % quantities == 0:
        return rank * (share // quantities) + item // quantities, item % quantities
    flat = rank * share + item
    return flat // quantities, flat % quantities


def pack(rank, fields, density):
    columns, cells, depth = density.shape
    slots = lax.axis_size("az")
    share = 4 * columns // slots
    f32 = jnp.float32
    layer = jax.ShapeDtypeStruct((PACKED, columns, depth), f32)
    rim = jax.ShapeDtypeStruct((PACKED, cells, depth), f32)
    vmem = pl.BlockSpec(memory_space=pltpu.VMEM)
    return pl.pallas_call(
        functools.partial(pack_kernel, 4),
        out_shape=(
            layer,
            layer,
            rim,
            rim,
            jax.ShapeDtypeStruct((slots, share, cells, depth), f32),
        ),
        in_specs=[pl.BlockSpec(memory_space=pltpu.SMEM), vmem, vmem],
        out_specs=[vmem] * 5,
        compiler_params=pltpu.CompilerParams(vmem_limit_bytes=16 * 2**20),
        name="pack",
    )(rank, fields, density)


def join_kernel(quantities, rank, moving, still, new_fields, new_density):
    slots, share = still.shape[0], still.shape[1]
    for slot in range(slots):
        for item in range(share):
            column, row = pair_of(slot, item, share, quantities)
            new_fields[6 if row == 3 else row, column] = moving[slot, item]
            column, row = pair_of(lax.bitwise_xor(rank[0], slot), item, share, quantities)
            if not isinstance(row, int):

                @pl.when(row == 0)
                def _():
                    new_density[column] = still[slot, item]

                @pl.when(row > 0)
                def _():
                    new_fields[2 + row, column] = still[slot, item]

            elif row == 0:
                new_density[column] = still[slot, item]
            else:
                new_fields[2 + row, column] = still[slot, item]


def join(rank, moving, still, columns):
    _, _, cells, depth = still.shape
    f32 = jnp.float32
    vmem = pl.BlockSpec(memory_space=pltpu.VMEM)
    return pl.pallas_call(
        functools.partial(join_kernel, 4),
        out_shape=(
            jax.ShapeDtypeStruct((7, columns, cells, depth), f32),
            jax.ShapeDtypeStruct((columns, cells, depth), f32),
        ),
        in_specs=[pl.BlockSpec(memory_space=pltpu.SMEM), vmem, vmem],
        out_specs=[vmem] * 2,
        compiler_params=pltpu.CompilerParams(vmem_limit_bytes=16 * 2**20),
        name="join",
    )(rank, moving, still)


def swap(slots):
    count = slots.shape[0]
    stride = count
    while stride > 1:
        radix = 4 if stride % 4 == 0 else 2
        stride //= radix
        cut = slots.reshape(count // (radix * stride), radix, stride, *slots.shape[1:])
        parts = [cut[:, 0]]
        for step in range(1, radix):
            pairs = [(rank, rank ^ (step * stride)) for rank in range(count)]
            parts.append(lax.ppermute(cut[:, step], "az", pairs))
        slots = jnp.stack(parts, axis=1).reshape(slots.shape)
    return slots


def stress_kernel(
    info,
    fields,
    density,
    head,
    tail,
    before,
    after,
    straight_below,
    straight_above,
    whole,
    next_one,
    out,
    joined,
    vel,
    mass,
    px,
    py,
    pzz,
    heat,
):
    columns, cells, depth = density.shape
    share = out.shape[1]
    first, last, remainder = info[0], info[1], info[2]
    end = TOP + cells

    def place(far, near, ghost, start, jump):
        for component in range(3):
            added = jump if component == 1 else 0.0
            vel[component, near, TOP - 1 : end + 1] = (
                joined[component, pl.ds(start, cells + 2)] + added
            )
            vel[component, far, TOP:end] = joined[7 + component, pl.ds(start + 1, cells)] + added
        for row in range(4):
            mass[row, ghost] = joined[3 + row, pl.ds(start + 1, cells)]

    def lay(one, two):
        for row in range(PACKED):
            joined[row, 1 : cells + 1] = one[row]
            if two is not None:
                joined[row, cells + 1 : 2 * cells + 1] = two[row]
        final = one if two is None else two
        spot = (1 if two is None else 2) * cells + 1
        for component in range(3):
            joined[component, 0:1] = one[PACKED, 2 * component : 2 * component + 1]
            joined[component, spot : spot + 1] = final[PACKED, 2 * component + 1 : 2 * component + 2]

    below = (0, 1, 0)
    above = (columns + 3, columns + 2, columns + 1)

    @pl.when(first == 1)
    def _():
        lay(next_one, whole)
        place(*below, cells - remainder, shear_jump)

    @pl.when(first == 0)
    def _():
        lay(straight_below, None)
        place(*below, 0, 0.0)

    @pl.when(last == 1)
    def _():
        lay(whole, next_one)
        place(*above, remainder, -shear_jump)

    @pl.when(last == 0)
    def _():
        lay(straight_above, None)
        place(*above, 0, 0.0)

    vel[:, 2 : columns + 2, TOP:end] = fields[0:3]
    mass[0, 1 : columns + 1] = density[...]
    mass[1:4, 1 : columns + 1] = fields[3:6]
    for component in range(3):
        for column in range(columns):
            vel[component, 2 + column, TOP - 1 : TOP] = before[component, column : column + 1]
            vel[component, 2 + column, end : end + 1] = after[component, column : column + 1]

    for layer, spot, high, low in (
        (before, TOP - 1, (head, 0), (before, 7)),
        (after, end, (after, 7), (tail, 0)),
    ):
        grad_x, grad_y, grad_z = [], [], []
        for component in range(3):
            row = layer[component]
            left = jnp.concatenate(
                [vel[component, 1, spot : spot + 1], layer[component, 0 : columns - 1]], axis=0
            )
            right = jnp.concatenate(
                [layer[component, 1:columns], vel[component, columns + 2, spot : spot + 1]], axis=0
            )
            grad_x.append((right - left) * 0.5)
            grad_y.append((high[0][high[1] + component] - low[0][low[1] + component]) * 0.5)
            grad_z.append(vertical_slope(row))
        magnet = [layer[4], layer[5], layer[6]]
        gap, _, unit = stress(layer[3], magnet, grad_x, grad_y, grad_z)
        edge = gap * unit[1]
        parts = (edge * unit[0], edge * unit[1] - gap * (1.0 / 3.0), edge * unit[2])
        for row in range(3):
            for column in range(columns):
                py[row, 1 + column, spot : spot + 1] = parts[row][column : column + 1]

    def tensor_column(ghost, carry):
        here = ghost + 1
        grad_x = [
            (vel[i, here + 1, TOP:end] - vel[i, here - 1, TOP:end]) * 0.5 for i in range(3)
        ]
        grad_y = [
            (vel[i, here, TOP + 1 : end + 1] - vel[i, here, TOP - 1 : end - 1]) * 0.5
            for i in range(3)
        ]
        grad_z = [vertical_slope(vel[i, here, TOP:end]) for i in range(3)]
        magnet = [mass[1, ghost], mass[2, ghost], mass[3, ghost]]
        gap, anisotropy, unit = stress(mass[0, ghost], magnet, grad_x, grad_y, grad_z)
        third = gap * (1.0 / 3.0)
        along_x, along_y = gap * unit[0], gap * unit[1]
        px[0, ghost] = along_x * unit[0] - third
        cross = along_x * unit[1]
        px[1, ghost] = cross
        px[2, ghost] = along_x * unit[2]
        py[0, ghost, TOP:end] = cross
        py[1, ghost, TOP:end] = along_y * unit[1] - third
        py[2, ghost, TOP:end] = along_y * unit[2]
        pzz[ghost] = gap * unit[2] * unit[2] - third
        heat[ghost] = gap * anisotropy
        return carry

    lax.fori_loop(0, columns + 2, tensor_column, 0)

    def update_column(column, carry):
        ghost = column + 1
        inverse = 1.0 / mass[0, ghost]

        def slope(axis):
            return (px[axis, ghost + 1] - px[axis, ghost - 1]) * 0.5 + (
                py[axis, ghost, TOP + 1 : end + 1] - py[axis, ghost, TOP - 1 : end - 1]
            ) * 0.5

        vertical = (px[2, ghost], py[2, ghost, TOP:end], pzz[ghost])
        for axis in range(4):
            flat = column * 4 + axis
            slot = flat // share
            if axis < 3:
                force = slope(axis) + vertical_slope(vertical[axis])
                out[slot, flat % share] = fields[axis, column] + force * inverse
            else:
                out[slot, flat % share] = fields[6, column] + heat[ghost]
        return carry

    lax.fori_loop(0, columns, update_column, 0)


def updated_columns(info, fields, density, *layers):
    columns, cells, depth = density.shape
    tall = cells + 2 * TOP
    slots = lax.axis_size("az")
    smem = pl.BlockSpec(memory_space=pltpu.SMEM)
    vmem = pl.BlockSpec(memory_space=pltpu.VMEM)
    f32 = jnp.float32
    return pl.pallas_call(
        stress_kernel,
        out_shape=jax.ShapeDtypeStruct((slots, 4 * columns // slots, cells, depth), f32),
        in_specs=[smem] + [vmem] * 10,
        out_specs=vmem,
        scratch_shapes=[
            pltpu.VMEM((PACKED, 2 * cells + TOP, depth), f32),
            pltpu.VMEM((3, columns + 4, tall, depth), f32),
            pltpu.VMEM((4, columns + 2, cells, depth), f32),
            pltpu.VMEM((3, columns + 2, cells, depth), f32),
            pltpu.VMEM((3, columns + 2, tall, depth), f32),
            pltpu.VMEM((columns + 2, cells, depth), f32),
            pltpu.VMEM((columns + 2, cells, depth), f32),
        ],
        compiler_params=pltpu.CompilerParams(vmem_limit_bytes=24 * 2**20),
        name="stress_update",
    )(info, fields, density, *layers)


def move_kernel(quantities, mixed, rank, shift, frac, gathered, out, twice):
    slots, share, cells, depth = gathered.shape
    total = slots * cells
    me = rank[0]
    for item in range(share):
        column, _ = pair_of(me, item, share, quantities)
        fraction = frac[column].astype(jnp.float32) * (1.0 / FRAC_DEN)
        bend = fraction * (1.0 - fraction) * 0.25
        start = TOP + lax.rem(total - shift[column], total)

        def lay(slot, carry):
            rows = gathered[slot, item]
            spot = pl.multiple_of(TOP + (lax.bitwise_xor(me, slot) if mixed else slot) * cells, TOP)
            twice[item, pl.ds(spot, cells)] = rows
            twice[item, pl.ds(pl.multiple_of(spot + total, TOP), cells)] = rows
            return carry

        lax.fori_loop(0, slots, lay, 0, unroll=4)
        twice[item, 0:TOP] = twice[item, total : total + TOP]

        def blend(slot, carry):
            spot = start + (lax.bitwise_xor(me, slot) if mixed else slot) * cells
            back_two = twice[item, pl.ds(spot - 2, cells)]
            back_one = twice[item, pl.ds(spot - 1, cells)]
            centre = twice[item, pl.ds(spot, cells)]
            ahead = twice[item, pl.ds(spot + 1, cells)]
            out[slot, item] = (
                centre
                + fraction * (back_one - centre)
                + bend * ((centre - back_two) - (ahead - back_one))
            )
            return carry

        lax.fori_loop(0, slots, blend, 0, unroll=4)


def move_columns(gathered, quantities, mixed, rank, shift_int, frac_num):
    azimuths, share, cells, depth = gathered.shape
    smem = pl.BlockSpec(memory_space=pltpu.SMEM)
    vmem = pl.BlockSpec(memory_space=pltpu.VMEM)
    return pl.pallas_call(
        functools.partial(move_kernel, quantities, mixed),
        out_shape=jax.ShapeDtypeStruct(gathered.shape, jnp.float32),
        in_specs=[smem, smem, smem, vmem],
        out_specs=vmem,
        scratch_shapes=[pltpu.VMEM((share, 2 * azimuths * cells + TOP, depth), jnp.float32)],
        compiler_params=pltpu.CompilerParams(vmem_limit_bytes=16 * 2**20),
        name="move",
    )(rank, shift_int, frac_num, gathered)


def azimuthal_layers(head, tail):
    azimuths = lax.axis_size("az")
    even = lax.axis_index("az") % 2 == 0
    inner = [(az, az ^ 1) for az in range(azimuths)]
    outer = [(az, (az - 1 if az % 2 == 0 else az + 1) % azimuths) for az in range(azimuths)]
    far = lax.ppermute(jnp.where(even, head, tail), "az", outer)
    near = lax.ppermute(jnp.where(even, tail, head), "az", inner)
    return jnp.where(even, far, near), jnp.where(even, near, far)


def rims(blocks, low, high, before, after):
    radials = lax.axis_size("rad")
    azimuths = lax.axis_size("az")
    rad = lax.axis_index("rad")
    last = radials - 1

    def flat(rad, az):
        return rad * azimuths + az % azimuths

    def wrap(data, steps):
        pairs = [(flat(last, az), flat(0, az + steps)) for az in range(azimuths)]
        pairs += [(flat(0, az), flat(last, az - steps)) for az in range(azimuths)]
        return lax.ppermute(data, ("rad", "az"), pairs)

    def with_ends(main, column):
        ends = jnp.stack([before[0:3, column], after[0:3, column]], axis=1)
        ends = ends.reshape(1, 6, main.shape[-1])
        ends = jnp.pad(ends, ((0, 0), (0, main.shape[1] - 6), (0, 0)))
        return jnp.concatenate([main, ends], axis=0)

    low, high = with_ends(low, 0), with_ends(high, -1)
    edge = jnp.where(rad == 0, low, high)
    if radials == 2:
        other = jnp.where(rad == 0, high, low)
        below = above = lax.ppermute(other, "rad", [(0, 1), (1, 0)])
    else:
        below = lax.ppermute(high, "rad", [(i, i + 1) for i in range(last)])
        above = lax.ppermute(low, "rad", [(i + 1, i) for i in range(last)])

    def branch(steps):
        return lambda data: (wrap(data, steps), wrap(data, steps + 1))

    whole, next_one = lax.switch(blocks, [branch(steps) for steps in range(azimuths)], edge)
    return below, above, whole, next_one


def local(fields, density, shift_int, frac_num, boundary_shift):
    columns, cells, _ = density.shape
    radials = lax.axis_size("rad")
    rad = lax.axis_index("rad")
    shear_cells = boundary_shift[0]
    az = lax.axis_index("az")
    rank = az.reshape(1)
    head, tail, low, high, still = pack(rank, fields, density)
    before, after = azimuthal_layers(head, tail)
    before, after, still = lax.optimization_barrier((before, after, still))
    still = swap(still)
    layers = rims(shear_cells // cells, low, high, before, after)
    info = jnp.stack(
        [
            (rad == 0).astype(jnp.int32),
            (rad == radials - 1).astype(jnp.int32),
            shear_cells % cells,
            az,
        ]
    )
    moving = updated_columns(info, fields, density, head, tail, before, after, *layers)
    moving = lax.all_to_all(moving, "az", 0, 0, tiled=True)
    still = swap(move_columns(still, 4, True, rank, shift_int, frac_num))
    moving = move_columns(moving, 4, False, rank, shift_int, frac_num)
    moving = lax.all_to_all(moving, "az", 0, 0, tiled=True)
    return join(rank, moving, still, columns)


def solution(mesh):
    in_specs = (P(None, "rad", "az", None), P("rad", "az", None), P("rad"), P("rad"), P())
    out_specs = (P(None, "rad", "az", None), P("rad", "az", None))
    return jax.shard_map(local, mesh=mesh, in_specs=in_specs, out_specs=out_specs, check_vma=False)
```

```python
import functools

import jax
import jax.numpy as jnp
from jax import lax
from jax.experimental import pallas as pl
from jax.experimental.pallas import tpu as pltpu
from jax.sharding import PartitionSpec as P

FRAC_DEN = 64

shear_jump = 1.5
visc_step = 0.05
field_floor = 0.25

PACKED = 10
TOP = 8


def up_and_down(values):
    lane = lax.broadcasted_iota(jnp.int32, values.shape, values.ndim - 1)
    depth = values.shape[-1]
    up = pltpu.roll(values, depth - 1, values.ndim - 1)
    down = pltpu.roll(values, 1, values.ndim - 1)
    return jnp.where(lane == depth - 1, values, up), jnp.where(lane == 0, values, down)


def vertical_slope(values):
    up, down = up_and_down(values)
    return (up - down) * 0.5


def stress(density, magnet, grad_x, grad_y, grad_z):
    square = magnet[0] * magnet[0] + magnet[1] * magnet[1] + magnet[2] * magnet[2]
    inverse = lax.rsqrt(jnp.maximum(square, field_floor))
    unit = [component * inverse for component in magnet]
    slopes = (grad_x, grad_y, grad_z)
    aligned = None
    for direction in range(3):
        along = (
            unit[0] * slopes[direction][0]
            + unit[1] * slopes[direction][1]
            + unit[2] * slopes[direction][2]
        )
        term = unit[direction] * along
        aligned = term if aligned is None else aligned + term
    anisotropy = aligned - (grad_x[0] + grad_y[1] + grad_z[2]) * (1.0 / 3.0)
    gap = (3.0 * visc_step) * density * anisotropy
    return gap, anisotropy, unit


def pack_kernel(
    quantities, rank, fields_in, density_in, head, tail, low, high, still, fields, density, sems
):
    columns, cells, depth = density.shape
    slots, share = still.shape[0], still.shape[1]
    copies = [
        pltpu.make_async_copy(density_in, density, sems.at[0]),
        pltpu.make_async_copy(fields_in.at[0:6], fields, sems.at[1]),
    ]
    for copy in copies:
        copy.start()
    for copy in copies:
        copy.wait()

    def source(row):
        if row == 3:
            return density
        return fields.at[row if row < 3 else row - 1 if row < 7 else row - 7]

    for row in range(PACKED):
        second = 1 if row >= 7 else 0
        origin = source(row)
        low[row] = origin[second]
        high[row] = origin[columns - 1 - second]
        for column in range(columns):
            head[row, column : column + 1] = origin[column, second : second + 1]
            tail[row, column : column + 1] = origin[column, cells - 1 - second : cells - second]
    for slot in range(slots):
        for item in range(share):
            column, row = pair_of(lax.bitwise_xor(rank[0], slot), item, share, quantities)
            if isinstance(row, int):
                still[slot, item] = density[column] if row == 0 else fields[2 + row, column]
            else:
                still[slot, item] = jnp.where(
                    row == 0, density[column], fields[jnp.maximum(row, 1) + 2, column]
                )


def pair_of(rank, item, share, quantities):
    if share % quantities == 0:
        return rank * (share // quantities) + item // quantities, item % quantities
    flat = rank * share + item
    return flat // quantities, flat % quantities


def pack(rank, fields, density):
    columns, cells, depth = density.shape
    slots = lax.axis_size("az")
    share = 4 * columns // slots
    f32 = jnp.float32
    layer = jax.ShapeDtypeStruct((PACKED, columns, depth), f32)
    rim = jax.ShapeDtypeStruct((PACKED, cells, depth), f32)
    vmem = pl.BlockSpec(memory_space=pltpu.VMEM)
    return pl.pallas_call(
        functools.partial(pack_kernel, 4),
        out_shape=(
            layer,
            layer,
            rim,
            rim,
            jax.ShapeDtypeStruct((slots, share, cells, depth), f32),
        ),
        in_specs=[pl.BlockSpec(memory_space=pltpu.SMEM)] + [pl.BlockSpec(memory_space=pl.ANY)] * 2,
        out_specs=[vmem] * 5,
        scratch_shapes=[
            pltpu.VMEM((6, columns, cells, depth), f32),
            pltpu.VMEM((columns, cells, depth), f32),
            pltpu.SemaphoreType.DMA((2,)),
        ],
        compiler_params=pltpu.CompilerParams(vmem_limit_bytes=16 * 2**20),
        name="pack",
    )(rank, fields, density)


def join_kernel(quantities, rank, moving, still, new_fields, new_density):
    slots, share = still.shape[0], still.shape[1]
    for slot in range(slots):
        for item in range(share):
            column, row = pair_of(lax.bitwise_xor(rank[0], slot), item, share, quantities)
            if isinstance(row, int):
                new_fields[6 if row == 3 else row, column] = moving[slot, item]
                if row == 0:
                    new_density[column] = still[slot, item]
                else:
                    new_fields[2 + row, column] = still[slot, item]
            else:
                new_fields[jnp.where(row == 3, 6, row), column] = moving[slot, item]

                @pl.when(row == 0)
                def _():
                    new_density[column] = still[slot, item]

                @pl.when(row > 0)
                def _():
                    new_fields[2 + row, column] = still[slot, item]


def join(rank, moving, still, columns):
    _, _, cells, depth = still.shape
    f32 = jnp.float32
    vmem = pl.BlockSpec(memory_space=pltpu.VMEM)
    return pl.pallas_call(
        functools.partial(join_kernel, 4),
        out_shape=(
            jax.ShapeDtypeStruct((7, columns, cells, depth), f32),
            jax.ShapeDtypeStruct((columns, cells, depth), f32),
        ),
        in_specs=[pl.BlockSpec(memory_space=pltpu.SMEM), vmem, vmem],
        out_specs=[vmem] * 2,
        compiler_params=pltpu.CompilerParams(vmem_limit_bytes=16 * 2**20),
        name="join",
    )(rank, moving, still)


def swap(slots):
    count = slots.shape[0]
    stride = count
    while stride > 1:
        radix = 4 if stride % 4 == 0 else 2
        stride //= radix
        cut = slots.reshape(count // (radix * stride), radix, stride, *slots.shape[1:])
        parts = [cut[:, 0]]
        for step in range(1, radix):
            pairs = [(rank, rank ^ (step * stride)) for rank in range(count)]
            parts.append(lax.ppermute(cut[:, step], "az", pairs))
        slots = jnp.stack(parts, axis=1).reshape(slots.shape)
    return slots


def window_kernel(info, straight_below, straight_above, whole, next_one, head, tail, below, above, start, stop, joined):
    cells = below.shape[1]
    first, last, remainder = info[0], info[1], info[2]

    def shear(one, two, spot, out, jump):
        joined[:, 0:cells] = one[...]
        joined[:, cells : 2 * cells] = two[...]
        for row in range(PACKED):
            out[row] = joined[row, pl.ds(spot, cells)] + (jump if row in (1, 8) else 0.0)

    @pl.when(first == 1)
    def _():
        shear(next_one, whole, cells - remainder, below, shear_jump)

    @pl.when(first == 0)
    def _():
        below[...] = straight_below[...]

    @pl.when(last == 1)
    def _():
        shear(whole, next_one, remainder, above, -shear_jump)

    @pl.when(last == 0)
    def _():
        above[...] = straight_above[...]

    for layer, out, row in ((head, start, 0), (tail, stop, cells - 1)):
        out[0:PACKED] = layer[...]
        for component in range(3):
            for side, strip in ((0, below), (1, above)):
                spot = 2 * component + side
                out[PACKED, spot : spot + 1] = strip[component, row : row + 1]
        out[PACKED, 6 : out.shape[1]] = jnp.zeros((out.shape[1] - 6, out.shape[2]), jnp.float32)


def window(info, straight_below, straight_above, whole, next_one, head, tail):
    _, cells, depth = whole.shape
    columns = head.shape[1]
    f32 = jnp.float32
    vmem = pl.BlockSpec(memory_space=pltpu.VMEM)
    rim = jax.ShapeDtypeStruct((PACKED, cells, depth), f32)
    layer = jax.ShapeDtypeStruct((PACKED + 1, columns, depth), f32)
    return pl.pallas_call(
        window_kernel,
        out_shape=(rim, rim, layer, layer),
        in_specs=[pl.BlockSpec(memory_space=pltpu.SMEM)] + [vmem] * 6,
        out_specs=[vmem] * 4,
        scratch_shapes=[pltpu.VMEM((PACKED, 2 * cells, depth), f32)],
        name="window",
    )(info, straight_below, straight_above, whole, next_one, head, tail)


def stress_kernel(
    info,
    fields,
    density,
    head,
    tail,
    before,
    after,
    below,
    above,
    out,
    vel,
    mass,
    px,
    py,
    pzz,
    heat,
):
    columns, cells, depth = density.shape
    share = out.shape[1]
    end = TOP + cells

    for strip, far, near, ghost, corner in (
        (below, 0, 1, 0, 0),
        (above, columns + 3, columns + 2, columns + 1, 1),
    ):
        for component in range(3):
            spot = 2 * component + corner
            vel[component, near, TOP:end] = strip[component]
            vel[component, near, TOP - 1 : TOP] = before[PACKED, spot : spot + 1]
            vel[component, near, end : end + 1] = after[PACKED, spot : spot + 1]
            vel[component, far, TOP:end] = strip[7 + component]
        for row in range(4):
            mass[row, ghost] = strip[3 + row]
    vel[:, 2 : columns + 2, TOP:end] = fields[0:3]
    mass[0, 1 : columns + 1] = density[...]
    mass[1:4, 1 : columns + 1] = fields[3:6]
    for component in range(3):
        for column in range(columns):
            vel[component, 2 + column, TOP - 1 : TOP] = before[component, column : column + 1]
            vel[component, 2 + column, end : end + 1] = after[component, column : column + 1]

    for layer, spot, high, low in (
        (before, TOP - 1, (head, 0), (before, 7)),
        (after, end, (after, 7), (tail, 0)),
    ):
        grad_x, grad_y, grad_z = [], [], []
        for component in range(3):
            row = layer[component]
            left = jnp.concatenate(
                [vel[component, 1, spot : spot + 1], layer[component, 0 : columns - 1]], axis=0
            )
            right = jnp.concatenate(
                [layer[component, 1:columns], vel[component, columns + 2, spot : spot + 1]], axis=0
            )
            grad_x.append((right - left) * 0.5)
            grad_y.append((high[0][high[1] + component] - low[0][low[1] + component]) * 0.5)
            grad_z.append(vertical_slope(row))
        magnet = [layer[4], layer[5], layer[6]]
        gap, _, unit = stress(layer[3], magnet, grad_x, grad_y, grad_z)
        edge = gap * unit[1]
        parts = (edge * unit[0], edge * unit[1] - gap * (1.0 / 3.0), edge * unit[2])
        for row in range(3):
            for column in range(columns):
                py[row, 1 + column, spot : spot + 1] = parts[row][column : column + 1]

    def tensor_column(ghost, carry):
        here = ghost + 1
        grad_x = [
            (vel[i, here + 1, TOP:end] - vel[i, here - 1, TOP:end]) * 0.5 for i in range(3)
        ]
        grad_y = [
            (vel[i, here, TOP + 1 : end + 1] - vel[i, here, TOP - 1 : end - 1]) * 0.5
            for i in range(3)
        ]
        grad_z = [vertical_slope(vel[i, here, TOP:end]) for i in range(3)]
        magnet = [mass[1, ghost], mass[2, ghost], mass[3, ghost]]
        gap, anisotropy, unit = stress(mass[0, ghost], magnet, grad_x, grad_y, grad_z)
        third = gap * (1.0 / 3.0)
        along_x, along_y = gap * unit[0], gap * unit[1]
        px[0, ghost] = along_x * unit[0] - third
        cross = along_x * unit[1]
        px[1, ghost] = cross
        px[2, ghost] = along_x * unit[2]
        py[0, ghost, TOP:end] = cross
        py[1, ghost, TOP:end] = along_y * unit[1] - third
        py[2, ghost, TOP:end] = along_y * unit[2]
        pzz[ghost] = gap * unit[2] * unit[2] - third
        heat[ghost] = gap * anisotropy
        return carry

    lax.fori_loop(0, columns + 2, tensor_column, 0, unroll=3)

    def update_column(column, carry):
        ghost = column + 1
        inverse = 1.0 / mass[0, ghost]

        def slope(axis):
            return (px[axis, ghost + 1] - px[axis, ghost - 1]) * 0.5 + (
                py[axis, ghost, TOP + 1 : end + 1] - py[axis, ghost, TOP - 1 : end - 1]
            ) * 0.5

        vertical = (px[2, ghost], py[2, ghost, TOP:end], pzz[ghost])
        for axis in range(4):
            flat = column * 4 + axis
            slot = lax.bitwise_xor(info[0], flat // share)
            if axis < 3:
                force = slope(axis) + vertical_slope(vertical[axis])
                out[slot, flat % share] = fields[axis, column] + force * inverse
            else:
                out[slot, flat % share] = fields[6, column] + heat[ghost]
        return carry

    lax.fori_loop(0, columns, update_column, 0, unroll=4)


def updated_columns(info, fields, density, *layers):
    columns, cells, depth = density.shape
    tall = cells + 2 * TOP
    slots = lax.axis_size("az")
    smem = pl.BlockSpec(memory_space=pltpu.SMEM)
    vmem = pl.BlockSpec(memory_space=pltpu.VMEM)
    f32 = jnp.float32
    return pl.pallas_call(
        stress_kernel,
        out_shape=jax.ShapeDtypeStruct((slots, 4 * columns // slots, cells, depth), f32),
        in_specs=[smem] + [vmem] * 8,
        out_specs=vmem,
        scratch_shapes=[
            pltpu.VMEM((3, columns + 4, tall, depth), f32),
            pltpu.VMEM((4, columns + 2, cells, depth), f32),
            pltpu.VMEM((3, columns + 2, cells, depth), f32),
            pltpu.VMEM((3, columns + 2, tall, depth), f32),
            pltpu.VMEM((columns + 2, cells, depth), f32),
            pltpu.VMEM((columns + 2, cells, depth), f32),
        ],
        compiler_params=pltpu.CompilerParams(vmem_limit_bytes=24 * 2**20),
        name="stress_update",
    )(info, fields, density, *layers)


def move_kernel(quantities, rank, shift, frac, gathered, out, twice):
    slots, share, cells, depth = gathered.shape
    total = slots * cells
    me = rank[0]
    for item in range(share):
        column, _ = pair_of(me, item, share, quantities)
        fraction = frac[column].astype(jnp.float32) * (1.0 / FRAC_DEN)
        bend = fraction * (1.0 - fraction) * 0.25
        start = TOP + lax.rem(total - shift[column], total)

        def lay(slot, carry):
            rows = gathered[slot, item]
            spot = pl.multiple_of(TOP + lax.bitwise_xor(me, slot) * cells, TOP)
            twice[item, pl.ds(spot, cells)] = rows
            twice[item, pl.ds(pl.multiple_of(spot + total, TOP), cells)] = rows
            return carry

        lax.fori_loop(0, slots, lay, 0, unroll=4)
        twice[item, 0:TOP] = twice[item, total : total + TOP]

        def blend(slot, carry):
            spot = start + lax.bitwise_xor(me, slot) * cells
            back_two = twice[item, pl.ds(spot - 2, cells)]
            back_one = twice[item, pl.ds(spot - 1, cells)]
            centre = twice[item, pl.ds(spot, cells)]
            ahead = twice[item, pl.ds(spot + 1, cells)]
            out[slot, item] = (
                centre
                + fraction * (back_one - centre)
                + bend * ((centre - back_two) - (ahead - back_one))
            )
            return carry

        lax.fori_loop(0, slots, blend, 0, unroll=4)


def move_columns(gathered, quantities, rank, shift_int, frac_num):
    azimuths, share, cells, depth = gathered.shape
    smem = pl.BlockSpec(memory_space=pltpu.SMEM)
    vmem = pl.BlockSpec(memory_space=pltpu.VMEM)
    return pl.pallas_call(
        functools.partial(move_kernel, quantities),
        out_shape=jax.ShapeDtypeStruct(gathered.shape, jnp.float32),
        in_specs=[smem, smem, smem, vmem],
        out_specs=vmem,
        scratch_shapes=[pltpu.VMEM((share, 2 * azimuths * cells + TOP, depth), jnp.float32)],
        compiler_params=pltpu.CompilerParams(vmem_limit_bytes=16 * 2**20),
        name="move",
    )(rank, shift_int, frac_num, gathered)


def azimuthal_layers(head, tail):
    azimuths = lax.axis_size("az")
    even = lax.axis_index("az") % 2 == 0
    inner = [(az, az ^ 1) for az in range(azimuths)]
    outer = [(az, (az - 1 if az % 2 == 0 else az + 1) % azimuths) for az in range(azimuths)]
    far = lax.ppermute(jnp.where(even, head, tail), "az", outer)
    near = lax.ppermute(jnp.where(even, tail, head), "az", inner)
    return jnp.where(even, far, near), jnp.where(even, near, far)


def rims(blocks, low, high):
    radials = lax.axis_size("rad")
    azimuths = lax.axis_size("az")
    rad = lax.axis_index("rad")
    last = radials - 1

    def flat(rad, az):
        return rad * azimuths + az % azimuths

    def wrap(data, steps):
        pairs = [(flat(last, az), flat(0, az + steps)) for az in range(azimuths)]
        pairs += [(flat(0, az), flat(last, az - steps)) for az in range(azimuths)]
        return lax.ppermute(data, ("rad", "az"), pairs)

    edge = jnp.where(rad == 0, low, high)
    if radials == 2:
        other = jnp.where(rad == 0, high, low)
        below = above = lax.ppermute(other, "rad", [(0, 1), (1, 0)])
    else:
        below = lax.ppermute(high, "rad", [(i, i + 1) for i in range(last)])
        above = lax.ppermute(low, "rad", [(i + 1, i) for i in range(last)])

    def branch(steps):
        return lambda data: (wrap(data, steps), wrap(data, steps + 1))

    whole, next_one = lax.switch(blocks, [branch(steps) for steps in range(azimuths)], edge)
    return below, above, whole, next_one


def local(fields, density, shift_int, frac_num, boundary_shift):
    columns, cells, _ = density.shape
    radials = lax.axis_size("rad")
    rad = lax.axis_index("rad")
    shear_cells = boundary_shift[0]
    rank = lax.axis_index("az").reshape(1)
    head, tail, low, high, still = pack(rank, fields, density)
    info = jnp.stack(
        [
            (rad == 0).astype(jnp.int32),
            (rad == radials - 1).astype(jnp.int32),
            shear_cells % cells,
        ]
    )
    below, above, start, stop = window(info, *rims(shear_cells // cells, low, high), head, tail)
    still, start, stop = lax.optimization_barrier((still, start, stop))
    before, after = azimuthal_layers(start, stop)
    still = swap(still)
    moving = updated_columns(rank, fields, density, head, tail, before, after, below, above)
    moving = swap(moving)
    still = swap(move_columns(still, 4, rank, shift_int, frac_num))
    moving = swap(move_columns(moving, 4, rank, shift_int, frac_num))
    return join(rank, moving, still, columns)


def solution(mesh):
    in_specs = (P(None, "rad", "az", None), P("rad", "az", None), P("rad"), P("rad"), P())
    out_specs = (P(None, "rad", "az", None), P("rad", "az", None))
    return jax.shard_map(local, mesh=mesh, in_specs=in_specs, out_specs=out_specs, check_vma=False)
```

```python
import functools

import jax
import jax.numpy as jnp
from jax import lax
from jax.experimental import pallas as pl
from jax.experimental.pallas import tpu as pltpu
from jax.sharding import PartitionSpec as P

FRAC_DEN = 64

shear_jump = 1.5
visc_step = 0.05
field_floor = 0.25

PACKED = 10
TOP = 8


def up_and_down(values):
    lane = lax.broadcasted_iota(jnp.int32, values.shape, values.ndim - 1)
    depth = values.shape[-1]
    up = pltpu.roll(values, depth - 1, values.ndim - 1)
    down = pltpu.roll(values, 1, values.ndim - 1)
    return jnp.where(lane == depth - 1, values, up), jnp.where(lane == 0, values, down)


def vertical_slope(values):
    up, down = up_and_down(values)
    return (up - down) * 0.5


def stress(density, magnet, grad_x, grad_y, grad_z):
    square = magnet[0] * magnet[0] + magnet[1] * magnet[1] + magnet[2] * magnet[2]
    inverse = lax.rsqrt(jnp.maximum(square, field_floor))
    unit = [component * inverse for component in magnet]
    slopes = (grad_x, grad_y, grad_z)
    aligned = None
    for direction in range(3):
        along = (
            unit[0] * slopes[direction][0]
            + unit[1] * slopes[direction][1]
            + unit[2] * slopes[direction][2]
        )
        term = unit[direction] * along
        aligned = term if aligned is None else aligned + term
    anisotropy = aligned - (grad_x[0] + grad_y[1] + grad_z[2]) * (1.0 / 3.0)
    gap = (3.0 * visc_step) * density * anisotropy
    return gap, anisotropy, unit


def pack_kernel(
    quantities, rank, fields_in, density_in, head, tail, low, high, still, fields, density, sems
):
    columns, cells, depth = density.shape
    slots, share = still.shape[0], still.shape[1]
    copies = [
        pltpu.make_async_copy(density_in, density, sems.at[0]),
        pltpu.make_async_copy(fields_in.at[0:6], fields, sems.at[1]),
    ]
    for copy in copies:
        copy.start()
    for copy in copies:
        copy.wait()

    def source(row):
        if row == 3:
            return density
        return fields.at[row if row < 3 else row - 1 if row < 7 else row - 7]

    for row in range(PACKED):
        second = 1 if row >= 7 else 0
        origin = source(row)
        low[row] = origin[second]
        high[row] = origin[columns - 1 - second]
        for column in range(columns):
            head[row, column : column + 1] = origin[column, second : second + 1]
            tail[row, column : column + 1] = origin[column, cells - 1 - second : cells - second]
    for slot in range(slots):
        for item in range(share):
            column, row = pair_of(lax.bitwise_xor(rank[0], slot), item, share, quantities)
            if isinstance(row, int):
                still[slot, item] = density[column] if row == 0 else fields[2 + row, column]
            else:
                still[slot, item] = jnp.where(
                    row == 0, density[column], fields[jnp.maximum(row, 1) + 2, column]
                )


def pair_of(rank, item, share, quantities):
    if share % quantities == 0:
        return rank * (share // quantities) + item // quantities, item % quantities
    flat = rank * share + item
    return flat // quantities, flat % quantities


def pack(rank, fields, density):
    columns, cells, depth = density.shape
    slots = lax.axis_size("az")
    share = 4 * columns // slots
    f32 = jnp.float32
    layer = jax.ShapeDtypeStruct((PACKED, columns, depth), f32)
    rim = jax.ShapeDtypeStruct((PACKED, cells, depth), f32)
    vmem = pl.BlockSpec(memory_space=pltpu.VMEM)
    return pl.pallas_call(
        functools.partial(pack_kernel, 4),
        out_shape=(
            layer,
            layer,
            rim,
            rim,
            jax.ShapeDtypeStruct((slots, share, cells, depth), f32),
        ),
        in_specs=[pl.BlockSpec(memory_space=pltpu.SMEM)] + [pl.BlockSpec(memory_space=pltpu.HBM)] * 2,
        out_specs=[vmem] * 5,
        scratch_shapes=[
            pltpu.VMEM((6, columns, cells, depth), f32),
            pltpu.VMEM((columns, cells, depth), f32),
            pltpu.SemaphoreType.DMA((2,)),
        ],
        compiler_params=pltpu.CompilerParams(vmem_limit_bytes=16 * 2**20),
        name="pack",
    )(rank, fields, density)


def join_kernel(quantities, rank, moving, still, new_fields, new_density):
    slots, share = still.shape[0], still.shape[1]
    for slot in range(slots):
        for item in range(share):
            column, row = pair_of(lax.bitwise_xor(rank[0], slot), item, share, quantities)
            if isinstance(row, int):
                new_fields[6 if row == 3 else row, column] = moving[slot, item]
                if row == 0:
                    new_density[column] = still[slot, item]
                else:
                    new_fields[2 + row, column] = still[slot, item]
            else:
                new_fields[jnp.where(row == 3, 6, row), column] = moving[slot, item]

                @pl.when(row == 0)
                def _():
                    new_density[column] = still[slot, item]

                @pl.when(row > 0)
                def _():
                    new_fields[2 + row, column] = still[slot, item]


def join(rank, moving, still, columns):
    _, _, cells, depth = still.shape
    f32 = jnp.float32
    vmem = pl.BlockSpec(memory_space=pltpu.VMEM)
    return pl.pallas_call(
        functools.partial(join_kernel, 4),
        out_shape=(
            jax.ShapeDtypeStruct((7, columns, cells, depth), f32),
            jax.ShapeDtypeStruct((columns, cells, depth), f32),
        ),
        in_specs=[pl.BlockSpec(memory_space=pltpu.SMEM), vmem, vmem],
        out_specs=[vmem] * 2,
        compiler_params=pltpu.CompilerParams(vmem_limit_bytes=16 * 2**20),
        name="join",
    )(rank, moving, still)


def digit_radix(span):
    return 4 if span % 4 == 0 else 2


def send_step(cut, step):
    radix, stride = cut.shape[1], cut.shape[2]
    count = cut.shape[0] * radix * stride
    pairs = [(rank, rank ^ (step * stride)) for rank in range(count)]
    return lax.ppermute(cut[:, step], "az", pairs)


def swap(slots, span=None):
    span = slots.shape[0] if span is None else span
    while span > 1:
        radix = digit_radix(span)
        span //= radix
        cut = slots.reshape(-1, radix, span, *slots.shape[1:])
        parts = [cut[:, 0]] + [send_step(cut, step) for step in range(1, radix)]
        slots = jnp.stack(parts, axis=1).reshape(slots.shape)
    return slots


def stress_kernel(
    info,
    fields,
    density,
    head,
    tail,
    before,
    after,
    straight_below,
    straight_above,
    whole,
    next_one,
    out,
    joined,
    vel,
    mass,
    px,
    py,
    pzz,
    heat,
):
    columns, cells, depth = density.shape
    share = out.shape[1]
    first, last, remainder = info[0], info[1], info[2]
    end = TOP + cells

    def place(far, near, ghost, start, jump):
        for component in range(3):
            added = jump if component == 1 else 0.0
            vel[component, near, TOP - 1 : end + 1] = (
                joined[component, pl.ds(start, cells + 2)] + added
            )
            vel[component, far, TOP:end] = joined[7 + component, pl.ds(start + 1, cells)] + added
        for row in range(4):
            mass[row, ghost] = joined[3 + row, pl.ds(start + 1, cells)]

    def lay(one, two):
        for row in range(PACKED):
            joined[row, 1 : cells + 1] = one[row]
            if two is not None:
                joined[row, cells + 1 : 2 * cells + 1] = two[row]
        final = one if two is None else two
        spot = (1 if two is None else 2) * cells + 1
        for component in range(3):
            joined[component, 0:1] = one[PACKED, 2 * component : 2 * component + 1]
            joined[component, spot : spot + 1] = final[PACKED, 2 * component + 1 : 2 * component + 2]

    below = (0, 1, 0)
    above = (columns + 3, columns + 2, columns + 1)

    @pl.when(first == 1)
    def _():
        lay(next_one, whole)
        place(*below, cells - remainder, shear_jump)

    @pl.when(first == 0)
    def _():
        lay(straight_below, None)
        place(*below, 0, 0.0)

    @pl.when(last == 1)
    def _():
        lay(whole, next_one)
        place(*above, remainder, -shear_jump)

    @pl.when(last == 0)
    def _():
        lay(straight_above, None)
        place(*above, 0, 0.0)

    vel[:, 2 : columns + 2, TOP:end] = fields[0:3]
    mass[0, 1 : columns + 1] = density[...]
    mass[1:4, 1 : columns + 1] = fields[3:6]
    for component in range(3):
        for column in range(columns):
            vel[component, 2 + column, TOP - 1 : TOP] = before[component, column : column + 1]
            vel[component, 2 + column, end : end + 1] = after[component, column : column + 1]

    for layer, spot, high, low in (
        (before, TOP - 1, (head, 0), (before, 7)),
        (after, end, (after, 7), (tail, 0)),
    ):
        grad_x, grad_y, grad_z = [], [], []
        for component in range(3):
            row = layer[component]
            left = jnp.concatenate(
                [vel[component, 1, spot : spot + 1], layer[component, 0 : columns - 1]], axis=0
            )
            right = jnp.concatenate(
                [layer[component, 1:columns], vel[component, columns + 2, spot : spot + 1]], axis=0
            )
            grad_x.append((right - left) * 0.5)
            grad_y.append((high[0][high[1] + component] - low[0][low[1] + component]) * 0.5)
            grad_z.append(vertical_slope(row))
        magnet = [layer[4], layer[5], layer[6]]
        gap, _, unit = stress(layer[3], magnet, grad_x, grad_y, grad_z)
        edge = gap * unit[1]
        parts = (edge * unit[0], edge * unit[1] - gap * (1.0 / 3.0), edge * unit[2])
        for row in range(3):
            for column in range(columns):
                py[row, 1 + column, spot : spot + 1] = parts[row][column : column + 1]

    def tensor_column(ghost, carry):
        here = ghost + 1
        grad_x = [
            (vel[i, here + 1, TOP:end] - vel[i, here - 1, TOP:end]) * 0.5 for i in range(3)
        ]
        grad_y = [
            (vel[i, here, TOP + 1 : end + 1] - vel[i, here, TOP - 1 : end - 1]) * 0.5
            for i in range(3)
        ]
        grad_z = [vertical_slope(vel[i, here, TOP:end]) for i in range(3)]
        magnet = [mass[1, ghost], mass[2, ghost], mass[3, ghost]]
        gap, anisotropy, unit = stress(mass[0, ghost], magnet, grad_x, grad_y, grad_z)
        third = gap * (1.0 / 3.0)
        along_x, along_y = gap * unit[0], gap * unit[1]
        px[0, ghost] = along_x * unit[0] - third
        cross = along_x * unit[1]
        px[1, ghost] = cross
        px[2, ghost] = along_x * unit[2]
        py[0, ghost, TOP:end] = cross
        py[1, ghost, TOP:end] = along_y * unit[1] - third
        py[2, ghost, TOP:end] = along_y * unit[2]
        pzz[ghost] = gap * unit[2] * unit[2] - third
        heat[ghost] = gap * anisotropy
        return carry

    lax.fori_loop(0, columns + 2, tensor_column, 0, unroll=3)

    def update_column(column, carry):
        ghost = column + 1
        inverse = 1.0 / mass[0, ghost]

        def slope(axis):
            return (px[axis, ghost + 1] - px[axis, ghost - 1]) * 0.5 + (
                py[axis, ghost, TOP + 1 : end + 1] - py[axis, ghost, TOP - 1 : end - 1]
            ) * 0.5

        vertical = (px[2, ghost], py[2, ghost, TOP:end], pzz[ghost])
        for axis in range(4):
            flat = column * 4 + axis
            slot = lax.bitwise_xor(info[3], flat // share)
            if axis < 3:
                force = slope(axis) + vertical_slope(vertical[axis])
                out[slot, flat % share] = fields[axis, column] + force * inverse
            else:
                out[slot, flat % share] = fields[6, column] + heat[ghost]
        return carry

    lax.fori_loop(0, columns, update_column, 0, unroll=4)


def updated_columns(info, fields, density, *layers):
    columns, cells, depth = density.shape
    tall = cells + 2 * TOP
    slots = lax.axis_size("az")
    smem = pl.BlockSpec(memory_space=pltpu.SMEM)
    vmem = pl.BlockSpec(memory_space=pltpu.VMEM)
    f32 = jnp.float32
    return pl.pallas_call(
        stress_kernel,
        out_shape=jax.ShapeDtypeStruct((slots, 4 * columns // slots, cells, depth), f32),
        in_specs=[smem] + [vmem] * 10,
        out_specs=vmem,
        scratch_shapes=[
            pltpu.VMEM((PACKED, 2 * cells + TOP, depth), f32),
            pltpu.VMEM((3, columns + 4, tall, depth), f32),
            pltpu.VMEM((4, columns + 2, cells, depth), f32),
            pltpu.VMEM((3, columns + 2, cells, depth), f32),
            pltpu.VMEM((3, columns + 2, tall, depth), f32),
            pltpu.VMEM((columns + 2, cells, depth), f32),
            pltpu.VMEM((columns + 2, cells, depth), f32),
        ],
        compiler_params=pltpu.CompilerParams(vmem_limit_bytes=24 * 2**20),
        name="stress_update",
    )(info, fields, density, *layers)


def move_kernel(quantities, rank, shift, frac, gathered, out, twice):
    slots, share, cells, depth = gathered.shape
    total = slots * cells
    me = rank[0]
    for item in range(share):
        column, _ = pair_of(me, item, share, quantities)
        fraction = frac[column].astype(jnp.float32) * (1.0 / FRAC_DEN)
        bend = fraction * (1.0 - fraction) * 0.25
        start = TOP + lax.rem(total - shift[column], total)

        def lay(slot, carry):
            rows = gathered[slot, item]
            spot = pl.multiple_of(TOP + lax.bitwise_xor(me, slot) * cells, TOP)
            twice[item, pl.ds(spot, cells)] = rows
            twice[item, pl.ds(pl.multiple_of(spot + total, TOP), cells)] = rows
            return carry

        lax.fori_loop(0, slots, lay, 0, unroll=4)
        twice[item, 0:TOP] = twice[item, total : total + TOP]

        def blend(slot, carry):
            spot = start + lax.bitwise_xor(me, slot) * cells
            back_two = twice[item, pl.ds(spot - 2, cells)]
            back_one = twice[item, pl.ds(spot - 1, cells)]
            centre = twice[item, pl.ds(spot, cells)]
            ahead = twice[item, pl.ds(spot + 1, cells)]
            out[slot, item] = (
                centre
                + fraction * (back_one - centre)
                + bend * ((centre - back_two) - (ahead - back_one))
            )
            return carry

        lax.fori_loop(0, slots, blend, 0, unroll=4)


def move_columns(gathered, quantities, rank, shift_int, frac_num):
    azimuths, share, cells, depth = gathered.shape
    smem = pl.BlockSpec(memory_space=pltpu.SMEM)
    vmem = pl.BlockSpec(memory_space=pltpu.VMEM)
    return pl.pallas_call(
        functools.partial(move_kernel, quantities),
        out_shape=jax.ShapeDtypeStruct(gathered.shape, jnp.float32),
        in_specs=[smem, smem, smem, vmem],
        out_specs=vmem,
        scratch_shapes=[pltpu.VMEM((share, 2 * azimuths * cells + TOP, depth), jnp.float32)],
        compiler_params=pltpu.CompilerParams(vmem_limit_bytes=16 * 2**20),
        name="move",
    )(rank, shift_int, frac_num, gathered)


def azimuthal_layers(head, tail):
    azimuths = lax.axis_size("az")
    even = lax.axis_index("az") % 2 == 0
    inner = [(az, az ^ 1) for az in range(azimuths)]
    outer = [(az, (az - 1 if az % 2 == 0 else az + 1) % azimuths) for az in range(azimuths)]
    far = lax.ppermute(jnp.where(even, head, tail), "az", outer)
    near = lax.ppermute(jnp.where(even, tail, head), "az", inner)
    return jnp.where(even, far, near), jnp.where(even, near, far)


def rims(blocks, low, high, before, after):
    radials = lax.axis_size("rad")
    azimuths = lax.axis_size("az")
    rad = lax.axis_index("rad")
    last = radials - 1

    def flat(rad, az):
        return rad * azimuths + az % azimuths

    def wrap(data, steps):
        pairs = [(flat(last, az), flat(0, az + steps)) for az in range(azimuths)]
        pairs += [(flat(0, az), flat(last, az - steps)) for az in range(azimuths)]
        return lax.ppermute(data, ("rad", "az"), pairs)

    def with_ends(main, column):
        ends = jnp.stack([before[0:3, column], after[0:3, column]], axis=1)
        ends = ends.reshape(1, 6, main.shape[-1])
        ends = jnp.pad(ends, ((0, 0), (0, main.shape[1] - 6), (0, 0)))
        return jnp.concatenate([main, ends], axis=0)

    low, high = with_ends(low, 0), with_ends(high, -1)
    edge = jnp.where(rad == 0, low, high)
    if radials == 2:
        other = jnp.where(rad == 0, high, low)
        below = above = lax.ppermute(other, "rad", [(0, 1), (1, 0)])
    else:
        below = lax.ppermute(high, "rad", [(i, i + 1) for i in range(last)])
        above = lax.ppermute(low, "rad", [(i + 1, i) for i in range(last)])

    def branch(steps):
        return lambda data: (wrap(data, steps), wrap(data, steps + 1))

    whole, next_one = lax.switch(blocks, [branch(steps) for steps in range(azimuths)], edge)
    return below, above, whole, next_one


def local(fields, density, shift_int, frac_num, boundary_shift):
    columns, cells, _ = density.shape
    radials = lax.axis_size("rad")
    rad = lax.axis_index("rad")
    shear_cells = boundary_shift[0]
    az = lax.axis_index("az")
    rank = az.reshape(1)
    head, tail, low, high, still = pack(rank, fields, density)
    before, after = azimuthal_layers(head, tail)
    count = still.shape[0]
    radix = digit_radix(count)
    span = count // radix
    cut = still.reshape(1, radix, span, *still.shape[1:])
    nearest = send_step(cut, 1)
    before, after, nearest, cut = lax.optimization_barrier((before, after, nearest, cut))
    parts = [cut[:, 0], nearest] + [send_step(cut, step) for step in range(2, radix)]
    layers = rims(shear_cells // cells, low, high, before, after)
    parts, layers = lax.optimization_barrier((parts, layers))
    still = swap(jnp.stack(parts, axis=1).reshape(still.shape), span)
    info = jnp.stack(
        [
            (rad == 0).astype(jnp.int32),
            (rad == radials - 1).astype(jnp.int32),
            shear_cells % cells,
            az,
        ]
    )
    moving = updated_columns(info, fields, density, head, tail, before, after, *layers)
    moving = swap(moving)
    still = swap(move_columns(still, 4, rank, shift_int, frac_num))
    moving = swap(move_columns(moving, 4, rank, shift_int, frac_num))
    return join(rank, moving, still, columns)


def solution(mesh):
    in_specs = (P(None, "rad", "az", None), P("rad", "az", None), P("rad"), P("rad"), P())
    out_specs = (P(None, "rad", "az", None), P("rad", "az", None))
    return jax.shard_map(local, mesh=mesh, in_specs=in_specs, out_specs=out_specs, check_vma=False)
```

```python
import functools

import jax
import jax.numpy as jnp
from jax import lax
from jax.experimental import pallas as pl
from jax.experimental.pallas import tpu as pltpu
from jax.sharding import PartitionSpec as P

FRAC_DEN = 64

shear_jump = 1.5
visc_step = 0.05
field_floor = 0.25

PACKED = 10
TOP = 8


def up_and_down(values):
    lane = lax.broadcasted_iota(jnp.int32, values.shape, values.ndim - 1)
    depth = values.shape[-1]
    up = pltpu.roll(values, depth - 1, values.ndim - 1)
    down = pltpu.roll(values, 1, values.ndim - 1)
    return jnp.where(lane == depth - 1, values, up), jnp.where(lane == 0, values, down)


def vertical_slope(values):
    up, down = up_and_down(values)
    return (up - down) * 0.5


def stress(density, magnet, grad_x, grad_y, grad_z):
    square = magnet[0] * magnet[0] + magnet[1] * magnet[1] + magnet[2] * magnet[2]
    inverse = lax.rsqrt(jnp.maximum(square, field_floor))
    unit = [component * inverse for component in magnet]
    slopes = (grad_x, grad_y, grad_z)
    aligned = None
    for direction in range(3):
        along = (
            unit[0] * slopes[direction][0]
            + unit[1] * slopes[direction][1]
            + unit[2] * slopes[direction][2]
        )
        term = unit[direction] * along
        aligned = term if aligned is None else aligned + term
    anisotropy = aligned - (grad_x[0] + grad_y[1] + grad_z[2]) * (1.0 / 3.0)
    gap = (3.0 * visc_step) * density * anisotropy
    return gap, anisotropy, unit


def pack_kernel(
    quantities, rank, fields_in, density_in, head, tail, low, high, still, fields, density, sems
):
    columns, cells, depth = density.shape
    slots, share = still.shape[0], still.shape[1]
    copies = [
        pltpu.make_async_copy(density_in, density, sems.at[0]),
        pltpu.make_async_copy(fields_in, fields, sems.at[1]),
    ]
    for copy in copies:
        copy.start()
    for copy in copies:
        copy.wait()

    def source(row):
        if row == 3:
            return density
        return fields.at[row if row < 3 else row - 1 if row < 7 else row - 7]

    for row in range(PACKED):
        second = 1 if row >= 7 else 0
        origin = source(row)
        low[row] = origin[second]
        high[row] = origin[columns - 1 - second]
        for column in range(columns):
            head[row, column : column + 1] = origin[column, second : second + 1]
            tail[row, column : column + 1] = origin[column, cells - 1 - second : cells - second]
    for slot in range(slots):
        for item in range(share):
            column, row = pair_of(lax.bitwise_xor(rank[0], slot), item, share, quantities)
            if isinstance(row, int):
                still[slot, item] = density[column] if row == 0 else fields[2 + row, column]
            else:
                still[slot, item] = jnp.where(
                    row == 0, density[column], fields[jnp.maximum(row, 1) + 2, column]
                )


def pair_of(rank, item, share, quantities):
    if share % quantities == 0:
        return rank * (share // quantities) + item // quantities, item % quantities
    flat = rank * share + item
    return flat // quantities, flat % quantities


def pack(rank, fields, density):
    columns, cells, depth = density.shape
    slots = lax.axis_size("az")
    share = 4 * columns // slots
    f32 = jnp.float32
    layer = jax.ShapeDtypeStruct((PACKED, columns, depth), f32)
    rim = jax.ShapeDtypeStruct((PACKED, cells, depth), f32)
    vmem = pl.BlockSpec(memory_space=pltpu.VMEM)
    return pl.pallas_call(
        functools.partial(pack_kernel, 4),
        out_shape=(
            layer,
            layer,
            rim,
            rim,
            jax.ShapeDtypeStruct((slots, share, cells, depth), f32),
            jax.ShapeDtypeStruct(fields.shape, f32),
            jax.ShapeDtypeStruct(density.shape, f32),
        ),
        in_specs=[pl.BlockSpec(memory_space=pltpu.SMEM)] + [pl.BlockSpec(memory_space=pltpu.HBM)] * 2,
        out_specs=[vmem] * 7,
        scratch_shapes=[pltpu.SemaphoreType.DMA((2,))],
        compiler_params=pltpu.CompilerParams(vmem_limit_bytes=16 * 2**20),
        name="pack",
    )(rank, fields, density)


def join_kernel(quantities, rank, moving, still, new_fields, new_density):
    slots, share = still.shape[0], still.shape[1]
    for slot in range(slots):
        for item in range(share):
            column, row = pair_of(lax.bitwise_xor(rank[0], slot), item, share, quantities)
            if isinstance(row, int):
                new_fields[6 if row == 3 else row, column] = moving[slot, item]
                if row == 0:
                    new_density[column] = still[slot, item]
                else:
                    new_fields[2 + row, column] = still[slot, item]
            else:
                new_fields[jnp.where(row == 3, 6, row), column] = moving[slot, item]

                @pl.when(row == 0)
                def _():
                    new_density[column] = still[slot, item]

                @pl.when(row > 0)
                def _():
                    new_fields[2 + row, column] = still[slot, item]


def join(rank, moving, still, columns):
    _, _, cells, depth = still.shape
    f32 = jnp.float32
    vmem = pl.BlockSpec(memory_space=pltpu.VMEM)
    return pl.pallas_call(
        functools.partial(join_kernel, 4),
        out_shape=(
            jax.ShapeDtypeStruct((7, columns, cells, depth), f32),
            jax.ShapeDtypeStruct((columns, cells, depth), f32),
        ),
        in_specs=[pl.BlockSpec(memory_space=pltpu.SMEM), vmem, vmem],
        out_specs=[vmem] * 2,
        compiler_params=pltpu.CompilerParams(vmem_limit_bytes=16 * 2**20),
        name="join",
    )(rank, moving, still)


def digit_radix(span):
    return 4 if span % 4 == 0 else 2


def send_step(cut, step):
    radix, stride = cut.shape[1], cut.shape[2]
    count = cut.shape[0] * radix * stride
    pairs = [(rank, rank ^ (step * stride)) for rank in range(count)]
    return lax.ppermute(cut[:, step], "az", pairs)


def swap(slots, span=None):
    span = slots.shape[0] if span is None else span
    while span > 1:
        radix = digit_radix(span)
        span //= radix
        cut = slots.reshape(-1, radix, span, *slots.shape[1:])
        parts = [cut[:, 0]] + [send_step(cut, step) for step in range(1, radix)]
        slots = jnp.stack(parts, axis=1).reshape(slots.shape)
    return slots


def stress_kernel(
    info,
    fields,
    density,
    head,
    tail,
    before,
    after,
    straight_below,
    straight_above,
    whole,
    next_one,
    out,
    joined,
    vel,
    mass,
    px,
    py,
    pzz,
    heat,
):
    columns, cells, depth = density.shape
    share = out.shape[1]
    first, last, remainder = info[0], info[1], info[2]
    end = TOP + cells

    def place(far, near, ghost, start, jump):
        for component in range(3):
            added = jump if component == 1 else 0.0
            vel[component, near, TOP - 1 : end + 1] = (
                joined[component, pl.ds(start, cells + 2)] + added
            )
            vel[component, far, TOP:end] = joined[7 + component, pl.ds(start + 1, cells)] + added
        for row in range(4):
            mass[row, ghost] = joined[3 + row, pl.ds(start + 1, cells)]

    def lay(one, two):
        for row in range(PACKED):
            joined[row, 1 : cells + 1] = one[row]
            if two is not None:
                joined[row, cells + 1 : 2 * cells + 1] = two[row]
        final = one if two is None else two
        spot = (1 if two is None else 2) * cells + 1
        for component in range(3):
            joined[component, 0:1] = one[PACKED, 2 * component : 2 * component + 1]
            joined[component, spot : spot + 1] = final[PACKED, 2 * component + 1 : 2 * component + 2]

    below = (0, 1, 0)
    above = (columns + 3, columns + 2, columns + 1)

    @pl.when(first == 1)
    def _():
        lay(next_one, whole)
        place(*below, cells - remainder, shear_jump)

    @pl.when(first == 0)
    def _():
        lay(straight_below, None)
        place(*below, 0, 0.0)

    @pl.when(last == 1)
    def _():
        lay(whole, next_one)
        place(*above, remainder, -shear_jump)

    @pl.when(last == 0)
    def _():
        lay(straight_above, None)
        place(*above, 0, 0.0)

    vel[:, 2 : columns + 2, TOP:end] = fields[0:3]
    mass[0, 1 : columns + 1] = density[...]
    mass[1:4, 1 : columns + 1] = fields[3:6]
    for component in range(3):
        for column in range(columns):
            vel[component, 2 + column, TOP - 1 : TOP] = before[component, column : column + 1]
            vel[component, 2 + column, end : end + 1] = after[component, column : column + 1]

    for layer, spot, high, low in (
        (before, TOP - 1, (head, 0), (before, 7)),
        (after, end, (after, 7), (tail, 0)),
    ):
        grad_x, grad_y, grad_z = [], [], []
        for component in range(3):
            row = layer[component]
            left = jnp.concatenate(
                [vel[component, 1, spot : spot + 1], layer[component, 0 : columns - 1]], axis=0
            )
            right = jnp.concatenate(
                [layer[component, 1:columns], vel[component, columns + 2, spot : spot + 1]], axis=0
            )
            grad_x.append((right - left) * 0.5)
            grad_y.append((high[0][high[1] + component] - low[0][low[1] + component]) * 0.5)
            grad_z.append(vertical_slope(row))
        magnet = [layer[4], layer[5], layer[6]]
        gap, _, unit = stress(layer[3], magnet, grad_x, grad_y, grad_z)
        edge = gap * unit[1]
        parts = (edge * unit[0], edge * unit[1] - gap * (1.0 / 3.0), edge * unit[2])
        for row in range(3):
            for column in range(columns):
                py[row, 1 + column, spot : spot + 1] = parts[row][column : column + 1]

    def tensor_column(ghost, carry):
        here = ghost + 1
        grad_x = [
            (vel[i, here + 1, TOP:end] - vel[i, here - 1, TOP:end]) * 0.5 for i in range(3)
        ]
        grad_y = [
            (vel[i, here, TOP + 1 : end + 1] - vel[i, here, TOP - 1 : end - 1]) * 0.5
            for i in range(3)
        ]
        grad_z = [vertical_slope(vel[i, here, TOP:end]) for i in range(3)]
        magnet = [mass[1, ghost], mass[2, ghost], mass[3, ghost]]
        gap, anisotropy, unit = stress(mass[0, ghost], magnet, grad_x, grad_y, grad_z)
        third = gap * (1.0 / 3.0)
        along_x, along_y = gap * unit[0], gap * unit[1]
        px[0, ghost] = along_x * unit[0] - third
        cross = along_x * unit[1]
        px[1, ghost] = cross
        px[2, ghost] = along_x * unit[2]
        py[0, ghost, TOP:end] = cross
        py[1, ghost, TOP:end] = along_y * unit[1] - third
        py[2, ghost, TOP:end] = along_y * unit[2]
        pzz[ghost] = gap * unit[2] * unit[2] - third
        heat[ghost] = gap * anisotropy
        return carry

    lax.fori_loop(0, columns + 2, tensor_column, 0, unroll=3)

    def update_column(column, carry):
        ghost = column + 1
        inverse = 1.0 / mass[0, ghost]

        def slope(axis):
            return (px[axis, ghost + 1] - px[axis, ghost - 1]) * 0.5 + (
                py[axis, ghost, TOP + 1 : end + 1] - py[axis, ghost, TOP - 1 : end - 1]
            ) * 0.5

        vertical = (px[2, ghost], py[2, ghost, TOP:end], pzz[ghost])
        for axis in range(4):
            flat = column * 4 + axis
            slot = lax.bitwise_xor(info[3], flat // share)
            if axis < 3:
                force = slope(axis) + vertical_slope(vertical[axis])
                out[slot, flat % share] = fields[axis, column] + force * inverse
            else:
                out[slot, flat % share] = fields[6, column] + heat[ghost]
        return carry

    lax.fori_loop(0, columns, update_column, 0, unroll=4)


def updated_columns(info, fields, density, *layers):
    columns, cells, depth = density.shape
    tall = cells + 2 * TOP
    slots = lax.axis_size("az")
    smem = pl.BlockSpec(memory_space=pltpu.SMEM)
    vmem = pl.BlockSpec(memory_space=pltpu.VMEM)
    f32 = jnp.float32
    return pl.pallas_call(
        stress_kernel,
        out_shape=jax.ShapeDtypeStruct((slots, 4 * columns // slots, cells, depth), f32),
        in_specs=[smem] + [vmem] * 10,
        out_specs=vmem,
        scratch_shapes=[
            pltpu.VMEM((PACKED, 2 * cells + TOP, depth), f32),
            pltpu.VMEM((3, columns + 4, tall, depth), f32),
            pltpu.VMEM((4, columns + 2, cells, depth), f32),
            pltpu.VMEM((3, columns + 2, cells, depth), f32),
            pltpu.VMEM((3, columns + 2, tall, depth), f32),
            pltpu.VMEM((columns + 2, cells, depth), f32),
            pltpu.VMEM((columns + 2, cells, depth), f32),
        ],
        compiler_params=pltpu.CompilerParams(vmem_limit_bytes=24 * 2**20),
        name="stress_update",
    )(info, fields, density, *layers)


def move_kernel(quantities, rank, shift, frac, gathered, out, twice):
    slots, share, cells, depth = gathered.shape
    total = slots * cells
    me = rank[0]
    for item in range(share):
        column, _ = pair_of(me, item, share, quantities)
        fraction = frac[column].astype(jnp.float32) * (1.0 / FRAC_DEN)
        bend = fraction * (1.0 - fraction) * 0.25
        start = TOP + lax.rem(total - shift[column], total)

        def lay(slot, carry):
            rows = gathered[slot, item]
            spot = pl.multiple_of(TOP + lax.bitwise_xor(me, slot) * cells, TOP)
            twice[item, pl.ds(spot, cells)] = rows
            twice[item, pl.ds(pl.multiple_of(spot + total, TOP), cells)] = rows
            return carry

        lax.fori_loop(0, slots, lay, 0, unroll=4)
        twice[item, 0:TOP] = twice[item, total : total + TOP]

        def blend(slot, carry):
            spot = start + lax.bitwise_xor(me, slot) * cells
            back_two = twice[item, pl.ds(spot - 2, cells)]
            back_one = twice[item, pl.ds(spot - 1, cells)]
            centre = twice[item, pl.ds(spot, cells)]
            ahead = twice[item, pl.ds(spot + 1, cells)]
            out[slot, item] = (
                centre
                + fraction * (back_one - centre)
                + bend * ((centre - back_two) - (ahead - back_one))
            )
            return carry

        lax.fori_loop(0, slots, blend, 0, unroll=4)


def move_columns(gathered, quantities, rank, shift_int, frac_num):
    azimuths, share, cells, depth = gathered.shape
    smem = pl.BlockSpec(memory_space=pltpu.SMEM)
    vmem = pl.BlockSpec(memory_space=pltpu.VMEM)
    return pl.pallas_call(
        functools.partial(move_kernel, quantities),
        out_shape=jax.ShapeDtypeStruct(gathered.shape, jnp.float32),
        in_specs=[smem, smem, smem, vmem],
        out_specs=vmem,
        scratch_shapes=[pltpu.VMEM((share, 2 * azimuths * cells + TOP, depth), jnp.float32)],
        compiler_params=pltpu.CompilerParams(vmem_limit_bytes=16 * 2**20),
        name="move",
    )(rank, shift_int, frac_num, gathered)


def azimuthal_layers(head, tail):
    azimuths = lax.axis_size("az")
    even = lax.axis_index("az") % 2 == 0
    inner = [(az, az ^ 1) for az in range(azimuths)]
    outer = [(az, (az - 1 if az % 2 == 0 else az + 1) % azimuths) for az in range(azimuths)]
    far = lax.ppermute(jnp.where(even, head, tail), "az", outer)
    near = lax.ppermute(jnp.where(even, tail, head), "az", inner)
    return jnp.where(even, far, near), jnp.where(even, near, far)


def rims(blocks, low, high, before, after):
    radials = lax.axis_size("rad")
    azimuths = lax.axis_size("az")
    rad = lax.axis_index("rad")
    last = radials - 1

    def flat(rad, az):
        return rad * azimuths + az % azimuths

    def wrap(data, steps):
        pairs = [(flat(last, az), flat(0, az + steps)) for az in range(azimuths)]
        pairs += [(flat(0, az), flat(last, az - steps)) for az in range(azimuths)]
        return lax.ppermute(data, ("rad", "az"), pairs)

    def with_ends(main, column):
        ends = jnp.stack([before[0:3, column], after[0:3, column]], axis=1)
        ends = ends.reshape(1, 6, main.shape[-1])
        ends = jnp.pad(ends, ((0, 0), (0, main.shape[1] - 6), (0, 0)))
        return jnp.concatenate([main, ends], axis=0)

    low, high = with_ends(low, 0), with_ends(high, -1)
    edge = jnp.where(rad == 0, low, high)
    if radials == 2:
        other = jnp.where(rad == 0, high, low)
        below = above = lax.ppermute(other, "rad", [(0, 1), (1, 0)])
    else:
        below = lax.ppermute(high, "rad", [(i, i + 1) for i in range(last)])
        above = lax.ppermute(low, "rad", [(i + 1, i) for i in range(last)])

    def branch(steps):
        return lambda data: (wrap(data, steps), wrap(data, steps + 1))

    whole, next_one = lax.switch(blocks, [branch(steps) for steps in range(azimuths)], edge)
    return below, above, whole, next_one


def local(fields, density, shift_int, frac_num, boundary_shift):
    columns, cells, _ = density.shape
    radials = lax.axis_size("rad")
    rad = lax.axis_index("rad")
    shear_cells = boundary_shift[0]
    az = lax.axis_index("az")
    rank = az.reshape(1)
    head, tail, low, high, still, fields, density = pack(rank, fields, density)
    before, after = azimuthal_layers(head, tail)
    count = still.shape[0]
    radix = digit_radix(count)
    span = count // radix
    cut = still.reshape(1, radix, span, *still.shape[1:])
    nearest = send_step(cut, 1)
    before, after, cut = lax.optimization_barrier((before, after, cut))
    parts = [cut[:, 0], nearest] + [send_step(cut, step) for step in range(2, radix)]
    layers = rims(shear_cells // cells, low, high, before, after)
    parts, layers = lax.optimization_barrier((parts, layers))
    still = swap(jnp.stack(parts, axis=1).reshape(still.shape), span)
    info = jnp.stack(
        [
            (rad == 0).astype(jnp.int32),
            (rad == radials - 1).astype(jnp.int32),
            shear_cells % cells,
            az,
        ]
    )
    moving = updated_columns(info, fields, density, head, tail, before, after, *layers)
    moving, still = lax.optimization_barrier((moving, still))
    moving = swap(moving)
    still = swap(move_columns(still, 4, rank, shift_int, frac_num))
    moving = swap(move_columns(moving, 4, rank, shift_int, frac_num))
    return join(rank, moving, still, columns)


def solution(mesh):
    in_specs = (P(None, "rad", "az", None), P("rad", "az", None), P("rad"), P("rad"), P())
    out_specs = (P(None, "rad", "az", None), P("rad", "az", None))
    return jax.shard_map(local, mesh=mesh, in_specs=in_specs, out_specs=out_specs, check_vma=False)
```

```python
import functools

import jax
import jax.numpy as jnp
from jax import lax
from jax.experimental import pallas as pl
from jax.experimental.pallas import tpu as pltpu
from jax.sharding import PartitionSpec as P

FRAC_DEN = 64

shear_jump = 1.5
visc_step = 0.05
field_floor = 0.25

PACKED = 10
TOP = 8


def up_and_down(values):
    lane = lax.broadcasted_iota(jnp.int32, values.shape, values.ndim - 1)
    depth = values.shape[-1]
    up = pltpu.roll(values, depth - 1, values.ndim - 1)
    down = pltpu.roll(values, 1, values.ndim - 1)
    return jnp.where(lane == depth - 1, values, up), jnp.where(lane == 0, values, down)


def vertical_slope(values):
    up, down = up_and_down(values)
    return (up - down) * 0.5


def stress(density, magnet, grad_x, grad_y, grad_z):
    square = magnet[0] * magnet[0] + magnet[1] * magnet[1] + magnet[2] * magnet[2]
    inverse = lax.rsqrt(jnp.maximum(square, field_floor))
    unit = [component * inverse for component in magnet]
    slopes = (grad_x, grad_y, grad_z)
    aligned = None
    for direction in range(3):
        along = (
            unit[0] * slopes[direction][0]
            + unit[1] * slopes[direction][1]
            + unit[2] * slopes[direction][2]
        )
        term = unit[direction] * along
        aligned = term if aligned is None else aligned + term
    anisotropy = aligned - (grad_x[0] + grad_y[1] + grad_z[2]) * (1.0 / 3.0)
    gap = (3.0 * visc_step) * density * anisotropy
    return gap, anisotropy, unit


def pack_kernel(
    quantities, rank, fields_in, density_in, head, tail, low, high, still, fields, density, sems
):
    columns, cells, depth = density.shape
    slots, share = still.shape[0], still.shape[1]
    copies = [
        pltpu.make_async_copy(density_in, density, sems.at[0]),
        pltpu.make_async_copy(fields_in.at[0:6], fields, sems.at[1]),
    ]
    for copy in copies:
        copy.start()
    for copy in copies:
        copy.wait()

    def source(row):
        if row == 3:
            return density
        return fields.at[row if row < 3 else row - 1 if row < 7 else row - 7]

    for row in range(PACKED):
        second = 1 if row >= 7 else 0
        origin = source(row)
        low[row] = origin[second]
        high[row] = origin[columns - 1 - second]
        for column in range(columns):
            head[row, column : column + 1] = origin[column, second : second + 1]
            tail[row, column : column + 1] = origin[column, cells - 1 - second : cells - second]
    for slot in range(slots):
        for item in range(share):
            column, row = pair_of(lax.bitwise_xor(rank[0], slot), item, share, quantities)
            if isinstance(row, int):
                still[slot, item] = density[column] if row == 0 else fields[2 + row, column]
            else:
                still[slot, item] = jnp.where(
                    row == 0, density[column], fields[jnp.maximum(row, 1) + 2, column]
                )


def pair_of(rank, item, share, quantities):
    if share % quantities == 0:
        return rank * (share // quantities) + item // quantities, item % quantities
    flat = rank * share + item
    return flat // quantities, flat % quantities


def pack(rank, fields, density):
    columns, cells, depth = density.shape
    slots = lax.axis_size("az")
    share = 4 * columns // slots
    f32 = jnp.float32
    layer = jax.ShapeDtypeStruct((PACKED, columns, depth), f32)
    rim = jax.ShapeDtypeStruct((PACKED, cells, depth), f32)
    vmem = pl.BlockSpec(memory_space=pltpu.VMEM)
    return pl.pallas_call(
        functools.partial(pack_kernel, 4),
        out_shape=(
            layer,
            layer,
            rim,
            rim,
            jax.ShapeDtypeStruct((slots, share, cells, depth), f32),
        ),
        in_specs=[pl.BlockSpec(memory_space=pltpu.SMEM)] + [pl.BlockSpec(memory_space=pltpu.HBM)] * 2,
        out_specs=[vmem] * 5,
        scratch_shapes=[
            pltpu.VMEM((6, columns, cells, depth), f32),
            pltpu.VMEM((columns, cells, depth), f32),
            pltpu.SemaphoreType.DMA((2,)),
        ],
        compiler_params=pltpu.CompilerParams(vmem_limit_bytes=16 * 2**20),
        name="pack",
    )(rank, fields, density)


def join_kernel(quantities, returned, new_fields, new_density):
    slots, share = returned.shape[0], returned.shape[1] // 2
    for slot in range(slots):
        for item in range(share):
            column, row = pair_of(slot, item, share, quantities)
            new_fields[6 if row == 3 else row, column] = returned[slot, item]
            if row == 0:
                new_density[column] = returned[slot, share + item]
            else:
                new_fields[2 + row, column] = returned[slot, share + item]


def join(returned, columns):
    _, _, cells, depth = returned.shape
    f32 = jnp.float32
    vmem = pl.BlockSpec(memory_space=pltpu.VMEM)
    return pl.pallas_call(
        functools.partial(join_kernel, 4),
        out_shape=(
            jax.ShapeDtypeStruct((7, columns, cells, depth), f32),
            jax.ShapeDtypeStruct((columns, cells, depth), f32),
        ),
        in_specs=[vmem],
        out_specs=[vmem] * 2,
        compiler_params=pltpu.CompilerParams(vmem_limit_bytes=16 * 2**20),
        name="join",
    )(returned)


def digit_radix(span):
    return 4 if span % 4 == 0 else 2


def send_step(cut, step):
    radix, stride = cut.shape[1], cut.shape[2]
    count = cut.shape[0] * radix * stride
    pairs = [(rank, rank ^ (step * stride)) for rank in range(count)]
    return lax.ppermute(cut[:, step], "az", pairs)


def swap(slots, span=None):
    span = slots.shape[0] if span is None else span
    while span > 1:
        radix = digit_radix(span)
        span //= radix
        cut = slots.reshape(-1, radix, span, *slots.shape[1:])
        parts = [cut[:, 0]] + [send_step(cut, step) for step in range(1, radix)]
        slots = jnp.stack(parts, axis=1).reshape(slots.shape)
    return slots


def stress_kernel(
    info,
    fields,
    density,
    head,
    tail,
    before,
    after,
    straight_below,
    straight_above,
    whole,
    next_one,
    out,
    joined,
    vel,
    mass,
    px,
    py,
    pzz,
    heat,
):
    columns, cells, depth = density.shape
    share = out.shape[1]
    first, last, remainder = info[0], info[1], info[2]
    end = TOP + cells

    def place(far, near, ghost, start, jump):
        for component in range(3):
            added = jump if component == 1 else 0.0
            vel[component, near, TOP - 1 : end + 1] = (
                joined[component, pl.ds(start, cells + 2)] + added
            )
            vel[component, far, TOP:end] = joined[7 + component, pl.ds(start + 1, cells)] + added
        for row in range(4):
            mass[row, ghost] = joined[3 + row, pl.ds(start + 1, cells)]

    def lay(one, two):
        for row in range(PACKED):
            joined[row, 1 : cells + 1] = one[row]
            if two is not None:
                joined[row, cells + 1 : 2 * cells + 1] = two[row]
        final = one if two is None else two
        spot = (1 if two is None else 2) * cells + 1
        for component in range(3):
            joined[component, 0:1] = one[PACKED, 2 * component : 2 * component + 1]
            joined[component, spot : spot + 1] = final[PACKED, 2 * component + 1 : 2 * component + 2]

    below = (0, 1, 0)
    above = (columns + 3, columns + 2, columns + 1)

    @pl.when(first == 1)
    def _():
        lay(next_one, whole)
        place(*below, cells - remainder, shear_jump)

    @pl.when(first == 0)
    def _():
        lay(straight_below, None)
        place(*below, 0, 0.0)

    @pl.when(last == 1)
    def _():
        lay(whole, next_one)
        place(*above, remainder, -shear_jump)

    @pl.when(last == 0)
    def _():
        lay(straight_above, None)
        place(*above, 0, 0.0)

    vel[:, 2 : columns + 2, TOP:end] = fields[0:3]
    mass[0, 1 : columns + 1] = density[...]
    mass[1:4, 1 : columns + 1] = fields[3:6]
    for component in range(3):
        for column in range(columns):
            vel[component, 2 + column, TOP - 1 : TOP] = before[component, column : column + 1]
            vel[component, 2 + column, end : end + 1] = after[component, column : column + 1]

    for layer, spot, high, low in (
        (before, TOP - 1, (head, 0), (before, 7)),
        (after, end, (after, 7), (tail, 0)),
    ):
        grad_x, grad_y, grad_z = [], [], []
        for component in range(3):
            row = layer[component]
            left = jnp.concatenate(
                [vel[component, 1, spot : spot + 1], layer[component, 0 : columns - 1]], axis=0
            )
            right = jnp.concatenate(
                [layer[component, 1:columns], vel[component, columns + 2, spot : spot + 1]], axis=0
            )
            grad_x.append((right - left) * 0.5)
            grad_y.append((high[0][high[1] + component] - low[0][low[1] + component]) * 0.5)
            grad_z.append(vertical_slope(row))
        magnet = [layer[4], layer[5], layer[6]]
        gap, _, unit = stress(layer[3], magnet, grad_x, grad_y, grad_z)
        edge = gap * unit[1]
        parts = (edge * unit[0], edge * unit[1] - gap * (1.0 / 3.0), edge * unit[2])
        for row in range(3):
            for column in range(columns):
                py[row, 1 + column, spot : spot + 1] = parts[row][column : column + 1]

    def tensor_column(ghost, carry):
        here = ghost + 1
        grad_x = [
            (vel[i, here + 1, TOP:end] - vel[i, here - 1, TOP:end]) * 0.5 for i in range(3)
        ]
        grad_y = [
            (vel[i, here, TOP + 1 : end + 1] - vel[i, here, TOP - 1 : end - 1]) * 0.5
            for i in range(3)
        ]
        grad_z = [vertical_slope(vel[i, here, TOP:end]) for i in range(3)]
        magnet = [mass[1, ghost], mass[2, ghost], mass[3, ghost]]
        gap, anisotropy, unit = stress(mass[0, ghost], magnet, grad_x, grad_y, grad_z)
        third = gap * (1.0 / 3.0)
        along_x, along_y = gap * unit[0], gap * unit[1]
        px[0, ghost] = along_x * unit[0] - third
        cross = along_x * unit[1]
        px[1, ghost] = cross
        px[2, ghost] = along_x * unit[2]
        py[0, ghost, TOP:end] = cross
        py[1, ghost, TOP:end] = along_y * unit[1] - third
        py[2, ghost, TOP:end] = along_y * unit[2]
        pzz[ghost] = gap * unit[2] * unit[2] - third
        heat[ghost] = gap * anisotropy
        return carry

    lax.fori_loop(0, columns + 2, tensor_column, 0, unroll=3)

    def update_column(column, carry):
        ghost = column + 1
        inverse = 1.0 / mass[0, ghost]

        def slope(axis):
            return (px[axis, ghost + 1] - px[axis, ghost - 1]) * 0.5 + (
                py[axis, ghost, TOP + 1 : end + 1] - py[axis, ghost, TOP - 1 : end - 1]
            ) * 0.5

        vertical = (px[2, ghost], py[2, ghost, TOP:end], pzz[ghost])
        for axis in range(4):
            flat = column * 4 + axis
            slot = flat // share
            if axis < 3:
                force = slope(axis) + vertical_slope(vertical[axis])
                out[slot, flat % share] = fields[axis, column] + force * inverse
            else:
                out[slot, flat % share] = fields[6, column] + heat[ghost]
        return carry

    lax.fori_loop(0, columns, update_column, 0, unroll=4)


def updated_columns(info, fields, density, *layers):
    columns, cells, depth = density.shape
    tall = cells + 2 * TOP
    slots = lax.axis_size("az")
    smem = pl.BlockSpec(memory_space=pltpu.SMEM)
    vmem = pl.BlockSpec(memory_space=pltpu.VMEM)
    f32 = jnp.float32
    return pl.pallas_call(
        stress_kernel,
        out_shape=jax.ShapeDtypeStruct((slots, 4 * columns // slots, cells, depth), f32),
        in_specs=[smem] + [vmem] * 10,
        out_specs=vmem,
        scratch_shapes=[
            pltpu.VMEM((PACKED, 2 * cells + TOP, depth), f32),
            pltpu.VMEM((3, columns + 4, tall, depth), f32),
            pltpu.VMEM((4, columns + 2, cells, depth), f32),
            pltpu.VMEM((3, columns + 2, cells, depth), f32),
            pltpu.VMEM((3, columns + 2, tall, depth), f32),
            pltpu.VMEM((columns + 2, cells, depth), f32),
            pltpu.VMEM((columns + 2, cells, depth), f32),
        ],
        compiler_params=pltpu.CompilerParams(vmem_limit_bytes=24 * 2**20),
        name="stress_update",
    )(info, fields, density, *layers)


def move_kernel(quantities, mixed, rank, shift, frac, gathered, out, twice):
    slots, share, cells, depth = gathered.shape
    total = slots * cells
    me = rank[0]
    for item in range(share):
        column, _ = pair_of(me, item, share, quantities)
        fraction = frac[column].astype(jnp.float32) * (1.0 / FRAC_DEN)
        bend = fraction * (1.0 - fraction) * 0.25
        start = TOP + lax.rem(total - shift[column], total)

        def lay(slot, carry):
            rows = gathered[slot, item]
            block = lax.bitwise_xor(me, slot) if mixed else slot
            spot = pl.multiple_of(TOP + block * cells, TOP)
            twice[item, pl.ds(spot, cells)] = rows
            twice[item, pl.ds(pl.multiple_of(spot + total, TOP), cells)] = rows
            return carry

        lax.fori_loop(0, slots, lay, 0, unroll=4)
        twice[item, 0:TOP] = twice[item, total : total + TOP]

        def blend(slot, carry):
            spot = start + slot * cells
            back_two = twice[item, pl.ds(spot - 2, cells)]
            back_one = twice[item, pl.ds(spot - 1, cells)]
            centre = twice[item, pl.ds(spot, cells)]
            ahead = twice[item, pl.ds(spot + 1, cells)]
            out[slot, item] = (
                centre
                + fraction * (back_one - centre)
                + bend * ((centre - back_two) - (ahead - back_one))
            )
            return carry

        lax.fori_loop(0, slots, blend, 0, unroll=4)


def move_columns(gathered, quantities, mixed, rank, shift_int, frac_num):
    azimuths, share, cells, depth = gathered.shape
    smem = pl.BlockSpec(memory_space=pltpu.SMEM)
    vmem = pl.BlockSpec(memory_space=pltpu.VMEM)
    return pl.pallas_call(
        functools.partial(move_kernel, quantities, mixed),
        out_shape=jax.ShapeDtypeStruct(gathered.shape, jnp.float32),
        in_specs=[smem, smem, smem, vmem],
        out_specs=vmem,
        scratch_shapes=[pltpu.VMEM((share, 2 * azimuths * cells + TOP, depth), jnp.float32)],
        compiler_params=pltpu.CompilerParams(vmem_limit_bytes=16 * 2**20),
        name="move",
    )(rank, shift_int, frac_num, gathered)


def azimuthal_layers(head, tail):
    azimuths = lax.axis_size("az")
    even = lax.axis_index("az") % 2 == 0
    inner = [(az, az ^ 1) for az in range(azimuths)]
    outer = [(az, (az - 1 if az % 2 == 0 else az + 1) % azimuths) for az in range(azimuths)]
    far = lax.ppermute(jnp.where(even, head, tail), "az", outer)
    near = lax.ppermute(jnp.where(even, tail, head), "az", inner)
    return jnp.where(even, far, near), jnp.where(even, near, far)


def rims(blocks, low, high, before, after):
    radials = lax.axis_size("rad")
    azimuths = lax.axis_size("az")
    rad = lax.axis_index("rad")
    last = radials - 1

    def flat(rad, az):
        return rad * azimuths + az % azimuths

    def wrap(data, steps):
        pairs = [(flat(last, az), flat(0, az + steps)) for az in range(azimuths)]
        pairs += [(flat(0, az), flat(last, az - steps)) for az in range(azimuths)]
        return lax.ppermute(data, ("rad", "az"), pairs)

    def with_ends(main, column):
        ends = jnp.stack([before[0:3, column], after[0:3, column]], axis=1)
        ends = ends.reshape(1, 6, main.shape[-1])
        ends = jnp.pad(ends, ((0, 0), (0, main.shape[1] - 6), (0, 0)))
        return jnp.concatenate([main, ends], axis=0)

    low, high = with_ends(low, 0), with_ends(high, -1)
    edge = jnp.where(rad == 0, low, high)
    if radials == 2:
        other = jnp.where(rad == 0, high, low)
        below = above = lax.ppermute(other, "rad", [(0, 1), (1, 0)])
    else:
        below = lax.ppermute(high, "rad", [(i, i + 1) for i in range(last)])
        above = lax.ppermute(low, "rad", [(i + 1, i) for i in range(last)])

    def branch(steps):
        return lambda data: (wrap(data, steps), wrap(data, steps + 1))

    whole, next_one = lax.switch(blocks, [branch(steps) for steps in range(azimuths)], edge)
    return below, above, whole, next_one


def local(fields, density, shift_int, frac_num, boundary_shift):
    columns, cells, _ = density.shape
    radials = lax.axis_size("rad")
    rad = lax.axis_index("rad")
    shear_cells = boundary_shift[0]
    az = lax.axis_index("az")
    rank = az.reshape(1)
    head, tail, low, high, still = pack(rank, fields, density)
    before, after = azimuthal_layers(head, tail)
    count = still.shape[0]
    radix = digit_radix(count)
    span = count // radix
    cut = still.reshape(1, radix, span, *still.shape[1:])
    nearest = send_step(cut, 1)
    before, after, nearest, cut = lax.optimization_barrier((before, after, nearest, cut))
    parts = [cut[:, 0], nearest] + [send_step(cut, step) for step in range(2, radix)]
    layers = rims(shear_cells // cells, low, high, before, after)
    parts, layers = lax.optimization_barrier((parts, layers))
    still = swap(jnp.stack(parts, axis=1).reshape(still.shape), span)
    info = jnp.stack(
        [
            (rad == 0).astype(jnp.int32),
            (rad == radials - 1).astype(jnp.int32),
            shear_cells % cells,
            az,
        ]
    )
    moving = updated_columns(info, fields, density, head, tail, before, after, *layers)
    moving = lax.all_to_all(moving, "az", 0, 0, tiled=True)
    still = move_columns(still, 4, True, rank, shift_int, frac_num)
    moving = move_columns(moving, 4, False, rank, shift_int, frac_num)
    both = jnp.concatenate([moving, still], axis=1)
    return join(lax.all_to_all(both, "az", 0, 0, tiled=True), columns)


def solution(mesh):
    in_specs = (P(None, "rad", "az", None), P("rad", "az", None), P("rad"), P("rad"), P())
    out_specs = (P(None, "rad", "az", None), P("rad", "az", None))
    return jax.shard_map(local, mesh=mesh, in_specs=in_specs, out_specs=out_specs, check_vma=False)
```

```python
import functools

import jax
import jax.numpy as jnp
from jax import lax
from jax.experimental import pallas as pl
from jax.experimental.pallas import tpu as pltpu
from jax.sharding import PartitionSpec as P

FRAC_DEN = 64

shear_jump = 1.5
visc_step = 0.05
field_floor = 0.25

PACKED = 10
TOP = 8


def up_and_down(values):
    lane = lax.broadcasted_iota(jnp.int32, values.shape, values.ndim - 1)
    depth = values.shape[-1]
    up = pltpu.roll(values, depth - 1, values.ndim - 1)
    down = pltpu.roll(values, 1, values.ndim - 1)
    return jnp.where(lane == depth - 1, values, up), jnp.where(lane == 0, values, down)


def vertical_slope(values):
    up, down = up_and_down(values)
    return (up - down) * 0.5


def stress(density, magnet, grad_x, grad_y, grad_z):
    square = magnet[0] * magnet[0] + magnet[1] * magnet[1] + magnet[2] * magnet[2]
    inverse = lax.rsqrt(jnp.maximum(square, field_floor))
    unit = [component * inverse for component in magnet]
    slopes = (grad_x, grad_y, grad_z)
    aligned = None
    for direction in range(3):
        along = (
            unit[0] * slopes[direction][0]
            + unit[1] * slopes[direction][1]
            + unit[2] * slopes[direction][2]
        )
        term = unit[direction] * along
        aligned = term if aligned is None else aligned + term
    anisotropy = aligned - (grad_x[0] + grad_y[1] + grad_z[2]) * (1.0 / 3.0)
    gap = (3.0 * visc_step) * density * anisotropy
    return gap, anisotropy, unit


def pack_kernel(
    quantities, rank, fields_in, density_in, head, tail, low, high, still, fields, density, sems
):
    columns, cells, depth = density.shape
    slots, share = still.shape[0], still.shape[1]
    copies = [
        pltpu.make_async_copy(density_in, density, sems.at[0]),
        pltpu.make_async_copy(fields_in, fields, sems.at[1]),
    ]
    for copy in copies:
        copy.start()
    for copy in copies:
        copy.wait()

    def source(row):
        if row == 3:
            return density
        return fields.at[row if row < 3 else row - 1 if row < 7 else row - 7]

    for row in range(PACKED):
        second = 1 if row >= 7 else 0
        origin = source(row)
        low[row] = origin[second]
        high[row] = origin[columns - 1 - second]
        for column in range(columns):
            head[row, column : column + 1] = origin[column, second : second + 1]
            tail[row, column : column + 1] = origin[column, cells - 1 - second : cells - second]
    for slot in range(slots):
        for item in range(share):
            column, row = pair_of(lax.bitwise_xor(rank[0], slot), item, share, quantities)
            if isinstance(row, int):
                still[slot, item] = density[column] if row == 0 else fields[2 + row, column]
            else:
                still[slot, item] = jnp.where(
                    row == 0, density[column], fields[jnp.maximum(row, 1) + 2, column]
                )


def pair_of(rank, item, share, quantities):
    if share % quantities == 0:
        return rank * (share // quantities) + item // quantities, item % quantities
    flat = rank * share + item
    return flat // quantities, flat % quantities


def pack(rank, fields, density):
    columns, cells, depth = density.shape
    slots = lax.axis_size("az")
    share = 4 * columns // slots
    f32 = jnp.float32
    layer = jax.ShapeDtypeStruct((PACKED, columns, depth), f32)
    rim = jax.ShapeDtypeStruct((PACKED, cells, depth), f32)
    vmem = pl.BlockSpec(memory_space=pltpu.VMEM)
    return pl.pallas_call(
        functools.partial(pack_kernel, 4),
        out_shape=(
            layer,
            layer,
            rim,
            rim,
            jax.ShapeDtypeStruct((slots, share, cells, depth), f32),
            jax.ShapeDtypeStruct(fields.shape, f32),
            jax.ShapeDtypeStruct(density.shape, f32),
        ),
        in_specs=[pl.BlockSpec(memory_space=pltpu.SMEM)] + [pl.BlockSpec(memory_space=pltpu.HBM)] * 2,
        out_specs=[vmem] * 7,
        scratch_shapes=[pltpu.SemaphoreType.DMA((2,))],
        compiler_params=pltpu.CompilerParams(vmem_limit_bytes=16 * 2**20),
        name="pack",
    )(rank, fields, density)


def join_kernel(quantities, rank, moving, still, new_fields, new_density):
    slots, share = still.shape[0], still.shape[1]
    for slot in range(slots):
        for item in range(share):
            column, row = pair_of(lax.bitwise_xor(rank[0], slot), item, share, quantities)
            if isinstance(row, int):
                new_fields[6 if row == 3 else row, column] = moving[slot, item]
                if row == 0:
                    new_density[column] = still[slot, item]
                else:
                    new_fields[2 + row, column] = still[slot, item]
            else:
                new_fields[jnp.where(row == 3, 6, row), column] = moving[slot, item]

                @pl.when(row == 0)
                def _():
                    new_density[column] = still[slot, item]

                @pl.when(row > 0)
                def _():
                    new_fields[2 + row, column] = still[slot, item]


def join(rank, moving, still, columns):
    _, _, cells, depth = still.shape
    f32 = jnp.float32
    vmem = pl.BlockSpec(memory_space=pltpu.VMEM)
    return pl.pallas_call(
        functools.partial(join_kernel, 4),
        out_shape=(
            jax.ShapeDtypeStruct((7, columns, cells, depth), f32),
            jax.ShapeDtypeStruct((columns, cells, depth), f32),
        ),
        in_specs=[pl.BlockSpec(memory_space=pltpu.SMEM), vmem, vmem],
        out_specs=[vmem] * 2,
        compiler_params=pltpu.CompilerParams(vmem_limit_bytes=16 * 2**20),
        name="join",
    )(rank, moving, still)


def digit_radix(span):
    return 4 if span % 4 == 0 else 2


def send_step(cut, step):
    radix, stride = cut.shape[1], cut.shape[2]
    count = cut.shape[0] * radix * stride
    pairs = [(rank, rank ^ (step * stride)) for rank in range(count)]
    return lax.ppermute(cut[:, step], "az", pairs)


def swap(slots, span=None):
    span = slots.shape[0] if span is None else span
    while span > 1:
        radix = digit_radix(span)
        span //= radix
        cut = slots.reshape(-1, radix, span, *slots.shape[1:])
        parts = [cut[:, 0]] + [send_step(cut, step) for step in range(1, radix)]
        slots = jnp.stack(parts, axis=1).reshape(slots.shape)
    return slots


def stress_kernel(
    info,
    fields,
    density,
    head,
    tail,
    before,
    after,
    straight_below,
    straight_above,
    whole,
    next_one,
    out,
    joined,
    vel,
    mass,
    px,
    py,
    pzz,
    heat,
):
    columns, cells, depth = density.shape
    share = out.shape[1]
    first, last, remainder = info[0], info[1], info[2]
    end = TOP + cells

    def place(far, near, ghost, start, jump):
        for component in range(3):
            added = jump if component == 1 else 0.0
            vel[component, near, TOP - 1 : end + 1] = (
                joined[component, pl.ds(start, cells + 2)] + added
            )
            vel[component, far, TOP:end] = joined[7 + component, pl.ds(start + 1, cells)] + added
        for row in range(4):
            mass[row, ghost] = joined[3 + row, pl.ds(start + 1, cells)]

    def lay(one, two):
        for row in range(PACKED):
            joined[row, 1 : cells + 1] = one[row]
            if two is not None:
                joined[row, cells + 1 : 2 * cells + 1] = two[row]
        final = one if two is None else two
        spot = (1 if two is None else 2) * cells + 1
        for component in range(3):
            joined[component, 0:1] = one[PACKED, 2 * component : 2 * component + 1]
            joined[component, spot : spot + 1] = final[PACKED, 2 * component + 1 : 2 * component + 2]

    below = (0, 1, 0)
    above = (columns + 3, columns + 2, columns + 1)

    @pl.when(first == 1)
    def _():
        lay(next_one, whole)
        place(*below, cells - remainder, shear_jump)

    @pl.when(first == 0)
    def _():
        lay(straight_below, None)
        place(*below, 0, 0.0)

    @pl.when(last == 1)
    def _():
        lay(whole, next_one)
        place(*above, remainder, -shear_jump)

    @pl.when(last == 0)
    def _():
        lay(straight_above, None)
        place(*above, 0, 0.0)

    vel[:, 2 : columns + 2, TOP:end] = fields[0:3]
    mass[0, 1 : columns + 1] = density[...]
    mass[1:4, 1 : columns + 1] = fields[3:6]
    for component in range(3):
        for column in range(columns):
            vel[component, 2 + column, TOP - 1 : TOP] = before[component, column : column + 1]
            vel[component, 2 + column, end : end + 1] = after[component, column : column + 1]

    for layer, spot, high, low in (
        (before, TOP - 1, (head, 0), (before, 7)),
        (after, end, (after, 7), (tail, 0)),
    ):
        grad_x, grad_y, grad_z = [], [], []
        for component in range(3):
            row = layer[component]
            left = jnp.concatenate(
                [vel[component, 1, spot : spot + 1], layer[component, 0 : columns - 1]], axis=0
            )
            right = jnp.concatenate(
                [layer[component, 1:columns], vel[component, columns + 2, spot : spot + 1]], axis=0
            )
            grad_x.append((right - left) * 0.5)
            grad_y.append((high[0][high[1] + component] - low[0][low[1] + component]) * 0.5)
            grad_z.append(vertical_slope(row))
        magnet = [layer[4], layer[5], layer[6]]
        gap, _, unit = stress(layer[3], magnet, grad_x, grad_y, grad_z)
        edge = gap * unit[1]
        parts = (edge * unit[0], edge * unit[1] - gap * (1.0 / 3.0), edge * unit[2])
        for row in range(3):
            for column in range(columns):
                py[row, 1 + column, spot : spot + 1] = parts[row][column : column + 1]

    def tensor_column(ghost, carry):
        here = ghost + 1
        grad_x = [
            (vel[i, here + 1, TOP:end] - vel[i, here - 1, TOP:end]) * 0.5 for i in range(3)
        ]
        grad_y = [
            (vel[i, here, TOP + 1 : end + 1] - vel[i, here, TOP - 1 : end - 1]) * 0.5
            for i in range(3)
        ]
        grad_z = [vertical_slope(vel[i, here, TOP:end]) for i in range(3)]
        magnet = [mass[1, ghost], mass[2, ghost], mass[3, ghost]]
        gap, anisotropy, unit = stress(mass[0, ghost], magnet, grad_x, grad_y, grad_z)
        third = gap * (1.0 / 3.0)
        along_x, along_y = gap * unit[0], gap * unit[1]
        px[0, ghost] = along_x * unit[0] - third
        cross = along_x * unit[1]
        px[1, ghost] = cross
        px[2, ghost] = along_x * unit[2]
        py[0, ghost, TOP:end] = cross
        py[1, ghost, TOP:end] = along_y * unit[1] - third
        py[2, ghost, TOP:end] = along_y * unit[2]
        pzz[ghost] = gap * unit[2] * unit[2] - third
        heat[ghost] = gap * anisotropy
        return carry

    lax.fori_loop(0, columns + 2, tensor_column, 0, unroll=3)

    def update_column(column, carry):
        ghost = column + 1
        inverse = 1.0 / mass[0, ghost]

        def slope(axis):
            return (px[axis, ghost + 1] - px[axis, ghost - 1]) * 0.5 + (
                py[axis, ghost, TOP + 1 : end + 1] - py[axis, ghost, TOP - 1 : end - 1]
            ) * 0.5

        vertical = (px[2, ghost], py[2, ghost, TOP:end], pzz[ghost])
        for axis in range(4):
            flat = column * 4 + axis
            slot = lax.bitwise_xor(info[3], flat // share)
            if axis < 3:
                force = slope(axis) + vertical_slope(vertical[axis])
                out[slot, flat % share] = fields[axis, column] + force * inverse
            else:
                out[slot, flat % share] = fields[6, column] + heat[ghost]
        return carry

    lax.fori_loop(0, columns, update_column, 0, unroll=4)


def updated_columns(info, fields, density, *layers):
    columns, cells, depth = density.shape
    tall = cells + 2 * TOP
    slots = lax.axis_size("az")
    smem = pl.BlockSpec(memory_space=pltpu.SMEM)
    vmem = pl.BlockSpec(memory_space=pltpu.VMEM)
    f32 = jnp.float32
    return pl.pallas_call(
        stress_kernel,
        out_shape=jax.ShapeDtypeStruct((slots, 4 * columns // slots, cells, depth), f32),
        in_specs=[smem] + [vmem] * 10,
        out_specs=vmem,
        scratch_shapes=[
            pltpu.VMEM((PACKED, 2 * cells + TOP, depth), f32),
            pltpu.VMEM((3, columns + 4, tall, depth), f32),
            pltpu.VMEM((4, columns + 2, cells, depth), f32),
            pltpu.VMEM((3, columns + 2, cells, depth), f32),
            pltpu.VMEM((3, columns + 2, tall, depth), f32),
            pltpu.VMEM((columns + 2, cells, depth), f32),
            pltpu.VMEM((columns + 2, cells, depth), f32),
        ],
        compiler_params=pltpu.CompilerParams(vmem_limit_bytes=24 * 2**20),
        name="stress_update",
    )(info, fields, density, *layers)


def move_kernel(quantities, rank, shift, frac, gathered, out, twice):
    slots, share, cells, depth = gathered.shape
    total = slots * cells
    me = rank[0]
    for item in range(share):
        column, _ = pair_of(me, item, share, quantities)
        fraction = frac[column].astype(jnp.float32) * (1.0 / FRAC_DEN)
        bend = fraction * (1.0 - fraction) * 0.25
        start = TOP + lax.rem(total - shift[column], total)

        def lay(slot, carry):
            rows = gathered[slot, item]
            spot = pl.multiple_of(TOP + lax.bitwise_xor(me, slot) * cells, TOP)
            twice[item, pl.ds(spot, cells)] = rows
            twice[item, pl.ds(pl.multiple_of(spot + total, TOP), cells)] = rows
            return carry

        lax.fori_loop(0, slots, lay, 0, unroll=4)
        twice[item, 0:TOP] = twice[item, total : total + TOP]

        def blend(slot, carry):
            spot = start + lax.bitwise_xor(me, slot) * cells
            back_two = twice[item, pl.ds(spot - 2, cells)]
            back_one = twice[item, pl.ds(spot - 1, cells)]
            centre = twice[item, pl.ds(spot, cells)]
            ahead = twice[item, pl.ds(spot + 1, cells)]
            out[slot, item] = (
                centre
                + fraction * (back_one - centre)
                + bend * ((centre - back_two) - (ahead - back_one))
            )
            return carry

        lax.fori_loop(0, slots, blend, 0, unroll=4)


def move_columns(gathered, quantities, rank, shift_int, frac_num):
    azimuths, share, cells, depth = gathered.shape
    smem = pl.BlockSpec(memory_space=pltpu.SMEM)
    vmem = pl.BlockSpec(memory_space=pltpu.VMEM)
    return pl.pallas_call(
        functools.partial(move_kernel, quantities),
        out_shape=jax.ShapeDtypeStruct(gathered.shape, jnp.float32),
        in_specs=[smem, smem, smem, vmem],
        out_specs=vmem,
        scratch_shapes=[pltpu.VMEM((share, 2 * azimuths * cells + TOP, depth), jnp.float32)],
        compiler_params=pltpu.CompilerParams(vmem_limit_bytes=16 * 2**20),
        name="move",
    )(rank, shift_int, frac_num, gathered)


def azimuthal_layers(head, tail):
    azimuths = lax.axis_size("az")
    even = lax.axis_index("az") % 2 == 0
    inner = [(az, az ^ 1) for az in range(azimuths)]
    outer = [(az, (az - 1 if az % 2 == 0 else az + 1) % azimuths) for az in range(azimuths)]
    far = lax.ppermute(jnp.where(even, head, tail), "az", outer)
    near = lax.ppermute(jnp.where(even, tail, head), "az", inner)
    return jnp.where(even, far, near), jnp.where(even, near, far)


def rims(blocks, low, high, before, after):
    radials = lax.axis_size("rad")
    azimuths = lax.axis_size("az")
    rad = lax.axis_index("rad")
    last = radials - 1

    def flat(rad, az):
        return rad * azimuths + az % azimuths

    def wrap(data, steps):
        pairs = [(flat(last, az), flat(0, az + steps)) for az in range(azimuths)]
        pairs += [(flat(0, az), flat(last, az - steps)) for az in range(azimuths)]
        return lax.ppermute(data, ("rad", "az"), pairs)

    def with_ends(main, column):
        ends = jnp.stack([before[0:3, column], after[0:3, column]], axis=1)
        ends = ends.reshape(1, 6, main.shape[-1])
        ends = jnp.pad(ends, ((0, 0), (0, main.shape[1] - 6), (0, 0)))
        return jnp.concatenate([main, ends], axis=0)

    low, high = with_ends(low, 0), with_ends(high, -1)
    edge = jnp.where(rad == 0, low, high)
    if radials == 2:
        other = jnp.where(rad == 0, high, low)
        below = above = lax.ppermute(other, "rad", [(0, 1), (1, 0)])
    else:
        below = lax.ppermute(high, "rad", [(i, i + 1) for i in range(last)])
        above = lax.ppermute(low, "rad", [(i + 1, i) for i in range(last)])

    def branch(steps):
        return lambda data: (wrap(data, steps), wrap(data, steps + 1))

    whole, next_one = lax.switch(blocks, [branch(steps) for steps in range(azimuths)], edge)
    return below, above, whole, next_one


def local(fields, density, shift_int, frac_num, boundary_shift):
    columns, cells, _ = density.shape
    radials = lax.axis_size("rad")
    rad = lax.axis_index("rad")
    shear_cells = boundary_shift[0]
    az = lax.axis_index("az")
    rank = az.reshape(1)
    head, tail, low, high, still, fields, density = pack(rank, fields, density)
    before, after = azimuthal_layers(head, tail)
    count = still.shape[0]
    radix = digit_radix(count)
    span = count // radix
    cut = still.reshape(1, radix, span, *still.shape[1:])
    parts = [cut[:, 0]] + [send_step(cut, step) for step in (2, 3, 1) if step < radix]
    before, after, parts = lax.optimization_barrier((before, after, parts))
    parts = parts[:1] + parts[-1:] + parts[1:-1]
    layers = rims(shear_cells // cells, low, high, before, after)
    parts, layers = lax.optimization_barrier((parts, layers))
    still = swap(jnp.stack(parts, axis=1).reshape(still.shape), span)
    info = jnp.stack(
        [
            (rad == 0).astype(jnp.int32),
            (rad == radials - 1).astype(jnp.int32),
            shear_cells % cells,
            az,
        ]
    )
    moving = updated_columns(info, fields, density, head, tail, before, after, *layers)
    moving, still = lax.optimization_barrier((moving, still))
    moving = swap(moving)
    still = swap(move_columns(still, 4, rank, shift_int, frac_num))
    moving = swap(move_columns(moving, 4, rank, shift_int, frac_num))
    return join(rank, moving, still, columns)


def solution(mesh):
    in_specs = (P(None, "rad", "az", None), P("rad", "az", None), P("rad"), P("rad"), P())
    out_specs = (P(None, "rad", "az", None), P("rad", "az", None))
    return jax.shard_map(local, mesh=mesh, in_specs=in_specs, out_specs=out_specs, check_vma=False)
```

```python
import functools

import jax
import jax.numpy as jnp
from jax import lax
from jax.experimental import pallas as pl
from jax.experimental.pallas import tpu as pltpu
from jax.sharding import PartitionSpec as P

FRAC_DEN = 64

shear_jump = 1.5
visc_step = 0.05
field_floor = 0.25

PACKED = 10
TOP = 8


def up_and_down(values):
    lane = lax.broadcasted_iota(jnp.int32, values.shape, values.ndim - 1)
    depth = values.shape[-1]
    up = pltpu.roll(values, depth - 1, values.ndim - 1)
    down = pltpu.roll(values, 1, values.ndim - 1)
    return jnp.where(lane == depth - 1, values, up), jnp.where(lane == 0, values, down)


def vertical_slope(values):
    up, down = up_and_down(values)
    return (up - down) * 0.5


def stress(density, magnet, grad_x, grad_y, grad_z):
    square = magnet[0] * magnet[0] + magnet[1] * magnet[1] + magnet[2] * magnet[2]
    inverse = lax.rsqrt(jnp.maximum(square, field_floor))
    unit = [component * inverse for component in magnet]
    slopes = (grad_x, grad_y, grad_z)
    aligned = None
    for direction in range(3):
        along = (
            unit[0] * slopes[direction][0]
            + unit[1] * slopes[direction][1]
            + unit[2] * slopes[direction][2]
        )
        term = unit[direction] * along
        aligned = term if aligned is None else aligned + term
    anisotropy = aligned - (grad_x[0] + grad_y[1] + grad_z[2]) * (1.0 / 3.0)
    gap = (3.0 * visc_step) * density * anisotropy
    return gap, anisotropy, unit


def pack_kernel(quantities, rank, fields, density, head, tail, low, high, still):
    columns, cells, depth = density.shape
    slots, share = still.shape[0], still.shape[1]

    def source(row):
        if row == 3:
            return density
        return fields.at[row if row < 3 else row - 1 if row < 7 else row - 7]

    for row in range(PACKED):
        second = 1 if row >= 7 else 0
        origin = source(row)
        low[row] = origin[second]
        high[row] = origin[columns - 1 - second]
        for column in range(columns):
            head[row, column : column + 1] = origin[column, second : second + 1]
            tail[row, column : column + 1] = origin[column, cells - 1 - second : cells - second]
    for slot in range(slots):
        for item in range(share):
            column, row = pair_of(lax.bitwise_xor(rank[0], slot), item, share, quantities)
            if isinstance(row, int):
                still[slot, item] = density[column] if row == 0 else fields[2 + row, column]
            else:
                still[slot, item] = jnp.where(
                    row == 0, density[column], fields[jnp.maximum(row, 1) + 2, column]
                )


def pair_of(rank, item, share, quantities):
    if share % quantities == 0:
        return rank * (share // quantities) + item // quantities, item % quantities
    flat = rank * share + item
    return flat // quantities, flat % quantities


def pack(rank, fields, density):
    columns, cells, depth = density.shape
    slots = lax.axis_size("az")
    share = 4 * columns // slots
    f32 = jnp.float32
    layer = jax.ShapeDtypeStruct((PACKED, columns, depth), f32)
    rim = jax.ShapeDtypeStruct((PACKED, cells, depth), f32)
    vmem = pl.BlockSpec(memory_space=pltpu.VMEM)
    return pl.pallas_call(
        functools.partial(pack_kernel, 4),
        out_shape=(
            layer,
            layer,
            rim,
            rim,
            jax.ShapeDtypeStruct((slots, share, cells, depth), f32),
        ),
        in_specs=[pl.BlockSpec(memory_space=pltpu.SMEM), vmem, vmem],
        out_specs=[vmem] * 5,
        compiler_params=pltpu.CompilerParams(vmem_limit_bytes=16 * 2**20),
        name="pack",
    )(rank, fields, density)


def join_kernel(quantities, rank, moving, still, new_fields, new_density):
    slots, share = still.shape[0], still.shape[1]
    for slot in range(slots):
        for item in range(share):
            column, row = pair_of(lax.bitwise_xor(rank[0], slot), item, share, quantities)
            if isinstance(row, int):
                new_fields[6 if row == 3 else row, column] = moving[slot, item]
                if row == 0:
                    new_density[column] = still[slot, item]
                else:
                    new_fields[2 + row, column] = still[slot, item]
            else:
                new_fields[jnp.where(row == 3, 6, row), column] = moving[slot, item]

                @pl.when(row == 0)
                def _():
                    new_density[column] = still[slot, item]

                @pl.when(row > 0)
                def _():
                    new_fields[2 + row, column] = still[slot, item]


def join(rank, moving, still, columns):
    _, _, cells, depth = still.shape
    f32 = jnp.float32
    vmem = pl.BlockSpec(memory_space=pltpu.VMEM)
    return pl.pallas_call(
        functools.partial(join_kernel, 4),
        out_shape=(
            jax.ShapeDtypeStruct((7, columns, cells, depth), f32),
            jax.ShapeDtypeStruct((columns, cells, depth), f32),
        ),
        in_specs=[pl.BlockSpec(memory_space=pltpu.SMEM), vmem, vmem],
        out_specs=[vmem] * 2,
        compiler_params=pltpu.CompilerParams(vmem_limit_bytes=16 * 2**20),
        name="join",
    )(rank, moving, still)


def swap(slots):
    count = slots.shape[0]
    stride = count
    while stride > 1:
        radix = 4 if stride % 4 == 0 else 2
        stride //= radix
        cut = slots.reshape(count // (radix * stride), radix, stride, *slots.shape[1:])
        parts = [cut[:, 0]]
        for step in range(1, radix):
            pairs = [(rank, rank ^ (step * stride)) for rank in range(count)]
            parts.append(lax.ppermute(cut[:, step], "az", pairs))
        slots = jnp.stack(parts, axis=1).reshape(slots.shape)
    return slots


def stress_kernel(
    info,
    fields,
    density,
    head,
    tail,
    before,
    after,
    straight_below,
    straight_above,
    whole,
    next_one,
    out,
    joined,
    vel,
    mass,
    px,
    py,
    pzz,
    heat,
):
    columns, cells, depth = density.shape
    share = out.shape[1]
    first, last, remainder = info[0], info[1], info[2]
    end = TOP + cells

    def place(far, near, ghost, start, jump):
        for component in range(3):
            added = jump if component == 1 else 0.0
            vel[component, near, TOP - 1 : end + 1] = (
                joined[component, pl.ds(start, cells + 2)] + added
            )
            vel[component, far, TOP:end] = joined[7 + component, pl.ds(start + 1, cells)] + added
        for row in range(4):
            mass[row, ghost] = joined[3 + row, pl.ds(start + 1, cells)]

    def lay(one, two):
        for row in range(PACKED):
            joined[row, 1 : cells + 1] = one[row]
            if two is not None:
                joined[row, cells + 1 : 2 * cells + 1] = two[row]
        final = one if two is None else two
        spot = (1 if two is None else 2) * cells + 1
        for component in range(3):
            joined[component, 0:1] = one[PACKED, 2 * component : 2 * component + 1]
            joined[component, spot : spot + 1] = final[PACKED, 2 * component + 1 : 2 * component + 2]

    below = (0, 1, 0)
    above = (columns + 3, columns + 2, columns + 1)

    @pl.when(first == 1)
    def _():
        lay(next_one, whole)
        place(*below, cells - remainder, shear_jump)

    @pl.when(first == 0)
    def _():
        lay(straight_below, None)
        place(*below, 0, 0.0)

    @pl.when(last == 1)
    def _():
        lay(whole, next_one)
        place(*above, remainder, -shear_jump)

    @pl.when(last == 0)
    def _():
        lay(straight_above, None)
        place(*above, 0, 0.0)

    vel[:, 2 : columns + 2, TOP:end] = fields[0:3]
    mass[0, 1 : columns + 1] = density[...]
    mass[1:4, 1 : columns + 1] = fields[3:6]
    for component in range(3):
        for column in range(columns):
            vel[component, 2 + column, TOP - 1 : TOP] = before[component, column : column + 1]
            vel[component, 2 + column, end : end + 1] = after[component, column : column + 1]

    for layer, spot, high, low in (
        (before, TOP - 1, (head, 0), (before, 7)),
        (after, end, (after, 7), (tail, 0)),
    ):
        grad_x, grad_y, grad_z = [], [], []
        for component in range(3):
            row = layer[component]
            left = jnp.concatenate(
                [vel[component, 1, spot : spot + 1], layer[component, 0 : columns - 1]], axis=0
            )
            right = jnp.concatenate(
                [layer[component, 1:columns], vel[component, columns + 2, spot : spot + 1]], axis=0
            )
            grad_x.append((right - left) * 0.5)
            grad_y.append((high[0][high[1] + component] - low[0][low[1] + component]) * 0.5)
            grad_z.append(vertical_slope(row))
        magnet = [layer[4], layer[5], layer[6]]
        gap, _, unit = stress(layer[3], magnet, grad_x, grad_y, grad_z)
        edge = gap * unit[1]
        parts = (edge * unit[0], edge * unit[1] - gap * (1.0 / 3.0), edge * unit[2])
        for row in range(3):
            for column in range(columns):
                py[row, 1 + column, spot : spot + 1] = parts[row][column : column + 1]

    def tensor_column(ghost, carry):
        here = ghost + 1
        grad_x = [
            (vel[i, here + 1, TOP:end] - vel[i, here - 1, TOP:end]) * 0.5 for i in range(3)
        ]
        grad_y = [
            (vel[i, here, TOP + 1 : end + 1] - vel[i, here, TOP - 1 : end - 1]) * 0.5
            for i in range(3)
        ]
        grad_z = [vertical_slope(vel[i, here, TOP:end]) for i in range(3)]
        magnet = [mass[1, ghost], mass[2, ghost], mass[3, ghost]]
        gap, anisotropy, unit = stress(mass[0, ghost], magnet, grad_x, grad_y, grad_z)
        third = gap * (1.0 / 3.0)
        along_x, along_y = gap * unit[0], gap * unit[1]
        px[0, ghost] = along_x * unit[0] - third
        cross = along_x * unit[1]
        px[1, ghost] = cross
        px[2, ghost] = along_x * unit[2]
        py[0, ghost, TOP:end] = cross
        py[1, ghost, TOP:end] = along_y * unit[1] - third
        py[2, ghost, TOP:end] = along_y * unit[2]
        pzz[ghost] = gap * unit[2] * unit[2] - third
        heat[ghost] = gap * anisotropy
        return carry

    lax.fori_loop(0, columns + 2, tensor_column, 0, unroll=3)

    def update_column(column, carry):
        ghost = column + 1
        inverse = 1.0 / mass[0, ghost]

        def slope(axis):
            return (px[axis, ghost + 1] - px[axis, ghost - 1]) * 0.5 + (
                py[axis, ghost, TOP + 1 : end + 1] - py[axis, ghost, TOP - 1 : end - 1]
            ) * 0.5

        vertical = (px[2, ghost], py[2, ghost, TOP:end], pzz[ghost])
        for axis in range(4):
            flat = column * 4 + axis
            slot = lax.bitwise_xor(info[3], flat // share)
            if axis < 3:
                force = slope(axis) + vertical_slope(vertical[axis])
                out[slot, flat % share] = fields[axis, column] + force * inverse
            else:
                out[slot, flat % share] = fields[6, column] + heat[ghost]
        return carry

    lax.fori_loop(0, columns, update_column, 0, unroll=4)


def updated_columns(info, fields, density, *layers):
    columns, cells, depth = density.shape
    tall = cells + 2 * TOP
    slots = lax.axis_size("az")
    smem = pl.BlockSpec(memory_space=pltpu.SMEM)
    vmem = pl.BlockSpec(memory_space=pltpu.VMEM)
    f32 = jnp.float32
    return pl.pallas_call(
        stress_kernel,
        out_shape=jax.ShapeDtypeStruct((slots, 4 * columns // slots, cells, depth), f32),
        in_specs=[smem] + [vmem] * 10,
        out_specs=vmem,
        scratch_shapes=[
            pltpu.VMEM((PACKED, 2 * cells + TOP, depth), f32),
            pltpu.VMEM((3, columns + 4, tall, depth), f32),
            pltpu.VMEM((4, columns + 2, cells, depth), f32),
            pltpu.VMEM((3, columns + 2, cells, depth), f32),
            pltpu.VMEM((3, columns + 2, tall, depth), f32),
            pltpu.VMEM((columns + 2, cells, depth), f32),
            pltpu.VMEM((columns + 2, cells, depth), f32),
        ],
        compiler_params=pltpu.CompilerParams(vmem_limit_bytes=24 * 2**20),
        name="stress_update",
    )(info, fields, density, *layers)


def move_kernel(quantities, rank, shift, frac, gathered, out, twice):
    slots, share, cells, depth = gathered.shape
    total = slots * cells
    me = rank[0]
    for item in range(share):
        column, _ = pair_of(me, item, share, quantities)
        fraction = frac[column].astype(jnp.float32) * (1.0 / FRAC_DEN)
        bend = fraction * (1.0 - fraction) * 0.25
        start = TOP + lax.rem(total - shift[column], total)

        def lay(slot, carry):
            rows = gathered[slot, item]
            spot = pl.multiple_of(TOP + lax.bitwise_xor(me, slot) * cells, TOP)
            twice[item, pl.ds(spot, cells)] = rows
            twice[item, pl.ds(pl.multiple_of(spot + total, TOP), cells)] = rows
            return carry

        lax.fori_loop(0, slots, lay, 0, unroll=4)
        twice[item, 0:TOP] = twice[item, total : total + TOP]

        def blend(slot, carry):
            spot = start + lax.bitwise_xor(me, slot) * cells
            back_two = twice[item, pl.ds(spot - 2, cells)]
            back_one = twice[item, pl.ds(spot - 1, cells)]
            centre = twice[item, pl.ds(spot, cells)]
            ahead = twice[item, pl.ds(spot + 1, cells)]
            out[slot, item] = (
                centre
                + fraction * (back_one - centre)
                + bend * ((centre - back_two) - (ahead - back_one))
            )
            return carry

        lax.fori_loop(0, slots, blend, 0, unroll=4)


def move_columns(gathered, quantities, rank, shift_int, frac_num):
    azimuths, share, cells, depth = gathered.shape
    smem = pl.BlockSpec(memory_space=pltpu.SMEM)
    vmem = pl.BlockSpec(memory_space=pltpu.VMEM)
    return pl.pallas_call(
        functools.partial(move_kernel, quantities),
        out_shape=jax.ShapeDtypeStruct(gathered.shape, jnp.float32),
        in_specs=[smem, smem, smem, vmem],
        out_specs=vmem,
        scratch_shapes=[pltpu.VMEM((share, 2 * azimuths * cells + TOP, depth), jnp.float32)],
        compiler_params=pltpu.CompilerParams(vmem_limit_bytes=16 * 2**20),
        name="move",
    )(rank, shift_int, frac_num, gathered)


def azimuthal_layers(head, tail):
    azimuths = lax.axis_size("az")
    even = lax.axis_index("az") % 2 == 0
    inner = [(az, az ^ 1) for az in range(azimuths)]
    outer = [(az, (az - 1 if az % 2 == 0 else az + 1) % azimuths) for az in range(azimuths)]
    far = lax.ppermute(jnp.where(even, head, tail), "az", outer)
    near = lax.ppermute(jnp.where(even, tail, head), "az", inner)
    return jnp.where(even, far, near), jnp.where(even, near, far)


def rims(blocks, low, high, before, after):
    radials = lax.axis_size("rad")
    azimuths = lax.axis_size("az")
    rad = lax.axis_index("rad")
    last = radials - 1

    def flat(rad, az):
        return rad * azimuths + az % azimuths

    def wrap(data, steps):
        pairs = [(flat(last, az), flat(0, az + steps)) for az in range(azimuths)]
        pairs += [(flat(0, az), flat(last, az - steps)) for az in range(azimuths)]
        return lax.ppermute(data, ("rad", "az"), pairs)

    def with_ends(main, column):
        ends = jnp.stack([before[0:3, column], after[0:3, column]], axis=1)
        ends = ends.reshape(1, 6, main.shape[-1])
        ends = jnp.pad(ends, ((0, 0), (0, main.shape[1] - 6), (0, 0)))
        return jnp.concatenate([main, ends], axis=0)

    low, high = with_ends(low, 0), with_ends(high, -1)
    edge = jnp.where(rad == 0, low, high)
    if radials == 2:
        other = jnp.where(rad == 0, high, low)
        below = above = lax.ppermute(other, "rad", [(0, 1), (1, 0)])
    else:
        below = lax.ppermute(high, "rad", [(i, i + 1) for i in range(last)])
        above = lax.ppermute(low, "rad", [(i + 1, i) for i in range(last)])

    def branch(steps):
        return lambda data: (wrap(data, steps), wrap(data, steps + 1))

    whole, next_one = lax.switch(blocks, [branch(steps) for steps in range(azimuths)], edge)
    return below, above, whole, next_one


def local(fields, density, shift_int, frac_num, boundary_shift):
    columns, cells, _ = density.shape
    radials = lax.axis_size("rad")
    rad = lax.axis_index("rad")
    shear_cells = boundary_shift[0]
    az = lax.axis_index("az")
    rank = az.reshape(1)
    head, tail, low, high, still = pack(rank, fields, density)
    before, after = azimuthal_layers(head, tail)
    before, after, still = lax.optimization_barrier((before, after, still))
    still = swap(still)
    layers = rims(shear_cells // cells, low, high, before, after)
    info = jnp.stack(
        [
            (rad == 0).astype(jnp.int32),
            (rad == radials - 1).astype(jnp.int32),
            shear_cells % cells,
            az,
        ]
    )
    moving = updated_columns(info, fields, density, head, tail, before, after, *layers)
    moving = swap(moving)
    still = swap(move_columns(still, 4, rank, shift_int, frac_num))
    moving = swap(move_columns(moving, 4, rank, shift_int, frac_num))
    return join(rank, moving, still, columns)


def solution(mesh):
    in_specs = (P(None, "rad", "az", None), P("rad", "az", None), P("rad"), P("rad"), P())
    out_specs = (P(None, "rad", "az", None), P("rad", "az", None))
    return jax.shard_map(local, mesh=mesh, in_specs=in_specs, out_specs=out_specs, check_vma=False)
```

```python
import functools

import jax
import jax.numpy as jnp
from jax import lax
from jax.experimental import pallas as pl
from jax.experimental.pallas import tpu as pltpu
from jax.sharding import PartitionSpec as P

FRAC_DEN = 64

shear_jump = 1.5
visc_step = 0.05
field_floor = 0.25

PACKED = 10
TOP = 8


def up_and_down(values):
    lane = lax.broadcasted_iota(jnp.int32, values.shape, values.ndim - 1)
    depth = values.shape[-1]
    up = pltpu.roll(values, depth - 1, values.ndim - 1)
    down = pltpu.roll(values, 1, values.ndim - 1)
    return jnp.where(lane == depth - 1, values, up), jnp.where(lane == 0, values, down)


def vertical_slope(values):
    up, down = up_and_down(values)
    return (up - down) * 0.5


def stress(density, magnet, grad_x, grad_y, grad_z):
    square = magnet[0] * magnet[0] + magnet[1] * magnet[1] + magnet[2] * magnet[2]
    inverse = lax.rsqrt(jnp.maximum(square, field_floor))
    unit = [component * inverse for component in magnet]
    slopes = (grad_x, grad_y, grad_z)
    aligned = None
    for direction in range(3):
        along = (
            unit[0] * slopes[direction][0]
            + unit[1] * slopes[direction][1]
            + unit[2] * slopes[direction][2]
        )
        term = unit[direction] * along
        aligned = term if aligned is None else aligned + term
    anisotropy = aligned - (grad_x[0] + grad_y[1] + grad_z[2]) * (1.0 / 3.0)
    gap = (3.0 * visc_step) * density * anisotropy
    return gap, anisotropy, unit


def pack_kernel(
    quantities, rank, fields_in, density_in, head, tail, low, high, still, fields, density, sems
):
    columns, cells, depth = density.shape
    slots, share = still.shape[0], still.shape[1]
    copies = [
        pltpu.make_async_copy(density_in, density, sems.at[0]),
        pltpu.make_async_copy(fields_in.at[0:6], fields, sems.at[1]),
    ]
    for copy in copies:
        copy.start()
    for copy in copies:
        copy.wait()

    def source(row):
        if row == 3:
            return density
        return fields.at[row if row < 3 else row - 1 if row < 7 else row - 7]

    for row in range(PACKED):
        second = 1 if row >= 7 else 0
        origin = source(row)
        low[row] = origin[second]
        high[row] = origin[columns - 1 - second]
        for column in range(columns):
            head[row, column : column + 1] = origin[column, second : second + 1]
            tail[row, column : column + 1] = origin[column, cells - 1 - second : cells - second]
    for slot in range(slots):
        for item in range(share):
            column, row = pair_of(lax.bitwise_xor(rank[0], slot), item, share, quantities)
            if isinstance(row, int):
                still[slot, item] = density[column] if row == 0 else fields[2 + row, column]
            else:
                still[slot, item] = jnp.where(
                    row == 0, density[column], fields[jnp.maximum(row, 1) + 2, column]
                )


def pair_of(rank, item, share, quantities):
    if share % quantities == 0:
        return rank * (share // quantities) + item // quantities, item % quantities
    flat = rank * share + item
    return flat // quantities, flat % quantities


def pack(rank, fields, density):
    columns, cells, depth = density.shape
    slots = lax.axis_size("az")
    share = 4 * columns // slots
    f32 = jnp.float32
    layer = jax.ShapeDtypeStruct((PACKED, columns, depth), f32)
    rim = jax.ShapeDtypeStruct((PACKED, cells, depth), f32)
    vmem = pl.BlockSpec(memory_space=pltpu.VMEM)
    return pl.pallas_call(
        functools.partial(pack_kernel, 4),
        out_shape=(
            layer,
            layer,
            rim,
            rim,
            jax.ShapeDtypeStruct((slots, share, cells, depth), f32),
        ),
        in_specs=[pl.BlockSpec(memory_space=pltpu.SMEM)] + [pl.BlockSpec(memory_space=pltpu.HBM)] * 2,
        out_specs=[vmem] * 5,
        scratch_shapes=[
            pltpu.VMEM((6, columns, cells, depth), f32),
            pltpu.VMEM((columns, cells, depth), f32),
            pltpu.SemaphoreType.DMA((2,)),
        ],
        compiler_params=pltpu.CompilerParams(vmem_limit_bytes=16 * 2**20),
        name="pack",
    )(rank, fields, density)


def join_kernel(quantities, returned, new_fields, new_density):
    slots, share = returned.shape[0], returned.shape[1] // 2
    for slot in range(slots):
        for item in range(share):
            column, row = pair_of(slot, item, share, quantities)
            new_fields[6 if row == 3 else row, column] = returned[slot, item]
            if row == 0:
                new_density[column] = returned[slot, share + item]
            else:
                new_fields[2 + row, column] = returned[slot, share + item]


def join(returned, columns):
    _, _, cells, depth = returned.shape
    f32 = jnp.float32
    vmem = pl.BlockSpec(memory_space=pltpu.VMEM)
    return pl.pallas_call(
        functools.partial(join_kernel, 4),
        out_shape=(
            jax.ShapeDtypeStruct((7, columns, cells, depth), f32),
            jax.ShapeDtypeStruct((columns, cells, depth), f32),
        ),
        in_specs=[vmem],
        out_specs=[vmem] * 2,
        compiler_params=pltpu.CompilerParams(vmem_limit_bytes=16 * 2**20),
        name="join",
    )(returned)


def digit_radix(span):
    return 4 if span % 4 == 0 else 2


def send_step(cut, step):
    radix, stride = cut.shape[1], cut.shape[2]
    count = cut.shape[0] * radix * stride
    pairs = [(rank, rank ^ (step * stride)) for rank in range(count)]
    return lax.ppermute(cut[:, step], "az", pairs)


def swap(slots, span=None):
    span = slots.shape[0] if span is None else span
    while span > 1:
        radix = digit_radix(span)
        span //= radix
        cut = slots.reshape(-1, radix, span, *slots.shape[1:])
        parts = [cut[:, 0]] + [send_step(cut, step) for step in range(1, radix)]
        slots = jnp.stack(parts, axis=1).reshape(slots.shape)
    return slots


def stress_kernel(
    info,
    fields,
    density,
    head,
    tail,
    before,
    after,
    straight_below,
    straight_above,
    whole,
    next_one,
    out,
    joined,
    vel,
    mass,
    px,
    py,
    pzz,
    heat,
):
    columns, cells, depth = density.shape
    share = out.shape[1]
    first, last, remainder = info[0], info[1], info[2]
    end = TOP + cells

    def place(far, near, ghost, start, jump):
        for component in range(3):
            added = jump if component == 1 else 0.0
            vel[component, near, TOP - 1 : end + 1] = (
                joined[component, pl.ds(start, cells + 2)] + added
            )
            vel[component, far, TOP:end] = joined[7 + component, pl.ds(start + 1, cells)] + added
        for row in range(4):
            mass[row, ghost] = joined[3 + row, pl.ds(start + 1, cells)]

    def lay(one, two):
        for row in range(PACKED):
            joined[row, 1 : cells + 1] = one[row]
            if two is not None:
                joined[row, cells + 1 : 2 * cells + 1] = two[row]
        final = one if two is None else two
        spot = (1 if two is None else 2) * cells + 1
        for component in range(3):
            joined[component, 0:1] = one[PACKED, 2 * component : 2 * component + 1]
            joined[component, spot : spot + 1] = final[PACKED, 2 * component + 1 : 2 * component + 2]

    below = (0, 1, 0)
    above = (columns + 3, columns + 2, columns + 1)

    @pl.when(first == 1)
    def _():
        lay(next_one, whole)
        place(*below, cells - remainder, shear_jump)

    @pl.when(first == 0)
    def _():
        lay(straight_below, None)
        place(*below, 0, 0.0)

    @pl.when(last == 1)
    def _():
        lay(whole, next_one)
        place(*above, remainder, -shear_jump)

    @pl.when(last == 0)
    def _():
        lay(straight_above, None)
        place(*above, 0, 0.0)

    vel[:, 2 : columns + 2, TOP:end] = fields[0:3]
    mass[0, 1 : columns + 1] = density[...]
    mass[1:4, 1 : columns + 1] = fields[3:6]
    for component in range(3):
        for column in range(columns):
            vel[component, 2 + column, TOP - 1 : TOP] = before[component, column : column + 1]
            vel[component, 2 + column, end : end + 1] = after[component, column : column + 1]

    for layer, spot, high, low in (
        (before, TOP - 1, (head, 0), (before, 7)),
        (after, end, (after, 7), (tail, 0)),
    ):
        grad_x, grad_y, grad_z = [], [], []
        for component in range(3):
            row = layer[component]
            left = jnp.concatenate(
                [vel[component, 1, spot : spot + 1], layer[component, 0 : columns - 1]], axis=0
            )
            right = jnp.concatenate(
                [layer[component, 1:columns], vel[component, columns + 2, spot : spot + 1]], axis=0
            )
            grad_x.append((right - left) * 0.5)
            grad_y.append((high[0][high[1] + component] - low[0][low[1] + component]) * 0.5)
            grad_z.append(vertical_slope(row))
        magnet = [layer[4], layer[5], layer[6]]
        gap, _, unit = stress(layer[3], magnet, grad_x, grad_y, grad_z)
        edge = gap * unit[1]
        parts = (edge * unit[0], edge * unit[1] - gap * (1.0 / 3.0), edge * unit[2])
        for row in range(3):
            for column in range(columns):
                py[row, 1 + column, spot : spot + 1] = parts[row][column : column + 1]

    def tensor_column(ghost, carry):
        here = ghost + 1
        grad_x = [
            (vel[i, here + 1, TOP:end] - vel[i, here - 1, TOP:end]) * 0.5 for i in range(3)
        ]
        grad_y = [
            (vel[i, here, TOP + 1 : end + 1] - vel[i, here, TOP - 1 : end - 1]) * 0.5
            for i in range(3)
        ]
        grad_z = [vertical_slope(vel[i, here, TOP:end]) for i in range(3)]
        magnet = [mass[1, ghost], mass[2, ghost], mass[3, ghost]]
        gap, anisotropy, unit = stress(mass[0, ghost], magnet, grad_x, grad_y, grad_z)
        third = gap * (1.0 / 3.0)
        along_x, along_y = gap * unit[0], gap * unit[1]
        px[0, ghost] = along_x * unit[0] - third
        cross = along_x * unit[1]
        px[1, ghost] = cross
        px[2, ghost] = along_x * unit[2]
        py[0, ghost, TOP:end] = cross
        py[1, ghost, TOP:end] = along_y * unit[1] - third
        py[2, ghost, TOP:end] = along_y * unit[2]
        pzz[ghost] = gap * unit[2] * unit[2] - third
        heat[ghost] = gap * anisotropy
        return carry

    lax.fori_loop(0, columns + 2, tensor_column, 0, unroll=3)

    def update_column(column, carry):
        ghost = column + 1
        inverse = 1.0 / mass[0, ghost]

        def slope(axis):
            return (px[axis, ghost + 1] - px[axis, ghost - 1]) * 0.5 + (
                py[axis, ghost, TOP + 1 : end + 1] - py[axis, ghost, TOP - 1 : end - 1]
            ) * 0.5

        vertical = (px[2, ghost], py[2, ghost, TOP:end], pzz[ghost])
        for axis in range(4):
            flat = column * 4 + axis
            slot = flat // share
            if axis < 3:
                force = slope(axis) + vertical_slope(vertical[axis])
                out[slot, flat % share] = fields[axis, column] + force * inverse
            else:
                out[slot, flat % share] = fields[6, column] + heat[ghost]
        return carry

    lax.fori_loop(0, columns, update_column, 0, unroll=4)


def updated_columns(info, fields, density, *layers):
    columns, cells, depth = density.shape
    tall = cells + 2 * TOP
    slots = lax.axis_size("az")
    smem = pl.BlockSpec(memory_space=pltpu.SMEM)
    vmem = pl.BlockSpec(memory_space=pltpu.VMEM)
    f32 = jnp.float32
    return pl.pallas_call(
        stress_kernel,
        out_shape=jax.ShapeDtypeStruct((slots, 4 * columns // slots, cells, depth), f32),
        in_specs=[smem] + [vmem] * 10,
        out_specs=vmem,
        scratch_shapes=[
            pltpu.VMEM((PACKED, 2 * cells + TOP, depth), f32),
            pltpu.VMEM((3, columns + 4, tall, depth), f32),
            pltpu.VMEM((4, columns + 2, cells, depth), f32),
            pltpu.VMEM((3, columns + 2, cells, depth), f32),
            pltpu.VMEM((3, columns + 2, tall, depth), f32),
            pltpu.VMEM((columns + 2, cells, depth), f32),
            pltpu.VMEM((columns + 2, cells, depth), f32),
        ],
        compiler_params=pltpu.CompilerParams(vmem_limit_bytes=24 * 2**20),
        name="stress_update",
    )(info, fields, density, *layers)


def move_kernel(quantities, mixed, rank, shift, frac, gathered, out, twice):
    slots, share, cells, depth = gathered.shape
    total = slots * cells
    me = rank[0]
    for item in range(share):
        column, _ = pair_of(me, item, share, quantities)
        fraction = frac[column].astype(jnp.float32) * (1.0 / FRAC_DEN)
        bend = fraction * (1.0 - fraction) * 0.25
        start = TOP + lax.rem(total - shift[column], total)

        def lay(slot, carry):
            rows = gathered[slot, item]
            block = lax.bitwise_xor(me, slot) if mixed else slot
            spot = pl.multiple_of(TOP + block * cells, TOP)
            twice[item, pl.ds(spot, cells)] = rows
            twice[item, pl.ds(pl.multiple_of(spot + total, TOP), cells)] = rows
            return carry

        lax.fori_loop(0, slots, lay, 0, unroll=4)
        twice[item, 0:TOP] = twice[item, total : total + TOP]

        def blend(slot, carry):
            spot = start + slot * cells
            back_two = twice[item, pl.ds(spot - 2, cells)]
            back_one = twice[item, pl.ds(spot - 1, cells)]
            centre = twice[item, pl.ds(spot, cells)]
            ahead = twice[item, pl.ds(spot + 1, cells)]
            out[slot, item] = (
                centre
                + fraction * (back_one - centre)
                + bend * ((centre - back_two) - (ahead - back_one))
            )
            return carry

        lax.fori_loop(0, slots, blend, 0, unroll=4)


def move_columns(gathered, quantities, mixed, rank, shift_int, frac_num):
    azimuths, share, cells, depth = gathered.shape
    smem = pl.BlockSpec(memory_space=pltpu.SMEM)
    vmem = pl.BlockSpec(memory_space=pltpu.VMEM)
    return pl.pallas_call(
        functools.partial(move_kernel, quantities, mixed),
        out_shape=jax.ShapeDtypeStruct(gathered.shape, jnp.float32),
        in_specs=[smem, smem, smem, vmem],
        out_specs=vmem,
        scratch_shapes=[pltpu.VMEM((share, 2 * azimuths * cells + TOP, depth), jnp.float32)],
        compiler_params=pltpu.CompilerParams(vmem_limit_bytes=16 * 2**20),
        name="move",
    )(rank, shift_int, frac_num, gathered)


def azimuthal_layers(head, tail):
    azimuths = lax.axis_size("az")
    even = lax.axis_index("az") % 2 == 0
    inner = [(az, az ^ 1) for az in range(azimuths)]
    outer = [(az, (az - 1 if az % 2 == 0 else az + 1) % azimuths) for az in range(azimuths)]
    far = lax.ppermute(jnp.where(even, head, tail), "az", outer)
    near = lax.ppermute(jnp.where(even, tail, head), "az", inner)
    return jnp.where(even, far, near), jnp.where(even, near, far)


def rims_and_stress(blocks, remainder, low, high, before, after, head, tail, fields, density, still):
    radials = lax.axis_size("rad")
    azimuths = lax.axis_size("az")
    rad = lax.axis_index("rad")
    last = radials - 1

    def flat(rad, az):
        return rad * azimuths + az % azimuths

    def wrap(data, steps):
        pairs = [(flat(last, az), flat(0, az + steps)) for az in range(azimuths)]
        pairs += [(flat(0, az), flat(last, az - steps)) for az in range(azimuths)]
        return lax.ppermute(data, ("rad", "az"), pairs)

    def with_ends(main, column):
        ends = jnp.stack([before[0:3, column], after[0:3, column]], axis=1)
        ends = ends.reshape(1, 6, main.shape[-1])
        ends = jnp.pad(ends, ((0, 0), (0, main.shape[1] - 6), (0, 0)))
        return jnp.concatenate([main, ends], axis=0)

    low, high = with_ends(low, 0), with_ends(high, -1)
    edge = jnp.where(rad == 0, low, high)
    others = (jnp.where(rad == 0, high, low),) if radials == 2 else (high, low)
    info = jnp.stack(
        [(rad == 0).astype(jnp.int32), (rad == last).astype(jnp.int32), remainder]
    )

    def branch(steps):
        def run(info, edge, others, before, after, head, tail, fields, density, still):
            whole, next_one = wrap(edge, steps), wrap(edge, steps + 1)
            if radials == 2:
                below = above = lax.ppermute(others[0], "rad", [(0, 1), (1, 0)])
            else:
                below = lax.ppermute(others[0], "rad", [(i, i + 1) for i in range(last)])
                above = lax.ppermute(others[1], "rad", [(i + 1, i) for i in range(last)])
            below, above, still = lax.optimization_barrier((below, above, still))
            count = still.shape[0]
            radix = digit_radix(count)
            cut = still.reshape(1, radix, count // radix, *still.shape[1:])
            parts = [send_step(cut, step) for step in range(1, radix)]
            moving = updated_columns(
                info, fields, density, head, tail, before, after, below, above, whole, next_one
            )
            return moving, jnp.stack([cut[:, 0]] + parts, axis=1).reshape(still.shape)

        return run

    branches = [branch(steps) for steps in range(azimuths)]
    return lax.switch(
        blocks, branches, info, edge, others, before, after, head, tail, fields, density, still
    )


def local(fields, density, shift_int, frac_num, boundary_shift):
    columns, cells, _ = density.shape
    shear_cells = boundary_shift[0]
    rank = lax.axis_index("az").reshape(1)
    head, tail, low, high, still = pack(rank, fields, density)
    before, after = azimuthal_layers(head, tail)
    moving, still = rims_and_stress(
        shear_cells // cells,
        shear_cells % cells,
        low,
        high,
        before,
        after,
        head,
        tail,
        fields,
        density,
        still,
    )
    still = swap(still, still.shape[0] // digit_radix(still.shape[0]))
    moving = lax.all_to_all(moving, "az", 0, 0, tiled=True)
    still = move_columns(still, 4, True, rank, shift_int, frac_num)
    moving = move_columns(moving, 4, False, rank, shift_int, frac_num)
    both = jnp.concatenate([moving, still], axis=1)
    return join(lax.all_to_all(both, "az", 0, 0, tiled=True), columns)


def solution(mesh):
    in_specs = (P(None, "rad", "az", None), P("rad", "az", None), P("rad"), P("rad"), P())
    out_specs = (P(None, "rad", "az", None), P("rad", "az", None))
    return jax.shard_map(local, mesh=mesh, in_specs=in_specs, out_specs=out_specs, check_vma=False)
```

```python
import functools

import jax
import jax.numpy as jnp
from jax import lax
from jax.experimental import pallas as pl
from jax.experimental.pallas import tpu as pltpu
from jax.sharding import PartitionSpec as P

FRAC_DEN = 64

shear_jump = 1.5
visc_step = 0.05
field_floor = 0.25

PACKED = 10
TOP = 8


def up_and_down(values):
    lane = lax.broadcasted_iota(jnp.int32, values.shape, values.ndim - 1)
    depth = values.shape[-1]
    up = pltpu.roll(values, depth - 1, values.ndim - 1)
    down = pltpu.roll(values, 1, values.ndim - 1)
    return jnp.where(lane == depth - 1, values, up), jnp.where(lane == 0, values, down)


def vertical_slope(values):
    up, down = up_and_down(values)
    return (up - down) * 0.5


def stress(density, magnet, grad_x, grad_y, grad_z):
    square = magnet[0] * magnet[0] + magnet[1] * magnet[1] + magnet[2] * magnet[2]
    inverse = lax.rsqrt(jnp.maximum(square, field_floor))
    unit = [component * inverse for component in magnet]
    slopes = (grad_x, grad_y, grad_z)
    aligned = None
    for direction in range(3):
        along = (
            unit[0] * slopes[direction][0]
            + unit[1] * slopes[direction][1]
            + unit[2] * slopes[direction][2]
        )
        term = unit[direction] * along
        aligned = term if aligned is None else aligned + term
    anisotropy = aligned - (grad_x[0] + grad_y[1] + grad_z[2]) * (1.0 / 3.0)
    gap = (3.0 * visc_step) * density * anisotropy
    return gap, anisotropy, unit


def pack_kernel(
    quantities, rank, fields_in, density_in, head, tail, low, high, still, fields, density, sems
):
    columns, cells, depth = density.shape
    slots, share = still.shape[0], still.shape[1]
    copies = [
        pltpu.make_async_copy(density_in, density, sems.at[0]),
        pltpu.make_async_copy(fields_in.at[0:6], fields, sems.at[1]),
    ]
    for copy in copies:
        copy.start()
    for copy in copies:
        copy.wait()

    def source(row):
        if row == 3:
            return density
        return fields.at[row if row < 3 else row - 1 if row < 7 else row - 7]

    for row in range(PACKED):
        second = 1 if row >= 7 else 0
        origin = source(row)
        low[row] = origin[second]
        high[row] = origin[columns - 1 - second]
        for column in range(columns):
            head[row, column : column + 1] = origin[column, second : second + 1]
            tail[row, column : column + 1] = origin[column, cells - 1 - second : cells - second]
    for slot in range(slots):
        for item in range(share):
            column, row = pair_of(slot, item, share, quantities)
            still[slot, item] = density[column] if row == 0 else fields[2 + row, column]


def pair_of(rank, item, share, quantities):
    if share % quantities == 0:
        return rank * (share // quantities) + item // quantities, item % quantities
    flat = rank * share + item
    return flat // quantities, flat % quantities


def pack(rank, fields, density):
    columns, cells, depth = density.shape
    slots = lax.axis_size("az")
    share = 4 * columns // slots
    f32 = jnp.float32
    layer = jax.ShapeDtypeStruct((PACKED, columns, depth), f32)
    rim = jax.ShapeDtypeStruct((PACKED, cells, depth), f32)
    vmem = pl.BlockSpec(memory_space=pltpu.VMEM)
    return pl.pallas_call(
        functools.partial(pack_kernel, 4),
        out_shape=(
            layer,
            layer,
            rim,
            rim,
            jax.ShapeDtypeStruct((slots, share, cells, depth), f32),
        ),
        in_specs=[pl.BlockSpec(memory_space=pltpu.SMEM)] + [pl.BlockSpec(memory_space=pltpu.HBM)] * 2,
        out_specs=[vmem] * 5,
        scratch_shapes=[
            pltpu.VMEM((6, columns, cells, depth), f32),
            pltpu.VMEM((columns, cells, depth), f32),
            pltpu.SemaphoreType.DMA((2,)),
        ],
        compiler_params=pltpu.CompilerParams(vmem_limit_bytes=16 * 2**20),
        name="pack",
    )(rank, fields, density)


def join_kernel(quantities, returned, new_fields, new_density):
    slots, share = returned.shape[0], returned.shape[1] // 2
    for slot in range(slots):
        for item in range(share):
            column, row = pair_of(slot, item, share, quantities)
            new_fields[6 if row == 3 else row, column] = returned[slot, item]
            if row == 0:
                new_density[column] = returned[slot, share + item]
            else:
                new_fields[2 + row, column] = returned[slot, share + item]


def join(returned, columns):
    _, _, cells, depth = returned.shape
    f32 = jnp.float32
    vmem = pl.BlockSpec(memory_space=pltpu.VMEM)
    return pl.pallas_call(
        functools.partial(join_kernel, 4),
        out_shape=(
            jax.ShapeDtypeStruct((7, columns, cells, depth), f32),
            jax.ShapeDtypeStruct((columns, cells, depth), f32),
        ),
        in_specs=[vmem],
        out_specs=[vmem] * 2,
        compiler_params=pltpu.CompilerParams(vmem_limit_bytes=16 * 2**20),
        name="join",
    )(returned)


def stress_kernel(
    info,
    fields,
    density,
    head,
    tail,
    before,
    after,
    straight_below,
    straight_above,
    whole,
    next_one,
    out,
    joined,
    vel,
    mass,
    px,
    py,
    pzz,
    heat,
):
    columns, cells, depth = density.shape
    share = out.shape[1]
    first, last, remainder = info[0], info[1], info[2]
    end = TOP + cells

    def place(far, near, ghost, start, jump):
        for component in range(3):
            added = jump if component == 1 else 0.0
            vel[component, near, TOP - 1 : end + 1] = (
                joined[component, pl.ds(start, cells + 2)] + added
            )
            vel[component, far, TOP:end] = joined[7 + component, pl.ds(start + 1, cells)] + added
        for row in range(4):
            mass[row, ghost] = joined[3 + row, pl.ds(start + 1, cells)]

    def lay(one, two):
        for row in range(PACKED):
            joined[row, 1 : cells + 1] = one[row]
            if two is not None:
                joined[row, cells + 1 : 2 * cells + 1] = two[row]
        final = one if two is None else two
        spot = (1 if two is None else 2) * cells + 1
        for component in range(3):
            joined[component, 0:1] = one[PACKED, 2 * component : 2 * component + 1]
            joined[component, spot : spot + 1] = final[PACKED, 2 * component + 1 : 2 * component + 2]

    below = (0, 1, 0)
    above = (columns + 3, columns + 2, columns + 1)

    @pl.when(first == 1)
    def _():
        lay(next_one, whole)
        place(*below, cells - remainder, shear_jump)

    @pl.when(first == 0)
    def _():
        lay(straight_below, None)
        place(*below, 0, 0.0)

    @pl.when(last == 1)
    def _():
        lay(whole, next_one)
        place(*above, remainder, -shear_jump)

    @pl.when(last == 0)
    def _():
        lay(straight_above, None)
        place(*above, 0, 0.0)

    vel[:, 2 : columns + 2, TOP:end] = fields[0:3]
    mass[0, 1 : columns + 1] = density[...]
    mass[1:4, 1 : columns + 1] = fields[3:6]
    for component in range(3):
        for column in range(columns):
            vel[component, 2 + column, TOP - 1 : TOP] = before[component, column : column + 1]
            vel[component, 2 + column, end : end + 1] = after[component, column : column + 1]

    for layer, spot, high, low in (
        (before, TOP - 1, (head, 0), (before, 7)),
        (after, end, (after, 7), (tail, 0)),
    ):
        grad_x, grad_y, grad_z = [], [], []
        for component in range(3):
            row = layer[component]
            left = jnp.concatenate(
                [vel[component, 1, spot : spot + 1], layer[component, 0 : columns - 1]], axis=0
            )
            right = jnp.concatenate(
                [layer[component, 1:columns], vel[component, columns + 2, spot : spot + 1]], axis=0
            )
            grad_x.append((right - left) * 0.5)
            grad_y.append((high[0][high[1] + component] - low[0][low[1] + component]) * 0.5)
            grad_z.append(vertical_slope(row))
        magnet = [layer[4], layer[5], layer[6]]
        gap, _, unit = stress(layer[3], magnet, grad_x, grad_y, grad_z)
        edge = gap * unit[1]
        parts = (edge * unit[0], edge * unit[1] - gap * (1.0 / 3.0), edge * unit[2])
        for row in range(3):
            for column in range(columns):
                py[row, 1 + column, spot : spot + 1] = parts[row][column : column + 1]

    def tensor_column(ghost, carry):
        here = ghost + 1
        grad_x = [
            (vel[i, here + 1, TOP:end] - vel[i, here - 1, TOP:end]) * 0.5 for i in range(3)
        ]
        grad_y = [
            (vel[i, here, TOP + 1 : end + 1] - vel[i, here, TOP - 1 : end - 1]) * 0.5
            for i in range(3)
        ]
        grad_z = [vertical_slope(vel[i, here, TOP:end]) for i in range(3)]
        magnet = [mass[1, ghost], mass[2, ghost], mass[3, ghost]]
        gap, anisotropy, unit = stress(mass[0, ghost], magnet, grad_x, grad_y, grad_z)
        third = gap * (1.0 / 3.0)
        along_x, along_y = gap * unit[0], gap * unit[1]
        px[0, ghost] = along_x * unit[0] - third
        cross = along_x * unit[1]
        px[1, ghost] = cross
        px[2, ghost] = along_x * unit[2]
        py[0, ghost, TOP:end] = cross
        py[1, ghost, TOP:end] = along_y * unit[1] - third
        py[2, ghost, TOP:end] = along_y * unit[2]
        pzz[ghost] = gap * unit[2] * unit[2] - third
        heat[ghost] = gap * anisotropy
        return carry

    lax.fori_loop(0, columns + 2, tensor_column, 0, unroll=3)

    def update_column(column, carry):
        ghost = column + 1
        inverse = 1.0 / mass[0, ghost]

        def slope(axis):
            return (px[axis, ghost + 1] - px[axis, ghost - 1]) * 0.5 + (
                py[axis, ghost, TOP + 1 : end + 1] - py[axis, ghost, TOP - 1 : end - 1]
            ) * 0.5

        vertical = (px[2, ghost], py[2, ghost, TOP:end], pzz[ghost])
        for axis in range(4):
            flat = column * 4 + axis
            slot = flat // share
            if axis < 3:
                force = slope(axis) + vertical_slope(vertical[axis])
                out[slot, flat % share] = fields[axis, column] + force * inverse
            else:
                out[slot, flat % share] = fields[6, column] + heat[ghost]
        return carry

    lax.fori_loop(0, columns, update_column, 0, unroll=4)


def updated_columns(info, fields, density, *layers):
    columns, cells, depth = density.shape
    tall = cells + 2 * TOP
    slots = lax.axis_size("az")
    smem = pl.BlockSpec(memory_space=pltpu.SMEM)
    vmem = pl.BlockSpec(memory_space=pltpu.VMEM)
    f32 = jnp.float32
    return pl.pallas_call(
        stress_kernel,
        out_shape=jax.ShapeDtypeStruct((slots, 4 * columns // slots, cells, depth), f32),
        in_specs=[smem] + [vmem] * 10,
        out_specs=vmem,
        scratch_shapes=[
            pltpu.VMEM((PACKED, 2 * cells + TOP, depth), f32),
            pltpu.VMEM((3, columns + 4, tall, depth), f32),
            pltpu.VMEM((4, columns + 2, cells, depth), f32),
            pltpu.VMEM((3, columns + 2, cells, depth), f32),
            pltpu.VMEM((3, columns + 2, tall, depth), f32),
            pltpu.VMEM((columns + 2, cells, depth), f32),
            pltpu.VMEM((columns + 2, cells, depth), f32),
        ],
        compiler_params=pltpu.CompilerParams(vmem_limit_bytes=24 * 2**20),
        name="stress_update",
    )(info, fields, density, *layers)


def move_kernel(quantities, mixed, rank, shift, frac, gathered, out, twice):
    slots, share, cells, depth = gathered.shape
    total = slots * cells
    me = rank[0]
    for item in range(share):
        column, _ = pair_of(me, item, share, quantities)
        fraction = frac[column].astype(jnp.float32) * (1.0 / FRAC_DEN)
        bend = fraction * (1.0 - fraction) * 0.25
        start = TOP + lax.rem(total - shift[column], total)

        def lay(slot, carry):
            rows = gathered[slot, item]
            block = lax.bitwise_xor(me, slot) if mixed else slot
            spot = pl.multiple_of(TOP + block * cells, TOP)
            twice[item, pl.ds(spot, cells)] = rows
            twice[item, pl.ds(pl.multiple_of(spot + total, TOP), cells)] = rows
            return carry

        lax.fori_loop(0, slots, lay, 0, unroll=4)
        twice[item, 0:TOP] = twice[item, total : total + TOP]

        def blend(slot, carry):
            spot = start + slot * cells
            back_two = twice[item, pl.ds(spot - 2, cells)]
            back_one = twice[item, pl.ds(spot - 1, cells)]
            centre = twice[item, pl.ds(spot, cells)]
            ahead = twice[item, pl.ds(spot + 1, cells)]
            out[slot, item] = (
                centre
                + fraction * (back_one - centre)
                + bend * ((centre - back_two) - (ahead - back_one))
            )
            return carry

        lax.fori_loop(0, slots, blend, 0, unroll=4)


def move_columns(gathered, quantities, mixed, rank, shift_int, frac_num):
    azimuths, share, cells, depth = gathered.shape
    smem = pl.BlockSpec(memory_space=pltpu.SMEM)
    vmem = pl.BlockSpec(memory_space=pltpu.VMEM)
    return pl.pallas_call(
        functools.partial(move_kernel, quantities, mixed),
        out_shape=jax.ShapeDtypeStruct(gathered.shape, jnp.float32),
        in_specs=[smem, smem, smem, vmem],
        out_specs=vmem,
        scratch_shapes=[pltpu.VMEM((share, 2 * azimuths * cells + TOP, depth), jnp.float32)],
        compiler_params=pltpu.CompilerParams(vmem_limit_bytes=16 * 2**20),
        name="move",
    )(rank, shift_int, frac_num, gathered)


def azimuthal_layers(head, tail):
    azimuths = lax.axis_size("az")
    even = lax.axis_index("az") % 2 == 0
    inner = [(az, az ^ 1) for az in range(azimuths)]
    outer = [(az, (az - 1 if az % 2 == 0 else az + 1) % azimuths) for az in range(azimuths)]
    far = lax.ppermute(jnp.where(even, head, tail), "az", outer)
    near = lax.ppermute(jnp.where(even, tail, head), "az", inner)
    return jnp.where(even, far, near), jnp.where(even, near, far)


def rims_and_stress(blocks, remainder, low, high, before, after, head, tail, fields, density):
    radials = lax.axis_size("rad")
    azimuths = lax.axis_size("az")
    rad = lax.axis_index("rad")
    last = radials - 1

    def flat(rad, az):
        return rad * azimuths + az % azimuths

    def wrap(data, steps):
        pairs = [(flat(last, az), flat(0, az + steps)) for az in range(azimuths)]
        pairs += [(flat(0, az), flat(last, az - steps)) for az in range(azimuths)]
        return lax.ppermute(data, ("rad", "az"), pairs)

    def with_ends(main, column):
        ends = jnp.stack([before[0:3, column], after[0:3, column]], axis=1)
        ends = ends.reshape(1, 6, main.shape[-1])
        ends = jnp.pad(ends, ((0, 0), (0, main.shape[1] - 6), (0, 0)))
        return jnp.concatenate([main, ends], axis=0)

    low, high = with_ends(low, 0), with_ends(high, -1)
    edge = jnp.where(rad == 0, low, high)
    others = (jnp.where(rad == 0, high, low),) if radials == 2 else (high, low)
    info = jnp.stack(
        [(rad == 0).astype(jnp.int32), (rad == last).astype(jnp.int32), remainder]
    )

    def branch(steps):
        def run(info, edge, others, before, after, head, tail, fields, density):
            whole, next_one = wrap(edge, steps), wrap(edge, steps + 1)
            if radials == 2:
                below = above = lax.ppermute(others[0], "rad", [(0, 1), (1, 0)])
            else:
                below = lax.ppermute(others[0], "rad", [(i, i + 1) for i in range(last)])
                above = lax.ppermute(others[1], "rad", [(i + 1, i) for i in range(last)])
            return updated_columns(
                info, fields, density, head, tail, before, after, below, above, whole, next_one
            )

        return run

    branches = [branch(steps) for steps in range(azimuths)]
    return lax.switch(
        blocks, branches, info, edge, others, before, after, head, tail, fields, density
    )


def local(fields, density, shift_int, frac_num, boundary_shift):
    columns, cells, _ = density.shape
    shear_cells = boundary_shift[0]
    rank = lax.axis_index("az").reshape(1)
    head, tail, low, high, still = pack(rank, fields, density)
    before, after = azimuthal_layers(head, tail)
    moving = rims_and_stress(
        shear_cells // cells, shear_cells % cells, low, high, before, after, head, tail, fields, density
    )
    share = still.shape[1]
    both = lax.all_to_all(jnp.concatenate([moving, still], axis=1), "az", 0, 0, tiled=True)
    moving = move_columns(both[:, :share], 4, False, rank, shift_int, frac_num)
    still = move_columns(both[:, share:], 4, False, rank, shift_int, frac_num)
    both = jnp.concatenate([moving, still], axis=1)
    return join(lax.all_to_all(both, "az", 0, 0, tiled=True), columns)


def solution(mesh):
    in_specs = (P(None, "rad", "az", None), P("rad", "az", None), P("rad"), P("rad"), P())
    out_specs = (P(None, "rad", "az", None), P("rad", "az", None))
    return jax.shard_map(local, mesh=mesh, in_specs=in_specs, out_specs=out_specs, check_vma=False)
```
